32 devices in a mesh: dp: 4 (over z), seq: 2 (over x), tensor: 4 (over y, core).
Axes of the slice: x: 2, y: 2, z: 4, core: 2. Of those that a mesh axis runs over, the one named last changes fastest.
Arguments:
- tokens: float32 [16, 1024, 768], P('dp', ('seq', 'tensor')), may hold values from -6 to 6
- out_grad: float32 [16, 1024, 768], P('dp', ('seq', 'tensor')), may hold values from -6 to 6
- segments: int32 [16, 1024], P('dp'), may hold values from 0 to 2, as said below
- gain_mix: float32 [768], replicated, may hold values from 0.5 to 1.5
- query_mix: bfloat16 [768, 768], P(None, 'tensor'), may hold values from -0.21875 to 0.21875
- key_mix: bfloat16 [768, 768], P(None, 'tensor'), may hold values from -0.21875 to 0.21875
- value_mix: bfloat16 [768, 768], P(None, 'tensor'), may hold values from -0.21875 to 0.21875
- output_mix: bfloat16 [768, 768], P('tensor'), may hold values from -0.013671875 to 0.013671875
- shift_kernel: float32 [64, 768], P(None, 'tensor'), may hold values from -0.75 to 0.75
- decay_rate: float32 [12, 64], P('tensor'), may hold values from 0.5 to 32
- gain_ff1: float32 [768], replicated, may hold values from 0.5 to 1.5
- ff_in1: bfloat16 [768, 3072], P(None, 'tensor'), may hold values from -0.21875 to 0.21875
- ff_out1: bfloat16 [3072, 768], P('tensor'), may hold values from -0.109375 to 0.109375
- gain_att: float32 [768], replicated, may hold values from 0.5 to 1.5
- query_att: bfloat16 [768, 768], P(None, 'tensor'), may hold values from -0.21875 to 0.21875
- key_att: bfloat16 [768, 768], P(None, 'tensor'), may hold values from -0.21875 to 0.21875
- value_att: bfloat16 [768, 768], P(None, 'tensor'), may hold values from -0.21875 to 0.21875
- output_att: bfloat16 [768, 768], P('tensor'), may hold values from -0.875 to 0.875
- gain_ff2: float32 [768], replicated, may hold values from 0.5 to 1.5
- ff_in2: bfloat16 [768, 3072], P(None, 'tensor'), may hold values from -0.21875 to 0.21875
- ff_out2: bfloat16 [3072, 768], P('tensor'), may hold values from -0.109375 to 0.109375
Outputs:
- mixed_out: float32 [16, 1024, 768], P('dp', ('seq', 'tensor'))
- tokens_grad: float32 [16, 1024, 768], P('dp', ('seq', 'tensor'))
- gain_mix_grad: float32 [768], replicated
- query_mix_grad: float32 [768, 768], P(None, 'tensor')
- key_mix_grad: float32 [768, 768], P(None, 'tensor')
- value_mix_grad: float32 [768, 768], P(None, 'tensor')
- output_mix_grad: float32 [768, 768], P('tensor')
- shift_kernel_grad: float32 [64, 768], P(None, 'tensor')
- gain_ff1_grad: float32 [768], replicated
- ff_in1_grad: float32 [768, 3072], P(None, 'tensor')
- ff_out1_grad: float32 [3072, 768], P('tensor')
- gain_att_grad: float32 [768], replicated
- query_att_grad: float32 [768, 768], P(None, 'tensor')
- key_att_grad: float32 [768, 768], P(None, 'tensor')
- value_att_grad: float32 [768, 768], P(None, 'tensor')
- output_att_grad: float32 [768, 768], P('tensor')
- gain_ff2_grad: float32 [768], replicated
- ff_in2_grad: float32 [768, 3072], P(None, 'tensor')
- ff_out2_grad: float32 [3072, 768], P('tensor')
- decay_rate_grad: float32 [12, 64], P('tensor')
The draws below stay inside these ranges and needn't reach their ends.
Inputs may be any that keep to these rules, and one draw needn't show every extreme that they name: `segments`: ids start at 0 in each row and rise by 0 or 1 from a position to the next; each row holds exactly 3 documents; in each aligned block of 4 rows one row, drawn from the seed, holds a single document from position 511 to position 512.
All inputs are finite; a program needn't handle non-finite values.
Results may differ from the reference program's by a relative error of at most 0.02.
Values may be sent and summed in bfloat16 or wider, within the bound.
No kernel may reach another device: no remote copies, remote signals or barrier semaphores. Data moves between devices by JAX's collectives and lax.ppermute only.
A program may use at most 320 MiB of HBM per device.

```python
import math
import jax
import jax.numpy as jnp
from jax import lax

D = 768
HEADS = 12
HEAD_DIM = 64
FF = 3072
TAPS = 64
ROWS_DEV = 4
LENGTH = 1024
GROUP = 512
ROWS = 16


def draw_segments(key, part):
    key = jax.random.fold_in(key, 7)
    score_key, pick_key = jax.random.split(key)
    places = jnp.arange(LENGTH, dtype=jnp.int32)
    picked = jax.random.randint(pick_key, (ROWS // ROWS_DEV, 1), 0, ROWS_DEV)
    within = jnp.arange(ROWS).reshape(ROWS // ROWS_DEV, ROWS_DEV) % ROWS_DEV
    spanning = (within == picked).reshape(ROWS, 1)
    middle = ((places >= GROUP) & (places <= LENGTH - GROUP))[None, :]
    allowed = (places > 0)[None, :] & jnp.logical_not(spanning & middle)
    raw = jax.random.randint(score_key, (ROWS, LENGTH), 0, 4096, dtype=jnp.int32) * LENGTH + places[None, :]
    scores = jnp.where(allowed, raw, -1 - places[None, :])
    _, chosen = lax.top_k(scores, LENGTH // GROUP)
    marks = jnp.sum((chosen[:, :, None] == places[None, None, :]).astype(jnp.int32), axis=1)
    return jnp.cumsum(marks, axis=1).astype(jnp.int32)


def levels(stream_key, shape, cuts, low, high):
    def one(axis_at, parts):
        steps = jax.random.uniform(jax.random.fold_in(jax.random.fold_in(stream_key, 6), axis_at), (parts,), jnp.float32, low / len(cuts), high / len(cuts))
        return jnp.repeat(jnp.exp(steps), shape[axis_at] // parts).reshape((-1,) + (1,) * (len(shape) - axis_at - 1))

    level = one(*cuts[0])
    for cut in cuts[1:]:
        level = level * one(*cut)
    return level


def scatter_about(own_key, extent, deviation, limit, cuts=(), kind=jnp.bfloat16):
    gain = levels(own_key, extent, cuts, -0.22, 0.18) if cuts else 1.0
    values = jax.random.normal(own_key, extent, jnp.float32) * deviation * gain
    return jnp.minimum(jnp.maximum(values, -limit), limit).astype(kind)


def setup_inputs(seed: int = 0) -> dict:
    splits = jax.random.split(jax.random.key(seed), 22)
    tokens = scatter_about(splits[0], (ROWS, LENGTH, D), 1.0, 6.0, ((0, 4), (1, 8)), jnp.float32)
    out_grad = scatter_about(splits[1], (ROWS, LENGTH, D), 1.0, 6.0, ((0, 4), (1, 8)), jnp.float32)
    segments = draw_segments(jax.random.fold_in(splits[21], 71), 0)
    gain_mix = jnp.clip(1.0 + 0.1 * jax.random.normal(splits[3], (D,), jnp.float32), 0.5, 1.5)
    query_mix = scatter_about(splits[4], (D, D), D ** -0.5, 0.21875, ((1, 4),))
    key_mix = scatter_about(splits[5], (D, D), D ** -0.5, 0.21875, ((1, 4),))
    value_mix = scatter_about(splits[6], (D, D), D ** -0.5, 0.21875, ((1, 4),))
    output_mix = scatter_about(splits[7], (D, D), (D * 256) ** -0.5, 0.013671875, ((0, 4),))
    shift_kernel = scatter_about(splits[8], (TAPS, D), TAPS ** -0.5, 0.75, ((1, 4),), jnp.float32)
    decay_rate = jnp.clip(jnp.exp(math.log(32.0) - 4.158883 * jax.random.uniform(splits[9], (HEADS, HEAD_DIM), jnp.float32) ** levels(splits[9], (HEADS, HEAD_DIM), ((0, 4),), -0.2, 0.2)), 0.5, 32.0)
    gain_ff1 = jnp.clip(1.0 + 0.1 * jax.random.normal(splits[10], (D,), jnp.float32), 0.5, 1.5)
    ff_in1 = scatter_about(splits[11], (D, FF), D ** -0.5, 0.21875, ((1, 4),))
    ff_out1 = scatter_about(splits[12], (FF, D), FF ** -0.5, 0.109375, ((0, 4),))
    gain_att = jnp.clip(1.0 + 0.1 * jax.random.normal(splits[13], (D,), jnp.float32), 0.5, 1.5)
    query_att = scatter_about(splits[14], (D, D), D ** -0.5, 0.21875, ((1, 4),))
    key_att = scatter_about(splits[15], (D, D), D ** -0.5, 0.21875, ((1, 4),))
    value_att = scatter_about(splits[16], (D, D), D ** -0.5, 0.21875, ((1, 4),))
    output_att = scatter_about(splits[17], (D, D), (D // 16) ** -0.5, 0.875, ((0, 4),))
    gain_ff2 = jnp.clip(1.0 + 0.1 * jax.random.normal(splits[18], (D,), jnp.float32), 0.5, 1.5)
    ff_in2 = scatter_about(splits[19], (D, FF), D ** -0.5, 0.21875, ((1, 4),))
    ff_out2 = scatter_about(splits[20], (FF, D), FF ** -0.5, 0.109375, ((0, 4),))
    return {"tokens": tokens, "out_grad": out_grad, "segments": segments, "gain_mix": gain_mix, "query_mix": query_mix, "key_mix": key_mix, "value_mix": value_mix, "output_mix": output_mix, "shift_kernel": shift_kernel, "decay_rate": decay_rate, "gain_ff1": gain_ff1, "ff_in1": ff_in1, "ff_out1": ff_out1, "gain_att": gain_att, "query_att": query_att, "key_att": key_att, "value_att": value_att, "output_att": output_att, "gain_ff2": gain_ff2, "ff_in2": ff_in2, "ff_out2": ff_out2}


@jax.custom_vjp
def low(v):
    return lax.optimization_barrier(v.astype(jnp.bfloat16)).astype(jnp.float32)

@jax.custom_vjp
def low_back(v):
    return v

def low_keep(v):
    return (low(v), None)

def low_pass(saved_residuals, grad):
    return (grad,)

def back_keep(v):
    return (v, None)

def back_low(saved_residuals, grad):
    return (low(grad),)
low.defvjp(low_keep, low_pass)
low_back.defvjp(back_keep, back_low)
highest = lax.Precision.HIGHEST

def rounded_both(value):
    return low(low_back(value))

def project(left, right):
    return jnp.dot(left, right, precision=highest, preferred_element_type=jnp.float32)

def layer_norm(residual_stream, norm_gain_weight):
    feature_mean = lax.optimization_barrier(jnp.mean(residual_stream, axis=-1, keepdims=True))
    mean_centered = residual_stream - feature_mean
    spread = lax.optimization_barrier(jnp.mean(mean_centered * mean_centered, axis=-1, keepdims=True))
    return mean_centered * lax.rsqrt(spread + 1e-05) * norm_gain_weight

def feed(residual_stream, norm_gain_weight, w_in, w_out):
    normalized_input = low(layer_norm(residual_stream, norm_gain_weight))
    hidden_units = low(jax.nn.gelu(low_back(project(normalized_input, w_in)), approximate=False))
    return residual_stream + low_back(project(hidden_units, w_out))

def mixer(residual_stream, seg, norm_gain_weight, w_q, w_k, w_v, w_o, kernel, rate):
    length = residual_stream.shape[0]
    normalized_input = low(layer_norm(residual_stream, norm_gain_weight))
    query_matrix = rounded_both(project(normalized_input, w_q))
    key_matrix = rounded_both(project(normalized_input, w_k))
    value_matrix = rounded_both(project(normalized_input, w_v))
    taps = kernel.shape[0]
    padded = jnp.pad(key_matrix, ((taps - 1, 0), (0, 0)))
    padded_seg = jnp.concatenate([jnp.full((taps - 1,), -1, jnp.int32), seg.astype(jnp.int32)])
    shifted = jnp.zeros_like(key_matrix)
    for tap in range(taps):
        first = taps - 1 - tap
        match = (padded_seg[first:first + length] == seg).astype(jnp.float32)
        shifted = shifted + kernel[tap] * padded[first:first + length] * match[:, None]
    heads, width = rate.shape
    logdec = -rate / length
    block = math.gcd(length, 64)
    count = length // block
    q_blocks = query_matrix.reshape(count, block, heads, width)
    k_blocks = shifted.reshape(count, block, heads, width)
    v_blocks = value_matrix.reshape(count, block, heads, width)
    s_blocks = seg.reshape(count, block)
    steps = jnp.arange(block, dtype=jnp.float32)[:, None, None]
    order = jnp.arange(block)
    causal = order[:, None] >= order[None, :]

    def run_block(carry, pieces):
        state, before = carry
        q_block, k_block, v_block, s_block = pieces
        rising = jnp.exp(steps * logdec)
        falling = jnp.exp(-steps * logdec)
        leading = jnp.exp((steps + 1.0) * logdec)
        trailing = jnp.exp((block - 1.0 - steps) * logdec)
        same = ((s_block[:, None] == s_block[None, :]) & causal).astype(jnp.float32)
        mixing = jnp.einsum('thi,shi->hts', q_block * rising, k_block * falling, precision=highest) * same[None]
        gate = (s_block == before).astype(jnp.float32)[:, None, None]
        final_result = jnp.einsum('hts,shj->thj', mixing, v_block, precision=highest)
        final_result = final_result + jnp.einsum('thi,hij->thj', q_block * leading * gate, state, precision=highest)
        final = s_block[-1]
        ends = (s_block == final).astype(jnp.float32)[:, None, None]
        carry_on = (final == before).astype(jnp.float32)
        state = state * (jnp.exp(block * logdec) * carry_on)[:, :, None]
        state = state + jnp.einsum('shi,shj->hij', k_block * trailing * ends, v_block, precision=highest)
        return ((state, final), final_result)
    initial = (jnp.zeros((heads, width, width), jnp.float32), jnp.array(-1, jnp.int32))
    _, mixed = lax.scan(jax.checkpoint(run_block), initial, (q_blocks, k_blocks, v_blocks, s_blocks))
    out_mix = low(mixed.reshape(length, heads * width) * (1.0 / math.sqrt(width)))
    return residual_stream + low_back(project(out_mix, w_o))

def attend(residual_stream, seg, norm_gain_weight, w_q, w_k, w_v, w_o):
    length = residual_stream.shape[0]
    heads = HEADS
    width = HEAD_DIM
    normalized_input = low(layer_norm(residual_stream, norm_gain_weight))
    query_matrix = rounded_both(project(normalized_input, w_q)).reshape(length, heads, width)
    key_matrix = rounded_both(project(normalized_input, w_k)).reshape(length, heads, width)
    value_matrix = rounded_both(project(normalized_input, w_v)).reshape(length, heads, width)
    block = min(512, length)
    positions = jnp.arange(length)
    scale = 1.0 / math.sqrt(width)

    def one_block(index):
        begin = (index * block).astype(jnp.int32)
        q_block = lax.dynamic_slice_in_dim(query_matrix, begin, block, 0)
        s_block = lax.dynamic_slice_in_dim(seg, begin, block, 0)
        q_pos = begin + jnp.arange(block)
        scores = low_back(jnp.einsum('thd,shd->hts', q_block, key_matrix, precision=highest) * scale)
        allowed = (q_pos[:, None] >= positions[None, :]) & (s_block[:, None] == seg[None, :])
        scores = jnp.where(allowed[None], scores, -1e+30)
        top = lax.optimization_barrier(jnp.max(scores, axis=-1, keepdims=True))
        expd = jnp.exp(scores - top)
        softened = expd / lax.optimization_barrier(jnp.sum(expd, axis=-1, keepdims=True))
        return jnp.einsum('hts,shd->thd', low(softened), value_matrix, precision=highest)
    final_result = lax.map(jax.checkpoint(one_block), jnp.arange(length // block))
    attention_output = rounded_both(final_result.reshape(length, heads * width))
    return residual_stream + low_back(project(attention_output, w_o))

def row_forward(params, residual_stream, seg):
    g_mix, q_mix, k_mix, v_mix, o_mix, kernel, g_ff1, in_one, out_one, g_att, q_att, k_att, v_att, o_att, g_ff2, in_two, out_two, rate = params
    residual_stream = mixer(residual_stream, seg, g_mix, q_mix, k_mix, v_mix, o_mix, kernel, rate)
    residual_stream = feed(residual_stream, g_ff1, in_one, out_one)
    residual_stream = attend(residual_stream, seg, g_att, q_att, k_att, v_att, o_att)
    return feed(residual_stream, g_ff2, in_two, out_two)

def reference(tokens, out_grad, segments, gain_mix, query_mix, key_mix, value_mix, output_mix, shift_kernel, decay_rate, gain_ff1, ff_in1, ff_out1, gain_att, query_att, key_att, value_att, output_att, gain_ff2, ff_in2, ff_out2):
    listed = (gain_mix, query_mix, key_mix, value_mix, output_mix, shift_kernel, gain_ff1, ff_in1, ff_out1, gain_att, query_att, key_att, value_att, output_att, gain_ff2, ff_in2, ff_out2, decay_rate)
    params = tuple((item.astype(jnp.float32) for item in listed))

    def step(summed, pieces):
        stream_row, grad_row, seg_row = pieces
        final_result, pull = jax.vjp(lambda weights, residual_stream: row_forward(weights, residual_stream, seg_row), params, stream_row)
        grads, grad_stream = pull(grad_row)
        return (jax.tree.map(lambda left, right: left + right, summed, grads), (final_result, grad_stream))
    zeros = jax.tree.map(jnp.zeros_like, params)
    grads, (results, stream_grads) = lax.scan(step, zeros, (tokens, out_grad, segments))
    return (results, stream_grads, grads[0], grads[1], grads[2], grads[3], grads[4], grads[5], grads[6], grads[7], grads[8], grads[9], grads[10], grads[11], grads[12], grads[13], grads[14], grads[15], grads[16], grads[17])
```

```python
import functools
import math

import jax
import jax.numpy as jnp
from jax import lax
from jax.experimental import pallas as pl
from jax.experimental.pallas import tpu as pltpu
from jax.sharding import PartitionSpec as P

HEAD_DIM = 64
DP, SEQ, TENSOR = "dp", "seq", "tensor"


highest = lax.Precision.HIGHEST
norm_eps = 1e-05
masked_score = -1e30


def passed_along(array, axis, by):
    devices = lax.axis_size(axis)
    pairs = [(i, i + by) for i in range(devices) if 0 <= i + by < devices]
    return lax.ppermute(array, axis, pairs)


def prefix(array, axis, combine, identity):
    devices, here = (lax.axis_size(axis), lax.axis_index(axis))
    everything = jax.tree.map(lambda part: lax.all_gather(part, axis), array)
    start = jax.tree.map(
        lambda part, zero: jnp.broadcast_to(jnp.asarray(zero, part.dtype), part.shape),
        array,
        identity,
    )

    def step(k, before):
        reached = k < here
        new = combine(before, jax.tree.map(lambda part: part[k], everything))
        return jax.tree.map(lambda a, b: jnp.where(reached, a, b), new, before)

    return lax.fori_loop(0, devices, step, start)


def prefix_2(array, axis, join, neutral):
    count = lax.axis_size(axis)
    place = lax.axis_index(axis)
    ahead = count - 1 - place
    gathered = jax.tree.map(
        lambda a, kind: lax.all_gather(a.astype(kind), axis), array, (jnp.bfloat16, jnp.bfloat16)
    )
    state = jax.tree.map(lambda a, e: jnp.zeros_like(a) + jnp.asarray(e, a.dtype), array, neutral)

    def one(step, state):
        source = count - 1 - step
        return join(
            state,
            jax.tree.map(
                lambda a, own: lax.dynamic_index_in_dim(a, source, 0, False).astype(own.dtype),
                gathered,
                array,
            ),
        )

    return lax.fori_loop(0, ahead, one, state)


def lower_triangle(value):
    return value.astype(jnp.bfloat16)


def bmul(form, left, right):
    return jnp.einsum(form, left, right, preferred_element_type=jnp.float32)


def fmul(form, left, right):
    return jnp.einsum(form, left, right, precision=highest, preferred_element_type=jnp.float32)


def layer_norm_forward(residual_stream, norm_gain_weight):
    feature_mean = jnp.mean(residual_stream, axis=-1, keepdims=True)
    mean_centered = residual_stream - feature_mean
    scale_factor = lax.rsqrt(
        jnp.mean(mean_centered * mean_centered, axis=-1, keepdims=True) + norm_eps
    )
    standardized_input = mean_centered * scale_factor
    return (lower_triangle(standardized_input * norm_gain_weight), standardized_input, scale_factor)


def layer_norm_backward(normalized_gradient, standardized_input, scale_factor, norm_gain_weight):
    gain_gradient = jnp.sum(normalized_gradient * standardized_input, axis=(0, 1))
    rescaled_input = normalized_gradient * norm_gain_weight
    mean_centered = rescaled_input - jnp.mean(rescaled_input, axis=-1, keepdims=True)
    return (
        scale_factor
        * (
            mean_centered
            - standardized_input
            * jnp.mean(rescaled_input * standardized_input, axis=-1, keepdims=True)
        ),
        gain_gradient,
    )


def widen(normalized_input):
    return lax.all_gather(normalized_input, TENSOR, axis=1, tiled=True)


def narrow(partial_value):
    return lax.psum_scatter(partial_value, TENSOR, scatter_dimension=1, tiled=True)


def widen_grad(grad_stream):
    return lax.all_gather(lower_triangle(grad_stream), TENSOR, axis=1, tiled=True)


def narrow_grad(partial_value):
    return lax.psum_scatter(partial_value, TENSOR, scatter_dimension=1, tiled=True)


def combine_states(earlier, later):
    return (earlier[0] * later[0], later[1] + later[0][..., None] * earlier[1])


def feed_forward(residual_stream, norm_gain_weight, w_in, w_out):
    normalized_input, standardized_input, scale_factor = layer_norm_forward(
        residual_stream, norm_gain_weight
    )
    widened_hidden = widen(normalized_input)
    hidden_preactivation = bmul("rtd,df->rtf", widened_hidden, w_in)
    hidden_units = lower_triangle(jax.nn.gelu(hidden_preactivation, approximate=False))
    final_result = residual_stream + narrow(bmul("rtf,fd->rtd", hidden_units, w_out))
    return (
        final_result,
        (widened_hidden, standardized_input, scale_factor, hidden_preactivation, hidden_units),
    )


def feed_backward(grad_stream, saved_residuals, norm_gain_weight, w_in, w_out):
    widened_hidden, standardized_input, scale_factor, hidden_preactivation, hidden_units = (
        saved_residuals
    )
    grad_wide = widen_grad(grad_stream)
    grad_out_w = bmul("rtf,rtd->fd", hidden_units, grad_wide)
    grad_hidden = bmul("rtd,fd->rtf", grad_wide, w_out)
    _, gelu_pull = jax.vjp(
        lambda value: jax.nn.gelu(value, approximate=False), hidden_preactivation
    )
    grad_before = lower_triangle(gelu_pull(grad_hidden)[0])
    grad_in_w = bmul("rtd,rtf->df", widened_hidden, grad_before)
    normalized_gradient = narrow_grad(bmul("rtf,df->rtd", grad_before, w_in))
    norm_input_gradient, gain_gradient = layer_norm_backward(
        normalized_gradient, standardized_input, scale_factor, norm_gain_weight
    )
    return (grad_stream + norm_input_gradient, gain_gradient, grad_in_w, grad_out_w)


def mixer_forward(residual_stream, seg_rows, norm_gain_weight, w_q, w_k, w_v, w_o, kernel, rate):
    normalized_input, standardized_input, scale_factor = layer_norm_forward(
        residual_stream, norm_gain_weight
    )
    widened_hidden = widen(normalized_input)
    rows, group_len = (widened_hidden.shape[0], widened_hidden.shape[1])
    heads, width = rate.shape
    query_matrix = lower_triangle(bmul("rtd,de->rte", widened_hidden, w_q))
    key_matrix = lower_triangle(bmul("rtd,de->rte", widened_hidden, w_k))
    value_matrix = lower_triangle(bmul("rtd,de->rte", widened_hidden, w_v))
    taps = kernel.shape[0]
    start = lax.axis_index(SEQ) * group_len
    length = group_len * lax.axis_size(SEQ)
    padded = jnp.concatenate([jnp.full((rows, taps), -1, jnp.int32), seg_rows], axis=1)
    seg_ext = lax.dynamic_slice_in_dim(padded, start + 1, group_len + taps - 1, 1)
    owning_segment = seg_ext[:, taps - 1 :]
    rim = passed_along(key_matrix[:, group_len - taps + 1 :, :], SEQ, 1)
    extended = jnp.concatenate([rim, key_matrix], axis=1).astype(jnp.float32)
    shifted = jnp.zeros(key_matrix.shape, jnp.float32)
    match_list = []
    for tap in range(taps):
        first = taps - 1 - tap
        match = (seg_ext[:, first : first + group_len] == owning_segment).astype(jnp.float32)[
            :, :, None
        ]
        match_list.append(match)
        shifted = shifted + kernel[tap] * extended[:, first : first + group_len] * match
    matches = jnp.stack(match_list)
    logdec = -rate / length
    steps = jnp.arange(group_len, dtype=jnp.float32)[:, None, None]
    rising = jnp.exp(steps * logdec)
    falling = jnp.exp(-steps * logdec)
    leading = jnp.exp((steps + 1.0) * logdec)
    trailing = jnp.exp((group_len - 1.0 - steps) * logdec)
    before = seg_ext[:, taps - 2]
    final = owning_segment[:, -1]
    order = jnp.arange(group_len)
    same = (
        (owning_segment[:, :, None] == owning_segment[:, None, :])
        & (order[:, None] >= order[None, :])
    ).astype(jnp.float32)
    gate = (owning_segment == before[:, None]).astype(jnp.float32)[:, :, None, None]
    ends = (owning_segment == final[:, None]).astype(jnp.float32)[:, :, None, None]
    carry_on = (final == before).astype(jnp.float32)[:, None, None]
    query_f = query_matrix.astype(jnp.float32).reshape(rows, group_len, heads, width)
    shift_f = shifted.reshape(rows, group_len, heads, width)
    value_f = value_matrix.astype(jnp.float32).reshape(rows, group_len, heads, width)
    query_up = query_f * rising
    key_down = shift_f * falling
    query_lead = query_f * leading * gate
    key_tail = shift_f * trailing * ends
    mixing = fmul("rthi,rshi->rhts", query_up, key_down) * same[:, None]
    decay = jnp.exp(group_len * logdec)[None] * carry_on
    end_state = fmul("rshi,rshj->rhij", key_tail, value_f)
    identity = (jnp.ones(decay.shape, jnp.float32), jnp.zeros(end_state.shape, jnp.float32))
    entering = prefix((decay, end_state), SEQ, combine_states, identity)[1]
    mixed = fmul("rhts,rshj->rthj", mixing, value_f) + fmul("rthi,rhij->rthj", query_lead, entering)
    out_mix = lower_triangle(
        mixed.reshape(rows, group_len, heads * width) * (1.0 / math.sqrt(width))
    )
    final_result = residual_stream + narrow(bmul("rte,ed->rtd", out_mix, w_o))
    saved_residuals = (
        widened_hidden,
        standardized_input,
        scale_factor,
        extended,
        matches,
        value_f,
        rising,
        falling,
        leading,
        trailing,
        gate,
        ends,
        same,
        query_up,
        key_down,
        query_lead,
        key_tail,
        mixing,
        decay,
        entering,
        identity,
        out_mix,
    )
    return (final_result, saved_residuals)


def mixer_backward(
    grad_stream, saved_residuals, norm_gain_weight, w_q, w_k, w_v, w_o, kernel, rate
):
    (
        widened_hidden,
        standardized_input,
        scale_factor,
        extended,
        matches,
        value_f,
        rising,
        falling,
        leading,
        trailing,
        gate,
        ends,
        same,
        query_up,
        key_down,
        query_lead,
        key_tail,
        mixing,
        decay,
        entering,
        identity,
        out_mix,
    ) = saved_residuals
    rows, group_len = (widened_hidden.shape[0], widened_hidden.shape[1])
    heads, width = rate.shape
    taps = kernel.shape[0]
    length = group_len * lax.axis_size(SEQ)
    grad_wide = widen_grad(grad_stream)
    grad_o = bmul("rte,rtd->ed", out_mix, grad_wide)
    grad_mixed = bmul("rtd,ed->rte", grad_wide, w_o).reshape(rows, group_len, heads, width) * (
        1.0 / math.sqrt(width)
    )
    grad_mixing = fmul("rthj,rshj->rhts", grad_mixed, value_f) * same[:, None]
    grad_qup = fmul("rhts,rshi->rthi", grad_mixing, key_down)
    grad_kdown = fmul("rhts,rthi->rshi", grad_mixing, query_up)
    reach = fmul("rthj,rhij->rthi", grad_mixed, entering)
    local_back = fmul("rthi,rthj->rhij", query_lead, grad_mixed)
    leaving = prefix_2((decay, local_back), SEQ, combine_states, identity)[1]
    spread = fmul("rshj,rhij->rshi", value_f, leaving)
    grad_value = fmul("rhts,rthj->rshj", mixing, grad_mixed) + fmul(
        "rshi,rhij->rshj", key_tail, leaving
    )
    grad_query = grad_qup * rising + reach * leading * gate
    grad_shift = grad_kdown * falling + spread * trailing * ends
    steps = jnp.arange(group_len, dtype=jnp.float32)[:, None, None]
    local_terms = steps * (query_up * grad_qup - key_down * grad_kdown)
    local_terms = (
        local_terms
        + (steps + 1.0) * query_lead * reach
        + (group_len - 1.0 - steps) * key_tail * spread
    )
    grad_log = jnp.sum(local_terms, axis=(0, 1))
    grad_log = grad_log + group_len * jnp.sum(jnp.sum(leaving * entering, axis=3) * decay, axis=0)
    grad_rate = -grad_log / length
    grad_shift = grad_shift.reshape(rows, group_len, heads * width)
    grad_ext = jnp.zeros(extended.shape, jnp.float32)
    kernel_rows = []
    for tap in range(taps):
        first = taps - 1 - tap
        masked = grad_shift * matches[tap]
        kernel_rows.append(jnp.sum(masked * extended[:, first : first + group_len], axis=(0, 1)))
        grad_ext = grad_ext + jnp.pad(
            kernel[tap] * masked, ((0, 0), (first, taps - 1 - first), (0, 0))
        )
    grad_kernel = jnp.stack(kernel_rows)
    returned = passed_along(grad_ext[:, : taps - 1].astype(jnp.bfloat16), SEQ, -1).astype(
        jnp.float32
    )
    grad_keys = grad_ext[:, taps - 1 :] + jnp.pad(
        returned, ((0, 0), (group_len - taps + 1, 0), (0, 0))
    )
    query_low = lower_triangle(grad_query.reshape(rows, group_len, heads * width))
    keys_low = lower_triangle(grad_keys)
    value_low = lower_triangle(grad_value.reshape(rows, group_len, heads * width))
    grad_qw = bmul("rtd,rte->de", widened_hidden, query_low)
    grad_kw = bmul("rtd,rte->de", widened_hidden, keys_low)
    grad_vw = bmul("rtd,rte->de", widened_hidden, value_low)
    partial_value = bmul("rte,de->rtd", query_low, w_q) + bmul("rte,de->rtd", keys_low, w_k)
    partial_value = partial_value + bmul("rte,de->rtd", value_low, w_v)
    normalized_gradient = narrow_grad(partial_value)
    norm_input_gradient, gain_gradient = layer_norm_backward(
        normalized_gradient, standardized_input, scale_factor, norm_gain_weight
    )
    return (
        grad_stream + norm_input_gradient,
        gain_gradient,
        grad_qw,
        grad_kw,
        grad_vw,
        grad_o,
        grad_kernel,
        grad_rate,
    )


def split_heads(value):
    return value.reshape(value.shape[0], value.shape[1] // HEAD_DIM, HEAD_DIM)


def scores_of(query_rows, key_rows, query_places, key_places, query_seg, key_seg):
    raw = bmul("thd,shd->hts", split_heads(query_rows), split_heads(key_rows)) * (
        1.0 / math.sqrt(HEAD_DIM)
    )
    allowed = (query_places[:, None] >= key_places[None, :]) & (
        query_seg[:, None] == key_seg[None, :]
    )
    return jnp.where(allowed[None], raw, masked_score)


def attend_forward(residual_stream, seg_rows, norm_gain_weight, w_q, w_k, w_v, w_o):
    normalized_input, standardized_input, scale_factor = layer_norm_forward(
        residual_stream, norm_gain_weight
    )
    widened_hidden = widen(normalized_input)
    rows, group_len = (widened_hidden.shape[0], widened_hidden.shape[1])
    query_matrix = lower_triangle(bmul("rtd,de->rte", widened_hidden, w_q))
    key_matrix = lower_triangle(bmul("rtd,de->rte", widened_hidden, w_k))
    value_matrix = lower_triangle(bmul("rtd,de->rte", widened_hidden, w_v))
    gathered_key_rows, gathered_value_rows = (
        lax.all_gather(key_matrix, SEQ, axis=1, tiled=True),
        lax.all_gather(value_matrix, SEQ, axis=1, tiled=True),
    )
    length = gathered_key_rows.shape[1]
    start = lax.axis_index(SEQ) * group_len
    owning_segment = lax.dynamic_slice_in_dim(seg_rows, start, group_len, 1)
    query_places = start + jnp.arange(group_len)
    key_places = jnp.arange(length)

    def forward_row(pieces):
        query_row, key_row, value_row, seg_own, seg_all = pieces
        scores = scores_of(query_row, key_row, query_places, key_places, seg_own, seg_all)
        top = jnp.max(scores, axis=-1, keepdims=True)
        expd = jnp.exp(scores - top)
        total = jnp.sum(expd, axis=-1, keepdims=True)
        softened = lower_triangle(expd / total)
        attended = bmul("hts,shd->thd", softened, split_heads(value_row))
        return (
            lower_triangle(attended.reshape(group_len, attended.shape[1] * HEAD_DIM)),
            (top + jnp.log(total))[..., 0],
        )

    attention_output, log_normalizer = lax.map(
        forward_row,
        (query_matrix, gathered_key_rows, gathered_value_rows, owning_segment, seg_rows),
    )
    final_result = residual_stream + narrow(bmul("rte,ed->rtd", attention_output, w_o))
    saved_residuals = (
        widened_hidden,
        standardized_input,
        scale_factor,
        query_matrix,
        key_matrix,
        value_matrix,
        gathered_key_rows,
        gathered_value_rows,
        owning_segment,
        log_normalizer,
        attention_output,
    )
    return (final_result, saved_residuals)


def attend_backward(grad_stream, saved_residuals, seg_rows, norm_gain_weight, w_q, w_k, w_v, w_o):
    (
        widened_hidden,
        standardized_input,
        scale_factor,
        query_matrix,
        key_matrix,
        value_matrix,
        gathered_key_rows,
        gathered_value_rows,
        owning_segment,
        log_normalizer,
        attention_output,
    ) = saved_residuals
    rows, group_len = (widened_hidden.shape[0], widened_hidden.shape[1])
    length = gathered_key_rows.shape[1]
    start = lax.axis_index(SEQ) * group_len
    query_places = start + jnp.arange(group_len)
    key_places = jnp.arange(length)
    scale = 1.0 / math.sqrt(HEAD_DIM)
    grad_wide = widen_grad(grad_stream)
    grad_o = bmul("rte,rtd->ed", attention_output, grad_wide)
    grad_out = lower_triangle(bmul("rtd,ed->rte", grad_wide, w_o))

    def query_common(pieces):
        query_row, key_row, value_row, seg_own, seg_all, total_row, grad_row = pieces
        scores = scores_of(query_row, key_row, query_places, key_places, seg_own, seg_all)
        softened = jnp.exp(scores - total_row[:, :, None])
        grad_soft = bmul("thd,shd->hts", split_heads(grad_row), split_heads(value_row))
        inner = jnp.sum(softened * grad_soft, axis=-1)
        grad_score = lower_triangle(softened * (grad_soft - inner[:, :, None]))
        grad_q = bmul("hts,shd->thd", grad_score, split_heads(key_row)) * scale
        return (softened, grad_score, grad_q.reshape(group_len, -1), inner)

    pieces = (
        query_matrix,
        gathered_key_rows,
        gathered_value_rows,
        owning_segment,
        seg_rows,
        log_normalizer,
        grad_out,
    )

    def query_only(row_pieces):
        _, _, grad_q, inner = query_common(row_pieces)
        return (grad_q, inner)

    grad_query, inner = lax.map(query_only, pieces)
    all_query, all_grad = (
        lax.all_gather(query_matrix, SEQ, axis=1, tiled=True),
        lax.all_gather(grad_out, SEQ, axis=1, tiled=True),
    )
    all_total, all_inner = (
        lax.all_gather(log_normalizer, SEQ, axis=2, tiled=True),
        lax.all_gather(inner, SEQ, axis=2, tiled=True),
    )

    def key_row_fn(row_pieces):
        query_row, key_row, value_row, seg_all, seg_own, total_row, inner_row, grad_row = row_pieces
        scores = scores_of(query_row, key_row, key_places, query_places, seg_all, seg_own)
        softened = jnp.exp(scores - total_row[:, :, None])
        grad_soft = bmul("thd,shd->hts", split_heads(grad_row), split_heads(value_row))
        grad_score = lower_triangle(softened * (grad_soft - inner_row[:, :, None]))
        grad_k = bmul("hts,thd->shd", grad_score, split_heads(query_row)) * scale
        grad_v = bmul("hts,thd->shd", lower_triangle(softened), split_heads(grad_row))
        return (grad_k.reshape(group_len, -1), grad_v.reshape(group_len, -1))

    grad_keys, grad_values = lax.map(
        key_row_fn,
        (
            all_query,
            key_matrix,
            value_matrix,
            seg_rows,
            owning_segment,
            all_total,
            all_inner,
            all_grad,
        ),
    )
    query_low = lower_triangle(grad_query)
    keys_low = lower_triangle(grad_keys)
    value_low = lower_triangle(grad_values)
    grad_qw = bmul("rtd,rte->de", widened_hidden, query_low)
    grad_kw = bmul("rtd,rte->de", widened_hidden, keys_low)
    grad_vw = bmul("rtd,rte->de", widened_hidden, value_low)
    partial_value = bmul("rte,de->rtd", query_low, w_q) + bmul("rte,de->rtd", keys_low, w_k)
    partial_value = partial_value + bmul("rte,de->rtd", value_low, w_v)
    normalized_gradient = narrow_grad(partial_value)
    norm_input_gradient, gain_gradient = layer_norm_backward(
        normalized_gradient, standardized_input, scale_factor, norm_gain_weight
    )
    return (grad_stream + norm_input_gradient, gain_gradient, grad_qw, grad_kw, grad_vw, grad_o)


def shards(
    tokens,
    out_grad,
    segments,
    gain_mix,
    query_mix,
    key_mix,
    value_mix,
    output_mix,
    shift_kernel,
    decay_rate,
    gain_ff1,
    ff_in1,
    ff_out1,
    gain_att,
    query_att,
    key_att,
    value_att,
    output_att,
    gain_ff2,
    ff_in2,
    ff_out2,
):
    stream_one, kept_mix = mixer_forward(
        tokens,
        segments,
        gain_mix,
        query_mix,
        key_mix,
        value_mix,
        output_mix,
        shift_kernel,
        decay_rate,
    )
    stream_two, kept_first = feed_forward(stream_one, gain_ff1, ff_in1, ff_out1)
    stream_three, kept_att = attend_forward(
        stream_two, segments, gain_att, query_att, key_att, value_att, output_att
    )
    stream_four, kept_second = feed_forward(stream_three, gain_ff2, ff_in2, ff_out2)
    back_three, gain_two_grad, in_two_grad, out_two_grad = feed_backward(
        out_grad, kept_second, gain_ff2, ff_in2, ff_out2
    )
    back_two, att_gain_grad, att_q_grad, att_k_grad, att_v_grad, att_o_grad = attend_backward(
        back_three, kept_att, segments, gain_att, query_att, key_att, value_att, output_att
    )
    back_one, gain_one_grad, in_one_grad, out_one_grad = feed_backward(
        back_two, kept_first, gain_ff1, ff_in1, ff_out1
    )
    (
        back_zero,
        mix_gain_grad,
        mix_q_grad,
        mix_k_grad,
        mix_v_grad,
        mix_o_grad,
        kernel_grad,
        rate_grad,
    ) = mixer_backward(
        back_one,
        kept_mix,
        gain_mix,
        query_mix,
        key_mix,
        value_mix,
        output_mix,
        shift_kernel,
        decay_rate,
    )
    summed = lax.psum(
        (
            mix_q_grad,
            mix_k_grad,
            mix_v_grad,
            mix_o_grad,
            kernel_grad,
            in_one_grad,
            out_one_grad,
            att_q_grad,
            att_k_grad,
            att_v_grad,
            att_o_grad,
            in_two_grad,
            out_two_grad,
            rate_grad,
        ),
        (DP, SEQ),
    )
    gains = lax.psum(
        (mix_gain_grad, gain_one_grad, att_gain_grad, gain_two_grad), (DP, SEQ, TENSOR)
    )
    return (
        stream_four,
        back_zero,
        gains[0],
        summed[0],
        summed[1],
        summed[2],
        summed[3],
        summed[4],
        gains[1],
        summed[5],
        summed[6],
        gains[2],
        summed[7],
        summed[8],
        summed[9],
        summed[10],
        gains[3],
        summed[11],
        summed[12],
        summed[13],
    )


CHUNK = 128
LANES = 128
BLOCK = 2 * CHUNK
FF_COLUMNS = 768
MIB = 1024 * 1024


def dot(left, right, over):
    return lax.dot_general(left, right, (over, ((), ())), preferred_element_type=jnp.float32)


over_nn, over_nt = ((1,), (0,)), ((1,), (1,))


def dot_nn(left, right):
    return dot(left, right, over_nn)


def dot_nt(left, right):
    return dot(left, right, over_nt)


def dot_tn(left, right):
    return dot(left, right, ((0,), (0,)))


def low16(value):
    return value.astype(jnp.bfloat16)


def wide32(value):
    return value.astype(jnp.float32)


def made(shape, kind=jnp.bfloat16):
    return jax.ShapeDtypeStruct(shape, kind)


def kernel_call(
    body, outs, scratch=(), grid=(), in_specs=None, out_specs=None, scalars=0, name=None, after=(), cost=0
):
    if in_specs is None:
        in_specs, out_specs = pl.BlockSpec(memory_space=pltpu.VMEM), [pl.BlockSpec(memory_space=pltpu.VMEM)] * len(outs)
    params = pltpu.CompilerParams(vmem_limit_bytes=50 * MIB)
    estimate = pl.CostEstimate(flops=cost * 10**9, bytes_accessed=0, transcendentals=0)

    def call(*arrays):
        count = len(arrays)
        ins = [in_specs] * (count - scalars) if isinstance(in_specs, pl.BlockSpec) else list(in_specs)
        spec = pltpu.PrefetchScalarGridSpec(
            num_scalar_prefetch=scalars,
            grid=grid,
            in_specs=ins + [pl.BlockSpec(memory_space=pl.ANY)] * len(after),
            out_specs=out_specs,
            scratch_shapes=scratch,
        )

        def whole_body(*refs):
            body(*refs[:count], *refs[count + len(after) :])

        return pl.pallas_call(
            whole_body, grid_spec=spec, out_shape=outs, compiler_params=params, cost_estimate=estimate, name=name
        )(*arrays, *after)

    return call


def place_of(n, core, half):
    return pl.multiple_of(((n & 1) ^ core) * half + (n >> 1) * CHUNK, CHUNK)


def lane_heads():
    lane = lax.broadcasted_iota(jnp.int32, (CHUNK, LANES), 1)
    return [lane // HEAD_DIM == head for head in range(LANES // HEAD_DIM)]


def head_diagonal():
    row = lax.broadcasted_iota(jnp.int32, (LANES, LANES), 0)
    lane = lax.broadcasted_iota(jnp.int32, (LANES, LANES), 1)
    return row // HEAD_DIM == lane // HEAD_DIM


def causal_same(seg_rows, seg_lanes):
    row = lax.broadcasted_iota(jnp.int32, (CHUNK, CHUNK), 0)
    lane = lax.broadcasted_iota(jnp.int32, (CHUNK, CHUNK), 1)
    return (seg_rows == seg_lanes) & (row >= lane)


def pick_heads(heads, parts):
    result = parts[0]
    for head in range(1, len(parts)):
        result = jnp.where(heads[head], parts[head], result)
    return result


def decays(logdec):
    steps = wide32(lax.broadcasted_iota(jnp.int32, (CHUNK, LANES), 0))
    rising, falling = jnp.exp(steps * logdec), jnp.exp(-steps * logdec)
    return steps, rising, falling, jnp.exp(logdec), jnp.exp((CHUNK - 1.0) * logdec), jnp.exp(CHUNK * logdec)


def documents(seg_s, n):
    at = pl.multiple_of(n * CHUNK, CHUNK)
    before = jnp.where(n == 0, -1, seg_s[jnp.maximum(at - 1, 0)])
    return at, seg_s[at], seg_s[at + CHUNK - 1], before


def split_columns(ref, tile=0):
    first = 3 * LANES * tile
    return [ref.at[:, first + i * LANES : first + (i + 1) * LANES] for i in range(3)]


def tile_of(tile):
    return slice(tile * LANES, (tile + 1) * LANES)


def h3_forward_body(
    first, tiles, taps, seg_s, qkv_ref, w_ref, logdec_ref, segb_ref, segl_ref,
    out_ref, shift_ref, state_ref, key_f, masked, state,
):
    length = qkv_ref.shape[0]
    chunks, half, core = length // CHUNK, length // 2, seg_s[length]
    tables = [decays(logdec_ref[:, tile_of(first + tile)]) for tile in range(tiles)]
    heads, diagonal = lane_heads(), head_diagonal()
    key_f[0:taps, :] = jnp.zeros((taps, tiles * LANES), jnp.float32)
    state[...] = jnp.zeros_like(state)

    def chunk_step(n, _):
        at, low_doc, high_doc, before = documents(seg_s, n)
        here = pl.ds(place_of(n, core, half), CHUNK)
        for tile in range(tiles):
            key_f[pl.ds(at + taps, CHUNK), tile_of(tile)] = wide32(split_columns(qkv_ref, tile)[1][here, :])
        seg_here = segb_ref[pl.ds(at + taps, CHUNK), :]

        def one_doc(doc, totals):
            window = segb_ref[pl.ds(at, CHUNK + taps), :] == doc
            result = []
            for tile in range(tiles):
                lanes = tile_of(tile)
                masked[:, lanes] = jnp.where(window, key_f[pl.ds(at, CHUNK + taps), lanes], 0.0)
                conv = jnp.zeros((CHUNK, LANES), jnp.float32)
                for b in range(8):
                    part = jnp.zeros((CHUNK + 8, LANES), jnp.float32)
                    for a in range(taps // 8):
                        tap = 8 * a + b
                        seen = masked[taps - 8 - 8 * a : taps + CHUNK - 8 * a, lanes]
                        part = part + w_ref[tap : tap + 1, tile_of(first + tile)] * seen
                    if b:
                        part = pltpu.roll(part, b, 0)
                    conv = conv + part[8:, :]
                result.append(totals[tile] + jnp.where(seg_here == doc, conv, 0.0))
            return tuple(result)

        zero = jnp.zeros((CHUNK, LANES), jnp.float32)
        shifts = lax.fori_loop(low_doc, high_doc + 1, one_doc, (zero,) * tiles)
        gate, ends = wide32(seg_here == before), wide32(seg_here == high_doc)
        carry = jnp.where(high_doc == before, 1.0, 0.0)
        same = causal_same(seg_here, segl_ref[pl.ds(n, 1), :])
        work = []
        for tile in range(tiles):
            _, rising, falling, one, last, whole = tables[tile]
            q_ref, _, v_ref = split_columns(qkv_ref, tile)
            shift_ref[pl.ds(at, CHUNK), tile_of(tile)] = shifts[tile]
            q_up = low16(wide32(q_ref[here, :]) * rising)
            k_down = low16(shifts[tile] * falling)
            work.append((q_up, k_down, v_ref[here, :], state[tile], one, last, whole))
        mixings = [
            [dot_nt(jnp.where(head, q_up, jnp.zeros_like(q_up)), k_down) for head in heads]
            for q_up, k_down, *_ in work
        ]
        for tile, (q_up, k_down, value, entering, one, last, whole) in enumerate(work):
            parts = [dot_nn(low16(jnp.where(same, mixing, 0.0)), value) for mixing in mixings[tile]]
            state_ref[tile, n] = entering
            mixed = pick_heads(heads, parts) + gate * dot_nt(q_up, low16(entering * one))
            out_ref[here, tile_of(tile)] = low16(mixed * (1.0 / math.sqrt(HEAD_DIM)))
            tail = dot_tn(low16(wide32(value) * ends), k_down) * last
            state[tile] = entering * (whole * carry) + jnp.where(diagonal, tail, 0.0)
        return 0

    lax.fori_loop(0, chunks, chunk_step, 0)


def h3_specs(length, taps, wide, chunks):
    whole = lambda *shape: pl.BlockSpec(shape, lambda i, s: (0,) * len(shape))
    tables = [whole(taps, wide), whole(1, wide), whole(length + 2 * taps, LANES), whole(chunks, CHUNK)]
    return whole, tables


def h3_forward_call(first, qkv, seg, kernel, logdec, marks, after=()):
    length, tiles, taps = qkv.shape[0], qkv.shape[1] // (3 * LANES), kernel.shape[0]
    chunks, wide = length // CHUNK, tiles * LANES
    whole, tables = h3_specs(length, taps, kernel.shape[1], chunks)
    return kernel_call(
        functools.partial(h3_forward_body, first, tiles, taps),
        [made((length, wide)), made((length, wide), jnp.float32), made((tiles, chunks, LANES, LANES), jnp.float32)],
        [
            pltpu.VMEM((length + taps, wide), jnp.float32),
            pltpu.VMEM((CHUNK + taps, wide), jnp.float32),
            pltpu.VMEM((tiles, LANES, LANES), jnp.float32),
        ],
        (1,),
        [whole(*qkv.shape)] + tables,
        [whole(length, wide), whole(length, wide), whole(tiles, chunks, LANES, LANES)],
        1,
        "h3_forward",
        after,
        10 * tiles,
    )(seg, qkv, kernel, logdec, *marks)


def h3_backward_body(
    first, tiles, taps, seg_s, qkv_ref, shift_ref, grad_ref, w_ref, logdec_ref, segb_ref, segl_ref,
    state_ref, dqkv_ref, dw_ref, dlog_ref, key_f, grad_f, masked, masked_grad, state, tap_sums, log_sum,
):
    length = qkv_ref.shape[0]
    chunks, half, core = length // CHUNK, length // 2, seg_s[length]
    tables = [decays(logdec_ref[:, tile_of(first + tile)]) for tile in range(tiles)]
    heads, diagonal = lane_heads(), head_diagonal()
    key_f[0:taps, :] = jnp.zeros((taps, tiles * LANES), jnp.float32)

    def copy_keys(n, _):
        at = pl.multiple_of(n * CHUNK, CHUNK)
        for tile in range(tiles):
            keys = split_columns(qkv_ref, tile)[1][pl.ds(place_of(n, core, half), CHUNK), :]
            key_f[pl.ds(at + taps, CHUNK), tile_of(tile)] = wide32(keys)
        return 0

    lax.fori_loop(0, chunks, copy_keys, 0)
    grad_f[length:, :] = jnp.zeros((taps, tiles * LANES), jnp.float32)
    state[...] = jnp.zeros_like(state)
    tap_sums[...] = jnp.zeros_like(tap_sums)
    log_sum[...] = jnp.zeros_like(log_sum)
    masked_grad[CHUNK + taps :, :] = jnp.zeros((8, tiles * LANES), jnp.float32)

    def chunk_step(back, _):
        n = chunks - 1 - back
        at, low_doc, high_doc, before = documents(seg_s, n)
        here = pl.ds(place_of(n, core, half), CHUNK)
        seg_here = segb_ref[pl.ds(at + taps, CHUNK), :]
        gate, ends = wide32(seg_here == before), wide32(seg_here == high_doc)
        carry = jnp.where(high_doc == before, 1.0, 0.0)
        same = causal_same(seg_here, segl_ref[pl.ds(n, 1), :])
        work = []
        for tile in range(tiles):
            _, rising, falling, *_ = tables[tile]
            q_ref, _, v_ref = split_columns(qkv_ref, tile)
            q_up = low16(wide32(q_ref[here, :]) * rising)
            k_down = low16(shift_ref[pl.ds(at, CHUNK), tile_of(tile)] * falling)
            work.append((q_up, k_down, v_ref[here, :], grad_ref[here, tile_of(first + tile)]))
        squares = []
        for q_up, k_down, value, grad in work:
            for head in heads:
                mixing = dot_nt(jnp.where(head, q_up, jnp.zeros_like(q_up)), k_down)
                grad_mixing = dot_nt(jnp.where(head, grad, jnp.zeros_like(grad)), value)
                squares.append([low16(jnp.where(same, square, 0.0)) for square in (mixing, grad_mixing)])
        for tile, (q_up, k_down, value, grad) in enumerate(work):
            steps, rising, falling, one, last, whole = tables[tile]
            lanes = tile_of(tile)
            dqkv = split_columns(dqkv_ref, tile)
            mine = squares[tile * len(heads) : (tile + 1) * len(heads)]
            dq_local = pick_heads(heads, [dot_nn(grad_mixing, k_down) for _, grad_mixing in mine])
            dk_local = pick_heads(heads, [dot_tn(grad_mixing, q_up) for _, grad_mixing in mine])
            dv = pick_heads(heads, [dot_tn(mixing, grad) for mixing, _ in mine])
            entering, leaving = state_ref[tile, n], state[tile]
            leaving_low = low16(leaving)
            reach = dot_nn(grad, low16(entering)) * (one * gate)
            spread = dot_nn(value, leaving_low) * (last * ends)
            q_up_f, k_down_f = wide32(q_up), wide32(k_down)
            dqkv[0][here, :] = low16((dq_local + reach) * rising)
            dqkv[2][here, :] = low16(dv + dot_nt(low16(k_down_f * (last * ends)), leaving_low))
            terms = steps * (q_up_f * dq_local - k_down_f * dk_local)
            terms = terms + (steps + 1.0) * q_up_f * reach + (CHUNK - 1.0 - steps) * k_down_f * spread
            log_sum[:, lanes] += terms + (CHUNK * carry) * (leaving * entering * whole)
            lead = dot_tn(low16(wide32(grad) * gate), q_up) * one
            state[tile] = leaving * (whole * carry) + jnp.where(diagonal, lead, 0.0)
            grad_f[pl.ds(at, CHUNK), lanes] = (dk_local + spread) * falling

        def one_doc(doc, totals):
            after = segb_ref[pl.ds(at + taps, CHUNK + taps), :] == doc
            ahead = segb_ref[pl.ds(at, CHUNK + taps), :] == doc
            result = []
            for tile in range(tiles):
                lanes = tile_of(tile)
                ahead_grad = jnp.where(after, grad_f[pl.ds(at, CHUNK + taps), lanes], 0.0)
                masked_grad[0 : CHUNK + taps, lanes] = ahead_grad
                masked[:, lanes] = jnp.where(ahead, key_f[pl.ds(at, CHUNK + taps), lanes], 0.0)
                own = jnp.concatenate([jnp.zeros((8, LANES), jnp.float32), masked_grad[0:CHUNK, lanes]], axis=0)
                conv = jnp.zeros((CHUNK, LANES), jnp.float32)
                for b in range(8):
                    part = jnp.zeros((CHUNK + 8, LANES), jnp.float32)
                    moved = pltpu.roll(own, CHUNK + 8 - b, 0) if b else own
                    for a in range(taps // 8):
                        tap = 8 * a + b
                        here_grad = masked_grad[8 * a : 8 * a + CHUNK + 8, lanes]
                        part = part + w_ref[tap : tap + 1, tile_of(first + tile)] * here_grad
                        seen = masked[taps - 8 - 8 * a : taps + CHUNK - 8 * a, lanes]
                        tap_sums[tap, :, lanes] += jnp.sum((moved * seen).reshape(-1, 8, LANES), axis=0)
                    if b:
                        part = pltpu.roll(part, CHUNK + 8 - b, 0)
                    conv = conv + part[:CHUNK, :]
                result.append(totals[tile] + jnp.where(seg_here == doc, conv, 0.0))
            return tuple(result)

        zero = jnp.zeros((CHUNK, LANES), jnp.float32)
        dks = lax.fori_loop(low_doc, high_doc + 1, one_doc, (zero,) * tiles)
        for tile in range(tiles):
            split_columns(dqkv_ref, tile)[1][here, :] = low16(dks[tile])
        return 0

    lax.fori_loop(0, chunks, chunk_step, 0)
    dw_ref[...] = jnp.sum(tap_sums[...], axis=1)
    dlog_ref[...] = jnp.sum(log_sum[...], axis=0, keepdims=True)


def h3_backward_call(first, qkv, shifted, grad, states, seg, kernel, logdec, marks, after=()):
    length, tiles, taps = qkv.shape[0], qkv.shape[1] // (3 * LANES), kernel.shape[0]
    chunks, wide = length // CHUNK, tiles * LANES
    whole, tables = h3_specs(length, taps, kernel.shape[1], chunks)
    tall = [pltpu.VMEM((n, wide), jnp.float32) for n in (length + taps, length + taps, CHUNK + taps, CHUNK + taps + 8)]
    return kernel_call(
        functools.partial(h3_backward_body, first, tiles, taps),
        [made(qkv.shape), made((taps, wide), jnp.float32), made((1, wide), jnp.float32)],
        tall
        + [
            pltpu.VMEM((tiles, LANES, LANES), jnp.float32),
            pltpu.VMEM((taps, 8, wide), jnp.float32),
            pltpu.VMEM((CHUNK, wide), jnp.float32),
        ],
        (1,),
        [whole(*qkv.shape), whole(*shifted.shape), whole(*grad.shape)] + tables + [whole(*states.shape)],
        [whole(*qkv.shape), whole(taps, wide), whole(1, wide)],
        1,
        "h3_backward",
        after,
        16 * tiles,
    )(seg, qkv, shifted, grad, kernel, logdec, *marks, states)


score_unit = 1.0 / math.sqrt(HEAD_DIM)


def row_block(ref, i, core, half):
    parts = [ref[pl.ds(place_of(2 * i + step, core, half), CHUNK), :] for step in range(2)]
    return jnp.concatenate(parts, axis=0)


def put_block(ref, i, core, half, block):
    for step in range(2):
        ref[pl.ds(place_of(2 * i + step, core, half), CHUNK), :] = block[step * CHUNK : (step + 1) * CHUNK, :]


def head_rows(block):
    lane, zero = lax.broadcasted_iota(jnp.int32, block.shape, 1), jnp.zeros_like(block)
    parts = [jnp.where(lane // HEAD_DIM == head, block, zero) for head in range(LANES // HEAD_DIM)]
    return jnp.concatenate(parts, axis=0)


def allowed_tile(first, segb_ref, segl_ref, q_block, k_block):
    seg_keys = segb_ref[first + k_block * BLOCK : first + (k_block + 1) * BLOCK, :]
    seg_keys = jnp.concatenate([seg_keys] * (BLOCK // LANES), axis=1)
    allowed = seg_keys == segl_ref[q_block : q_block + 1, :]
    if q_block == k_block:
        row = lax.broadcasted_iota(jnp.int32, (BLOCK, BLOCK), 0)
        lane = lax.broadcasted_iota(jnp.int32, (BLOCK, BLOCK), 1)
        allowed = allowed & (row <= lane)
    return jnp.concatenate([allowed] * (LANES // HEAD_DIM), axis=1)


def picked_rows(tall):
    parts = []
    for head in range(LANES // HEAD_DIM):
        rows = slice(head * HEAD_DIM, (head + 1) * HEAD_DIM)
        parts.append(tall[rows, head * BLOCK : (head + 1) * BLOCK])
    return jnp.concatenate(parts, axis=0)


def att_forward_body(first, seg_s, qkv_ref, segb_ref, segl_ref, out_ref, total_ref, key, value, score):
    length = qkv_ref.shape[0]
    q_ref, k_ref, v_ref = split_columns(qkv_ref)
    blocks, half, core = length // BLOCK, length // 2, seg_s[length]
    for i in range(blocks):
        key[i * BLOCK : (i + 1) * BLOCK, :] = row_block(k_ref, i, core, half)
        value[i * BLOCK : (i + 1) * BLOCK, :] = row_block(v_ref, i, core, half)
    for i in range(blocks):
        query = head_rows(row_block(q_ref, i, core, half) * jnp.bfloat16(score_unit))
        top = jnp.full((1, 2 * BLOCK), masked_score, jnp.float32)
        for j in range(i + 1):
            keys = slice(j * BLOCK, (j + 1) * BLOCK)
            tile = dot_nt(key[keys, :], query)
            tile = jnp.where(allowed_tile(first, segb_ref, segl_ref, i, j), tile, masked_score)
            score[keys, :] = tile
            top = jnp.maximum(top, jnp.max(tile, axis=0, keepdims=True))
        total = jnp.zeros((1, 2 * BLOCK), jnp.float32)
        tall = jnp.zeros((LANES, 2 * BLOCK), jnp.float32)
        for j in range(i + 1):
            keys = slice(j * BLOCK, (j + 1) * BLOCK)
            expd = jnp.exp(score[keys, :] - top)
            total = total + jnp.sum(expd, axis=0, keepdims=True)
            tall = tall + dot_tn(value[keys, :], low16(expd))
        put_block(out_ref, i, core, half, low16(picked_rows(tall / total).T))
        total_ref[i : i + 1, :] = top + jnp.log(total)


def att_backward_body(
    first, seg_s, qkv_ref, grad_ref, total_ref, segb_ref, segl_ref, dqkv_ref,
    key, value, probs, grad_probs, dk_sum, dv_sum,
):
    length = qkv_ref.shape[0]
    q_ref, k_ref, v_ref = split_columns(qkv_ref)
    dq_ref, dk_ref, dv_ref = split_columns(dqkv_ref)
    blocks, half, core = length // BLOCK, length // 2, seg_s[length]
    for i in range(blocks):
        key[i * BLOCK : (i + 1) * BLOCK, :] = row_block(k_ref, i, core, half)
        value[i * BLOCK : (i + 1) * BLOCK, :] = row_block(v_ref, i, core, half)
    for i in range(blocks):
        query = head_rows(row_block(q_ref, i, core, half) * jnp.bfloat16(score_unit))
        grad = head_rows(row_block(grad_ref, i, core, half))
        inner = jnp.zeros((1, 2 * BLOCK), jnp.float32)
        for j in range(i + 1):
            keys = slice(j * BLOCK, (j + 1) * BLOCK)
            tile = dot_nt(key[keys, :], query) - total_ref[i : i + 1, :]
            tile = jnp.exp(jnp.where(allowed_tile(first, segb_ref, segl_ref, i, j), tile, masked_score))
            grad_tile = dot_nt(value[keys, :], grad)
            probs[keys, :] = tile
            grad_probs[keys, :] = grad_tile
            inner = inner + jnp.sum(tile * grad_tile, axis=0, keepdims=True)
        tall = jnp.zeros((LANES, 2 * BLOCK), jnp.float32)
        for j in range(i + 1):
            keys = slice(j * BLOCK, (j + 1) * BLOCK)
            tile = probs[keys, :]
            grad_score = low16(tile * (grad_probs[keys, :] - inner))
            dk, dv = dot_nn(grad_score, query), dot_nn(low16(tile), grad)
            if i == j:
                dk_sum[keys, :], dv_sum[keys, :] = dk, dv
            else:
                dk_sum[keys, :] += dk
                dv_sum[keys, :] += dv
            tall = tall + dot_tn(key[keys, :], grad_score)
        put_block(dq_ref, i, core, half, low16(picked_rows(tall).T * score_unit))
    for i in range(blocks):
        put_block(dk_ref, i, core, half, low16(dk_sum[i * BLOCK : (i + 1) * BLOCK, :]))
        put_block(dv_ref, i, core, half, low16(dv_sum[i * BLOCK : (i + 1) * BLOCK, :]))


def att_specs(length, wide, marks):
    own = lambda columns: pl.BlockSpec((length, columns), lambda i, s: (0, i))
    whole = [pl.BlockSpec(mark.shape, lambda i, s: (0, 0)) for mark in marks]
    totals = pl.BlockSpec((None, length // BLOCK, 2 * BLOCK), lambda i, s: (i, 0, 0))
    return wide // LANES, own, whole, totals


def att_forward_call(first, seg, qkv, marks, *after):
    length, wide = qkv.shape[0], qkv.shape[1] // 3
    tiles, own, whole, totals = att_specs(length, wide, marks)
    return kernel_call(
        functools.partial(att_forward_body, first),
        [made((length, wide)), made((tiles, length // BLOCK, 2 * BLOCK), jnp.float32)],
        [pltpu.VMEM((length, LANES), jnp.bfloat16)] * 2 + [pltpu.VMEM((length, 2 * BLOCK), jnp.float32)],
        (tiles,),
        [own(3 * LANES)] + whole,
        [own(LANES), totals],
        1,
        "att_forward",
        after,
        11,
    )(seg, qkv, *marks)


def att_backward_call(first, seg, qkv, grad, total, marks, *after):
    length, wide = grad.shape
    tiles, own, whole, totals = att_specs(length, wide, marks)
    return kernel_call(
        functools.partial(att_backward_body, first),
        [made(qkv.shape)],
        [pltpu.VMEM((length, LANES), jnp.bfloat16)] * 2
        + [pltpu.VMEM((length, 2 * BLOCK), jnp.float32)] * 2
        + [pltpu.VMEM((length, LANES), jnp.float32)] * 2,
        (tiles,),
        [own(3 * LANES), own(LANES), totals] + whole,
        [own(3 * LANES)],
        1,
        "att_backward",
        after,
        18,
    )(seg, qkv, grad, total, *marks)[0]


def tile_rows(i, quarter, rest):
    found = []
    for kind in range(3):
        for unit in range(2):
            head = (unit * quarter, LANES, kind * LANES)
            tail = (unit * quarter + LANES, rest, 3 * LANES + kind * rest)
            for first, count, row in (head, tail):
                low, high = max(first, i * LANES), min(first + count, (i + 1) * LANES)
                if low < high:
                    found.append((unit, row + low - first, kind * LANES + low - i * LANES, high - low))
    return found


def join_body(first, own_ref, far_ref, out_ref):
    quarter = own_ref.shape[0] // 3
    for i in range(out_ref.shape[0] // (3 * LANES)):
        for unit, row, at, count in tile_rows(first + i, quarter, quarter - LANES):
            at += i * 3 * LANES
            out_ref[at : at + count, :] = (own_ref, far_ref)[unit][row : row + count, :]


def joined_tiles(first, tiles, own, far, *after):
    shape = (tiles * 3 * LANES, own.shape[1])
    body = functools.partial(join_body, first)
    return kernel_call(body, [made(shape)], name="join", after=after)(own, far)[0]


def stack_body(one_ref, two_ref, out_ref):
    rows = one_ref.shape[0]
    out_ref[:rows, :] = one_ref[...]
    out_ref[rows:, :] = two_ref[...]


def stacked(one, two, *after):
    shape = (one.shape[0] + two.shape[0], one.shape[1])
    return kernel_call(stack_body, [made(shape)], name="stack", after=after)(one, two)[0]


def pack_body(q_ref, k_ref, v_ref, *refs):
    unit_ref, quarter = refs[-1], q_ref.shape[0]
    rest = quarter - LANES
    for kind, ref in enumerate((q_ref, k_ref, v_ref)):
        unit_ref[kind * LANES : (kind + 1) * LANES, :] = ref[:LANES, :]
        unit_ref[3 * LANES + kind * rest : 3 * LANES + (kind + 1) * rest, :] = ref[LANES:, :]
    for ref in refs[:-1]:
        unit_ref[3 * quarter :, :] = ref[...]


def packed(parts, *after):
    shape = (sum(part.shape[0] for part in parts), parts[0].shape[1])
    return kernel_call(pack_body, [made(shape)], name="pack", after=after)(*parts)[0]


def put_grads(first, x_ref, dqkv_ref, units, quarter):
    for i in range(dqkv_ref.shape[1] // (3 * LANES)):
        total = dot_tn(dqkv_ref[:, i * 3 * LANES : (i + 1) * 3 * LANES], x_ref[...])
        for unit, row, at, count in tile_rows(first + i, quarter, quarter - LANES):
            units[unit][row : row + count, :] = low16(total[at : at + count, :])


def far_grads_body(first, x_ref, dqkv_ref, g_ref, *refs):
    outs, unit_ref, far_ref = refs[:-2], refs[-2], refs[-1]
    quarter = unit_ref.shape[0] // 4
    put_grads(first, x_ref, dqkv_ref, (unit_ref, far_ref), quarter)
    at = 3 * quarter
    total = jnp.concatenate([dot_tn(ref[...], g_ref[...]) for ref in outs[: len(outs) - 1 + (first == 0)]], axis=0)
    unit_ref[at:, :] = low16(total[:quarter, :])
    far_ref[at : at + quarter, :] = low16(total[quarter:, :])
    if first:
        far_ref[at + quarter :, :] = outs[-1][...]


def far_grads(first, x, dqkv, g, outs, *small, after=()):
    quarter, width = sum(out.shape[1] for out in outs) // 2, x.shape[1]
    shapes = [(4 * quarter, width), (4 * quarter + sum(rows.shape[0] for rows in small), width)]
    body = functools.partial(far_grads_body, first)
    return kernel_call(body, [made(shape) for shape in shapes], name="far_grads", after=after)(x, dqkv, g, *outs, *small)


def own_grads_body(x_ref, dqkv_ref, rest_ref, small_ref, unit_ref):
    quarter = rest_ref.shape[0] // 4
    put_grads(0, x_ref, dqkv_ref, (unit_ref, unit_ref), quarter)
    unit_ref[3 * LANES : 4 * quarter, :] = rest_ref[3 * LANES :, :]
    unit_ref[4 * quarter :, :] = small_ref[...]


def own_grads(x, dqkv, rest, small, *after):
    shape = (rest.shape[0] + small.shape[0], x.shape[1])
    return kernel_call(own_grads_body, [made(shape)], name="own_grads", after=after)(x, dqkv, rest, small)[0]


def gelu_and_slope(value):
    bell = jnp.exp(value * value * -0.5)
    below = 0.5 + 0.5 * lax.erf(value * math.sqrt(0.5))
    return value * below, below + value * bell * (1.0 / math.sqrt(2.0 * math.pi))


def ff_forward_body(x_ref, in_own, in_far, out_own, out_far, *refs):
    own_ref, other_ref = refs[-2:]
    total = None
    for i, (w_in, w_out) in enumerate(((in_own, out_own), (in_far, out_far))):
        hidden, slope = gelu_and_slope(dot_nn(x_ref[...], w_in[...]))
        hidden = low16(hidden)
        refs[i][...] = hidden
        refs[2 + i][...] = low16(slope)
        part = dot_nn(hidden, w_out[...])
        total = part if total is None else total + part

    @pl.when(pl.program_id(0) == 0)
    def _():
        other_ref[...] = low16(total)

    @pl.when(pl.program_id(0) == 1)
    def _():
        own_ref[...] = total


def ff_forward_call(x, w_in, w_out, far):
    half, width, units = x.shape[0] // 2, x.shape[1], w_in.shape[1]
    flipped = lambda columns: pl.BlockSpec((half, columns), lambda i: (1 - i, 0))
    rows = pl.BlockSpec((half, width), lambda i: (0, 0))
    weight = lambda at: pl.BlockSpec((width, units), lambda i: (at, 0))
    return kernel_call(
        ff_forward_body,
        [made((2 * half, units))] * 4 + [made((half, width), jnp.float32), made((half, width))],
        grid=(2,),
        in_specs=[flipped(width), weight(0), weight(0), weight(0), weight(1)],
        out_specs=[flipped(units)] * 4 + [rows, rows],
        name="ff_forward",
        cost=12,
    )(x, w_in, far, w_out, far)


def standardized(stream):
    centered = stream - jnp.mean(stream, axis=-1, keepdims=True)
    scale = lax.rsqrt(jnp.mean(centered * centered, axis=-1, keepdims=True) + norm_eps)
    return centered * scale, scale


def deal_rows_body(place, array_ref, *refs):
    for by, ref in enumerate(refs):
        ref[...] = low16(array_ref[place[2] ^ by])


def deal_rows(place, array, *after):
    count, *shape = array.shape
    return kernel_call(
        deal_rows_body,
        [made(tuple(shape))] * count,
        grid=(1,),
        in_specs=[pl.BlockSpec(array.shape, lambda i, s: (0, 0, 0))],
        out_specs=[pl.BlockSpec(tuple(shape), lambda i, s: (0, 0))] * count,
        scalars=1,
        name="deal_rows",
        after=after,
    )(place, array)


def collect_rows_body(place, *refs):
    for by, ref in enumerate(refs[:-1]):
        refs[-1][place[2] ^ by] = ref[...].astype(refs[-1].dtype)


def collect_rows(place, parts, kind, *after):
    shape = (len(parts), *parts[0].shape)
    return kernel_call(
        collect_rows_body,
        [made(shape, kind)],
        grid=(1,),
        in_specs=[pl.BlockSpec(parts[0].shape, lambda i, s: (0, 0))] * len(parts),
        out_specs=[pl.BlockSpec(shape, lambda i, s: (0, 0, 0))],
        scalars=1,
        name="collect_rows",
        after=after,
    )(place, *parts)[0]


def first_norm_body(place, *refs):
    *parts, gain_ref, stream_ref, normed_ref = refs
    rows = parts[0].shape[0]
    for by, ref in enumerate(parts):
        here = pl.ds(pl.multiple_of((place[2] ^ by) * rows, rows), rows)
        stream = wide32(ref[...])
        stream_ref[here, :] = stream
        normed_ref[here, :] = low16(standardized(stream)[0] * gain_ref[...])


def first_norm(place, parts, gain, *after):
    rows, width = parts[0].shape
    shape = (rows * len(parts), width)
    whole = lambda shape: pl.BlockSpec(shape, lambda i, s: (0, 0))
    return kernel_call(
        first_norm_body,
        [made(shape, jnp.float32), made(shape)],
        grid=(1,),
        in_specs=[whole(part.shape) for part in parts] + [whole(gain.shape)],
        out_specs=[whole(shape)] * 2,
        scalars=1,
        name="first_norm",
        after=after,
    )(place, *parts, gain)


def touch_body(*refs):
    pass


def touched(arrays, *after):
    anywhere = pl.BlockSpec(memory_space=pl.ANY)
    return pl.pallas_call(
        touch_body,
        in_specs=[anywhere] * (len(arrays) + len(after)),
        out_specs=[anywhere] * len(arrays),
        out_shape=[made(array.shape, array.dtype) for array in arrays],
        input_output_aliases={i: i for i in range(len(arrays))},
        cost_estimate=pl.CostEstimate(flops=0, bytes_accessed=0, transcendentals=0),
        name="touch",
    )(*arrays, *after)


def add_norm_body(stream_ref, own_ref, recv_ref, gain_ref, sum_ref, normed_ref):
    stream = stream_ref[...] + (own_ref[...] + wide32(recv_ref[...]))
    sum_ref[...] = stream
    normed_ref[...] = low16(standardized(stream)[0] * gain_ref[...])


def add_norm(stream, own, recv, gain, *after):
    outs = [made(stream.shape, jnp.float32), made(stream.shape)]
    return kernel_call(add_norm_body, outs, name="add_norm", after=after)(stream, own, recv, gain)


def norm_back_body(grad_ref, own_ref, recv_ref, stream_ref, gain_ref, sum_ref, low_ref):
    xhat, scale = standardized(stream_ref[...])
    e = (own_ref[...] + wide32(recv_ref[...])) * gain_ref[...]
    inner = jnp.mean(e * xhat, axis=-1, keepdims=True)
    back = scale * (e - jnp.mean(e, axis=-1, keepdims=True) - xhat * inner)
    total = grad_ref[...] + back
    sum_ref[...] = total
    low_ref[...] = low16(total)


def norm_back(grad, own, recv, stream, gain, *after):
    outs = [made(grad.shape, jnp.float32), made(grad.shape)]
    return kernel_call(norm_back_body, outs, name="norm_back", after=after)(grad, own, recv, stream, gain)


def fold_body(place, own_keep, recv_keep, own_send, recv_send, keep_ref, send_ref):
    send_ref[...] = low16(wide32(own_send[...]) + wide32(recv_send[...]))
    keep_ref[...] = low16(wide32(own_keep[...]) + wide32(recv_keep[...]))


def fold(place, own, recv, *after):
    shape = (own.shape[0] // 2, own.shape[1])
    keep = pl.BlockSpec(shape, lambda i, s: (s[0], 0))
    send = pl.BlockSpec(shape, lambda i, s: (1 - s[0], 0))
    same = pl.BlockSpec(shape, lambda i, s: (0, 0))
    return kernel_call(
        fold_body,
        [made(shape)] * 2,
        grid=(1,),
        in_specs=[keep, keep, send, send],
        out_specs=[same] * 2,
        scalars=1,
        name="fold",
        after=after,
    )(place, own, recv, own, recv)


def ff_fold_body(place, own_in, recv_in, own_out, recv_out, keep_ref, send_ref):
    both_in = low16(wide32(own_in[...]) + wide32(recv_in[...]))
    both_out = low16(wide32(own_out[...]) + wide32(recv_out[...]))
    keep_ref[...] = jnp.where(place[0] == 0, both_in, both_out)
    send_ref[...] = jnp.where(place[0] == 0, both_out, both_in)


def ff_fold(place, own, recv, *after):
    shape = own[0].shape
    same = pl.BlockSpec(shape, lambda i, s: (0, 0))
    return kernel_call(
        ff_fold_body,
        [made(shape)] * 2,
        grid=(1,),
        in_specs=[same] * 4,
        out_specs=[same] * 2,
        scalars=1,
        name="ff_fold",
        after=after,
    )(place, own[0], recv[0], own[1], recv[1])


def add_two_body(one_ref, two_ref, out_ref):
    out_ref[...] = low16(wide32(one_ref[...]) + wide32(two_ref[...]))


def add_two(one, two, *after):
    return kernel_call(add_two_body, [made(one.shape)], name="add_two", after=after)(one, two)[0]


def deal_body(count, place, *refs):
    for i in range(count):
        refs[2 * count + i][...] = low16(wide32(refs[i][...]) + wide32(refs[count + i][...]))


def deal(place, one, two, count, *after):
    shape = (one.shape[0] // count, one.shape[1])
    parts = [pl.BlockSpec(shape, lambda i, s, by=by: (s[1] ^ by, 0)) for by in range(count)]
    same = pl.BlockSpec(shape, lambda i, s: (0, 0))
    return kernel_call(
        functools.partial(deal_body, count),
        [made(shape)] * count,
        grid=(1,),
        in_specs=parts * 2,
        out_specs=[same] * count,
        scalars=1,
        name="deal",
        after=after,
    )(place, *([one] * count), *([two] * count))


def add_all_body(*refs):
    total = wide32(refs[0][...])
    for ref in refs[1:-1]:
        total = total + wide32(ref[...])
    refs[-1][...] = low16(total)


def add_all(parts, *after):
    return kernel_call(add_all_body, [made(parts[0].shape)], name="add_all", after=after)(*parts)[0]


def gather_body(place, *refs):
    out_ref, rows = refs[-1], refs[0].shape[0]
    for by, ref in enumerate(refs[:-1]):
        out_ref[pl.ds(pl.multiple_of((place[1] ^ by) * rows, 16), rows), :] = ref[...]


def gather_parts(place, parts, *after):
    rows, columns = parts[0].shape
    whole = pl.BlockSpec((rows, columns), lambda i, s: (0, 0))
    shape = (rows * len(parts), columns)
    return kernel_call(
        gather_body,
        [made(shape)],
        grid=(1,),
        in_specs=[whole] * len(parts),
        out_specs=[pl.BlockSpec(shape, lambda i, s: (0, 0))],
        scalars=1,
        name="gather_parts",
        after=after,
    )(place, *parts)[0]


def ff_finish_body(all_ref, w_ref, gain_ref, in_ref, out_ref, gain_grad_ref):
    width = w_ref.shape[0]
    out_ref[...] = wide32(all_ref[:width, :])
    grad = wide32(all_ref[width:, :])
    in_ref[...] = grad
    sums = jnp.sum(grad * wide32(w_ref[...]), axis=1, keepdims=True)
    gain_grad_ref[...] = jnp.broadcast_to(sums, (width, LANES)).T[:8, :] / gain_ref[...]


def ff_finish(summed, w_in, gain, *after):
    shapes = [w_in.shape, w_in.shape, (8, w_in.shape[0])]
    return kernel_call(ff_finish_body, [made(shape, jnp.float32) for shape in shapes], name="ff_finish", after=after)(
        summed, w_in, gain
    )


def mixer_finish_body(place, half_ref, recv_ref, w_ref, gain_ref, *refs):
    *outs, gain_grad_ref, unit = refs
    rows, quarter = half_ref.shape[0], outs[0].shape[0]
    rest = quarter - LANES
    for by, ref in enumerate((half_ref, recv_ref)):
        unit[pl.ds(pl.multiple_of((place[0] ^ by) * rows, 16), rows), :] = wide32(ref[...])
    for kind in range(3):
        outs[kind][:LANES, :] = unit[kind * LANES : (kind + 1) * LANES, :]
        outs[kind][LANES:, :] = unit[3 * LANES + kind * rest : 3 * LANES + (kind + 1) * rest, :]
    outs[3][...] = unit[3 * quarter : 4 * quarter, :]
    if len(outs) > 4:
        outs[4][...] = unit[4 * quarter :, :]
    sums = jnp.sum(unit[: 3 * quarter, :] * wide32(w_ref[...]), axis=0, keepdims=True)
    gain_grad_ref[...] = jnp.broadcast_to(sums / gain_ref[...], gain_grad_ref.shape)


def mixer_finish(place, half, recv, weights, gain, *after):
    rows, columns = half.shape
    quarter = weights.shape[0] // 3
    whole = lambda *shape: pl.BlockSpec(shape, lambda i, s: (0, 0))
    shapes = [(quarter, columns)] * 4 + [(2 * rows - 4 * quarter, columns)] * (2 * rows > 4 * quarter) + [(8, columns)]
    return kernel_call(
        mixer_finish_body,
        [made(shape, jnp.float32) for shape in shapes],
        [pltpu.VMEM((2 * rows, columns), jnp.float32)],
        (1,),
        [whole(rows, columns)] * 2 + [whole(*weights.shape), whole(*gain.shape)],
        [whole(*shape) for shape in shapes],
        1,
        "mixer_finish",
        after,
    )(place, half, recv, weights, gain)


def share_body(place, in_ref, out_ref, share_ref):
    share_ref[...] = jnp.where(place[0] == 0, in_ref[...], out_ref[...])


def far_share(place, w_in, w_out, count, *after):
    shape = (w_in.shape[0] // count, w_in.shape[1])
    rows = pl.BlockSpec(shape, lambda i, s: (s[1], 0))
    return kernel_call(
        share_body,
        [made(shape)],
        grid=(1,),
        in_specs=[rows, rows],
        out_specs=[pl.BlockSpec(shape, lambda i, s: (0, 0))],
        scalars=1,
        name="far_share",
        after=after,
    )(place, w_in, w_out)[0]


def exchanged(array, axis, by):
    devices = lax.axis_size(axis)
    return lax.ppermute(array, axis, [(i, i ^ by) for i in range(devices)])


def core_swap(array):
    return exchanged(array, TENSOR, 1)


def half_swap(array):
    return exchanged(array, TENSOR, 2)


def chip_place():
    return lax.axis_index(SEQ) * (lax.axis_size(TENSOR) // 2) + lax.axis_index(TENSOR) // 2


def swapped_rows(parts):
    return [parts[0]] + [exchanged(part, (SEQ, TENSOR), 2 * by) for by, part in enumerate(parts) if by]


def nt(left, right):
    return dot_nt(left, right)


def tn(left, right):
    return dot_tn(left, right)


def with_other(own):
    return jnp.concatenate([own, core_swap(own)], axis=0)


def closing(parts):
    half = parts[0][0].shape[0] // 2
    other = sum(dot(left[half:], right, over) for left, right, over in parts)
    own = sum(dot(left[:half], right, over) for left, right, over in parts)
    return own, core_swap(low16(other))


def row_shards(
    tokens,
    out_grad,
    segments,
    gain_mix,
    query_mix,
    key_mix,
    value_mix,
    output_mix,
    shift_kernel,
    decay_rate,
    gain_ff1,
    ff_in1,
    ff_out1,
    gain_att,
    query_att,
    key_att,
    value_att,
    output_att,
    gain_ff2,
    ff_in2,
    ff_out2,
):
    features = tokens.shape[2]
    taps, quarter = shift_kernel.shape
    length = segments.shape[1]
    place = jnp.stack([lax.axis_index(SEQ), lax.axis_index(DP), chip_place()]).astype(jnp.int32)
    count = lax.axis_size(DP)

    mine = deal_rows(place, tokens)
    share = half_swap(far_share(place, ff_in1, ff_out1, count, mine[0]))
    mix_own = packed([query_mix.T, key_mix.T, value_mix.T], mine[0])
    mine = swapped_rows(mine)
    mix_far = half_swap(mix_own)
    far_one = lax.all_gather(share, (SEQ, DP), axis=0, tiled=True)
    few = jnp.concatenate([shift_kernel, decay_rate.reshape(1, -1) * (-1.0 / length)], axis=0)
    both = jnp.concatenate([few, half_swap(few)], axis=1)

    seg_row = lax.dynamic_index_in_dim(segments, chip_place(), 0, False)
    core = (lax.axis_index(TENSOR) % 2).astype(jnp.int32)
    seg = jnp.concatenate([seg_row, core.reshape(1)])
    padded = jnp.pad(seg_row, (taps, taps), constant_values=-1)
    segb = jnp.broadcast_to(padded[:, None], (padded.shape[0], LANES))
    marks = (segb, seg_row.reshape(-1, CHUNK))
    att_marks = (segb, seg_row.reshape(-1, BLOCK))
    gains = [gain.reshape(1, -1) for gain in (gain_mix, gain_ff1, gain_att, gain_ff2)]
    h3 = [{"seg": seg, "kernel": table[:taps], "logdec": table[taps:], "marks": marks} for table in (few, both)]

    stream0, normed = first_norm(place, mine, gains[0])
    x_mix = with_other(normed)
    mix_w = [mix_own[: 3 * LANES]]
    qkv_mix = [low16(nt(x_mix, mix_w[0]))]
    kept_mix = [h3_forward_call(0, qkv_mix[0], **h3[0])]
    mix_w.append(joined_tiles(1, 2, mix_own, mix_far, kept_mix[0][0]))
    qkv_mix.append(low16(nt(x_mix, mix_w[1])))
    share = half_swap(far_share(place, ff_in2, ff_out2, count, mix_w[1]))
    mix_o = half_swap(output_mix)
    kept_mix.append(touched(h3_forward_call(1, qkv_mix[1], **h3[1]), share, mix_o))
    out_mix = [kept[0] for kept in kept_mix]
    mix_o = stacked(output_mix, mix_o, out_mix[1])
    far_two = lax.all_gather(share, (SEQ, DP), axis=0, tiled=True)
    att_own = packed([query_att.T, key_att.T, value_att.T], mix_w[1])
    out_w = [mix_o[:LANES], mix_o[LANES:]]
    sums = closing([(out, weight, over_nn) for out, weight in zip(out_mix, out_w)])
    stream1, normed = add_norm(stream0, *sums, gains[1])
    x_one = with_other(normed)
    att_far = half_swap(att_own)
    kept_one = touched(ff_forward_call(x_one, ff_in1, ff_out1, far_one), att_far)
    att_w = joined_tiles(0, 3, att_own, att_far, kept_one[4])
    stream2, normed = add_norm(stream1, kept_one[4], core_swap(kept_one[5]), gains[2])
    x_att = with_other(normed)
    qkv_att = low16(nt(x_att, att_w))
    back_parts = swapped_rows(deal_rows(place, out_grad, kept_one[4]))
    att_o = half_swap(output_att)
    out_att, total = touched(att_forward_call(taps, seg, qkv_att, att_marks), *back_parts[1:], att_o, far_two)
    att_o = stacked(output_att, att_o, out_att)
    back_low = collect_rows(place, back_parts, jnp.bfloat16, out_att).reshape(-1, features)
    stream3, normed = add_norm(stream2, *closing([(out_att, att_o, over_nn)]), gains[3])
    x_two = with_other(normed)
    kept_two = ff_forward_call(x_two, ff_in2, ff_out2, far_two)
    mixed = stream3 + (kept_two[4] + wide32(core_swap(kept_two[5])))
    mixed_parts = deal_rows(place, mixed.reshape(tokens.shape))

    def ff_back(g, x, kept, w_in, w_out, far):
        far_in, far_out = far[:features], far[features:]
        far_grad = low16(nt(g, far_out) * wide32(kept[3]))
        own_grad = low16(nt(g, w_out) * wide32(kept[2]))
        sums = closing([(far_grad, far_in, over_nt), (own_grad, w_in, over_nt)])
        far_unit = (low16(tn(kept[1], g)), low16(tn(x, far_grad)))
        own_unit = (low16(tn(kept[0], g)), low16(tn(x, own_grad)))
        return sums, own_unit, far_unit

    g_two = with_other(back_low)
    sums, two_own, two_far = ff_back(g_two, x_two, kept_two, ff_in2, ff_out2, far_two)
    back, back_low = norm_back(wide32(back_low), *sums, stream3, gains[3], *two_far)
    two_recv = [half_swap(part) for part in two_far]

    g_att = with_other(back_low)
    dqkv_att = att_backward_call(taps, seg, qkv_att, low16(nt(g_att, att_o)), total, att_marks, mixed_parts[0])
    att_unit, att_far_unit = far_grads(0, x_att, dqkv_att, g_att, [out_att])
    att_recv = half_swap(att_far_unit)
    sums = closing([(dqkv_att, att_w, over_nn)])
    back, back_low = norm_back(back, *sums, stream2, gains[2], att_far_unit, two_recv[0])

    g_one = with_other(back_low)
    sums, one_own, one_far = ff_back(g_one, x_one, kept_one, ff_in1, ff_out1, far_one)
    two = ff_fold(place, two_own, two_recv, one_far[0])
    back, back_low = norm_back(back, *sums, stream1, gains[1], *one_far, two[1])
    one_recv = [half_swap(part) for part in one_far]

    g_mix = with_other(back_low)
    grad_mixed = low16(nt(g_mix, mix_o) * (1.0 / math.sqrt(HEAD_DIM)))
    att = fold(place, att_unit, att_recv, grad_mixed)
    att_got = exchanged(att[1], SEQ, 1)
    two_parts = deal(place, two[0], exchanged(two[1], SEQ, 1), count, grad_mixed)
    two_recv = [exchanged(part, DP, by) for by, part in enumerate(two_parts) if by]

    def small_rows(kernel_grad, log_grad):
        small = jnp.concatenate([kernel_grad, log_grad * (-1.0 / length)], axis=0)
        return jnp.pad(low16(small), ((0, -small.shape[0] % 512), (0, 0))).reshape(-1, features)

    h3_back = lambda i, *after: h3_backward_call(
        i, qkv_mix[i], kept_mix[i][1], grad_mixed, kept_mix[i][2], **h3[i], after=after
    )
    late = touched(h3_back(1, att[1], two_parts[1], *one_own), att_got, *two_recv, *one_recv)
    skip = quarter - LANES
    small = small_rows(late[1][:, skip:], late[2][:, skip:])
    att_parts = deal(place, att[0], att_got, count, late[0])
    att_recv = [exchanged(part, DP, by) for by, part in enumerate(att_parts) if by]
    two_final = add_all([two_parts[0], *two_recv], late[0])
    one = ff_fold(place, one_own, one_recv, late[0])
    one_got = exchanged(one[1], SEQ, 1)
    rest, mix_far_unit = far_grads(1, x_mix, late[0], g_mix, out_mix, small, after=(att_parts[1], one[1], two_final))
    mix_recv = half_swap(mix_far_unit)
    early = touched(h3_back(0, mix_far_unit), *att_recv, one_got, mix_recv)
    small = small_rows(
        jnp.concatenate([early[1], late[1][:, :skip]], axis=1), jnp.concatenate([early[2], late[2][:, :skip]], axis=1)
    )
    def dp_swapped(parts):
        return [exchanged(part, DP, by) for by, part in enumerate(parts) if by]

    one_parts = deal(place, one[0], one_got, count, early[0])
    one_recv = dp_swapped(one_parts)
    mix_unit = own_grads(x_mix, early[0], rest, small, one_parts[1])
    mix = fold(place, mix_unit, mix_recv)
    mix_got = exchanged(mix[1], SEQ, 1)
    att_final = add_all([att_parts[0], *att_recv], mix[1])
    att_recv = dp_swapped([att_final] * count)
    last = touched(early[:1], att_final)[0]
    sums = closing([(last, mix_w[0], over_nn), (late[0], mix_w[1], over_nn)])
    back, _ = norm_back(back, *sums, stream0, gains[0])
    tokens_parts = deal_rows(place, back.reshape(tokens.shape), att_final)
    mixed_parts = touched(mixed_parts, tokens_parts[0])
    tokens_parts, mixed_parts = swapped_rows(tokens_parts), swapped_rows(mixed_parts)
    mix_parts = deal(place, mix[0], mix_got, count, tokens_parts[0])
    mix_recv = dp_swapped(mix_parts)
    one_final = add_all([one_parts[0], *one_recv], mix_parts[1])
    one = lax.all_gather(one_final, (SEQ, DP), axis=0, tiled=True)
    att = gather_parts(place, [att_final, *att_recv], one_final)
    att_back = exchanged(att, SEQ, 1)
    two = lax.all_gather(two_final, (SEQ, DP), axis=0, tiled=True)
    in_two, out_two, two_gain = ff_finish(two, ff_in2, gains[3], att)
    mix_final = add_all([mix_parts[0], *mix_recv], two_gain)
    mix_recv = dp_swapped([mix_final] * count)
    tokens_grad = collect_rows(place, tokens_parts, jnp.float32, mix_final)
    mixed_out = collect_rows(place, mixed_parts, jnp.float32, tokens_grad)
    mix = gather_parts(place, [mix_final, *mix_recv], mixed_out)
    mix_back = exchanged(mix, SEQ, 1)
    q_att, k_att, v_att, o_att, att_gain = mixer_finish(place, att, att_back, att_own, gains[2], mix)
    in_one, out_one, one_gain = ff_finish(one, ff_in1, gains[1], att_gain)
    q_mix, k_mix, v_mix, o_mix, small, mix_gain = mixer_finish(place, mix, mix_back, mix_own, gains[0], one_gain)
    gain_grads = jnp.concatenate([part[:1] for part in (mix_gain, one_gain, att_gain, two_gain)])
    gain_grads = gain_grads + half_swap(gain_grads)
    gain_grads = gain_grads + core_swap(gain_grads)
    small = small.reshape(-1, quarter)
    return (
        mixed_out,
        tokens_grad,
        gain_grads[0],
        q_mix.T,
        k_mix.T,
        v_mix.T,
        o_mix,
        small[:taps],
        gain_grads[1],
        in_one,
        out_one,
        gain_grads[2],
        q_att.T,
        k_att.T,
        v_att.T,
        o_att,
        gain_grads[3],
        in_two,
        out_two,
        small[taps].reshape(decay_rate.shape),
    )


def row_plan_fits(sizes):
    return sizes[SEQ] == 2 and sizes[TENSOR] == 4


def solution(mesh):
    plan = row_shards if row_plan_fits(dict(mesh.shape)) else shards
    return jax.shard_map(
        plan,
        mesh=mesh,
        in_specs=(
            P(DP, (SEQ, TENSOR), None),
            P(DP, (SEQ, TENSOR), None),
            P(DP, None),
            P(),
            P(None, TENSOR),
            P(None, TENSOR),
            P(None, TENSOR),
            P(TENSOR, None),
            P(None, TENSOR),
            P(TENSOR, None),
            P(),
            P(None, TENSOR),
            P(TENSOR, None),
            P(),
            P(None, TENSOR),
            P(None, TENSOR),
            P(None, TENSOR),
            P(TENSOR, None),
            P(),
            P(None, TENSOR),
            P(TENSOR, None),
        ),
        out_specs=(
            P(DP, (SEQ, TENSOR), None),
            P(DP, (SEQ, TENSOR), None),
            P(),
            P(None, TENSOR),
            P(None, TENSOR),
            P(None, TENSOR),
            P(TENSOR, None),
            P(None, TENSOR),
            P(),
            P(None, TENSOR),
            P(TENSOR, None),
            P(),
            P(None, TENSOR),
            P(None, TENSOR),
            P(None, TENSOR),
            P(TENSOR, None),
            P(),
            P(None, TENSOR),
            P(TENSOR, None),
            P(TENSOR, None),
        ),
        check_vma=False,
    )
```

```python
import functools
import math

import jax
import jax.numpy as jnp
from jax import lax
from jax.experimental import pallas as pl
from jax.experimental.pallas import tpu as pltpu
from jax.sharding import PartitionSpec as P

HEAD_DIM = 64
DP, SEQ, TENSOR = "dp", "seq", "tensor"


highest = lax.Precision.HIGHEST
norm_eps = 1e-05
masked_score = -1e30


def passed_along(array, axis, by):
    devices = lax.axis_size(axis)
    pairs = [(i, i + by) for i in range(devices) if 0 <= i + by < devices]
    return lax.ppermute(array, axis, pairs)


def prefix(array, axis, combine, identity):
    devices, here = (lax.axis_size(axis), lax.axis_index(axis))
    everything = jax.tree.map(lambda part: lax.all_gather(part, axis), array)
    start = jax.tree.map(
        lambda part, zero: jnp.broadcast_to(jnp.asarray(zero, part.dtype), part.shape),
        array,
        identity,
    )

    def step(k, before):
        reached = k < here
        new = combine(before, jax.tree.map(lambda part: part[k], everything))
        return jax.tree.map(lambda a, b: jnp.where(reached, a, b), new, before)

    return lax.fori_loop(0, devices, step, start)


def prefix_2(array, axis, join, neutral):
    count = lax.axis_size(axis)
    place = lax.axis_index(axis)
    ahead = count - 1 - place
    gathered = jax.tree.map(
        lambda a, kind: lax.all_gather(a.astype(kind), axis), array, (jnp.bfloat16, jnp.bfloat16)
    )
    state = jax.tree.map(lambda a, e: jnp.zeros_like(a) + jnp.asarray(e, a.dtype), array, neutral)

    def one(step, state):
        source = count - 1 - step
        return join(
            state,
            jax.tree.map(
                lambda a, own: lax.dynamic_index_in_dim(a, source, 0, False).astype(own.dtype),
                gathered,
                array,
            ),
        )

    return lax.fori_loop(0, ahead, one, state)


def lower_triangle(value):
    return value.astype(jnp.bfloat16)


def bmul(form, left, right):
    return jnp.einsum(form, left, right, preferred_element_type=jnp.float32)


def fmul(form, left, right):
    return jnp.einsum(form, left, right, precision=highest, preferred_element_type=jnp.float32)


def layer_norm_forward(residual_stream, norm_gain_weight):
    feature_mean = jnp.mean(residual_stream, axis=-1, keepdims=True)
    mean_centered = residual_stream - feature_mean
    scale_factor = lax.rsqrt(
        jnp.mean(mean_centered * mean_centered, axis=-1, keepdims=True) + norm_eps
    )
    standardized_input = mean_centered * scale_factor
    return (lower_triangle(standardized_input * norm_gain_weight), standardized_input, scale_factor)


def layer_norm_backward(normalized_gradient, standardized_input, scale_factor, norm_gain_weight):
    gain_gradient = jnp.sum(normalized_gradient * standardized_input, axis=(0, 1))
    rescaled_input = normalized_gradient * norm_gain_weight
    mean_centered = rescaled_input - jnp.mean(rescaled_input, axis=-1, keepdims=True)
    return (
        scale_factor
        * (
            mean_centered
            - standardized_input
            * jnp.mean(rescaled_input * standardized_input, axis=-1, keepdims=True)
        ),
        gain_gradient,
    )


def widen(normalized_input):
    return lax.all_gather(normalized_input, TENSOR, axis=1, tiled=True)


def narrow(partial_value):
    return lax.psum_scatter(partial_value, TENSOR, scatter_dimension=1, tiled=True)


def widen_grad(grad_stream):
    return lax.all_gather(lower_triangle(grad_stream), TENSOR, axis=1, tiled=True)


def narrow_grad(partial_value):
    return lax.psum_scatter(partial_value, TENSOR, scatter_dimension=1, tiled=True)


def combine_states(earlier, later):
    return (earlier[0] * later[0], later[1] + later[0][..., None] * earlier[1])


def feed_forward(residual_stream, norm_gain_weight, w_in, w_out):
    normalized_input, standardized_input, scale_factor = layer_norm_forward(
        residual_stream, norm_gain_weight
    )
    widened_hidden = widen(normalized_input)
    hidden_preactivation = bmul("rtd,df->rtf", widened_hidden, w_in)
    hidden_units = lower_triangle(jax.nn.gelu(hidden_preactivation, approximate=False))
    final_result = residual_stream + narrow(bmul("rtf,fd->rtd", hidden_units, w_out))
    return (
        final_result,
        (widened_hidden, standardized_input, scale_factor, hidden_preactivation, hidden_units),
    )


def feed_backward(grad_stream, saved_residuals, norm_gain_weight, w_in, w_out):
    widened_hidden, standardized_input, scale_factor, hidden_preactivation, hidden_units = (
        saved_residuals
    )
    grad_wide = widen_grad(grad_stream)
    grad_out_w = bmul("rtf,rtd->fd", hidden_units, grad_wide)
    grad_hidden = bmul("rtd,fd->rtf", grad_wide, w_out)
    _, gelu_pull = jax.vjp(
        lambda value: jax.nn.gelu(value, approximate=False), hidden_preactivation
    )
    grad_before = lower_triangle(gelu_pull(grad_hidden)[0])
    grad_in_w = bmul("rtd,rtf->df", widened_hidden, grad_before)
    normalized_gradient = narrow_grad(bmul("rtf,df->rtd", grad_before, w_in))
    norm_input_gradient, gain_gradient = layer_norm_backward(
        normalized_gradient, standardized_input, scale_factor, norm_gain_weight
    )
    return (grad_stream + norm_input_gradient, gain_gradient, grad_in_w, grad_out_w)


def mixer_forward(residual_stream, seg_rows, norm_gain_weight, w_q, w_k, w_v, w_o, kernel, rate):
    normalized_input, standardized_input, scale_factor = layer_norm_forward(
        residual_stream, norm_gain_weight
    )
    widened_hidden = widen(normalized_input)
    rows, group_len = (widened_hidden.shape[0], widened_hidden.shape[1])
    heads, width = rate.shape
    query_matrix = lower_triangle(bmul("rtd,de->rte", widened_hidden, w_q))
    key_matrix = lower_triangle(bmul("rtd,de->rte", widened_hidden, w_k))
    value_matrix = lower_triangle(bmul("rtd,de->rte", widened_hidden, w_v))
    taps = kernel.shape[0]
    start = lax.axis_index(SEQ) * group_len
    length = group_len * lax.axis_size(SEQ)
    padded = jnp.concatenate([jnp.full((rows, taps), -1, jnp.int32), seg_rows], axis=1)
    seg_ext = lax.dynamic_slice_in_dim(padded, start + 1, group_len + taps - 1, 1)
    owning_segment = seg_ext[:, taps - 1 :]
    rim = passed_along(key_matrix[:, group_len - taps + 1 :, :], SEQ, 1)
    extended = jnp.concatenate([rim, key_matrix], axis=1).astype(jnp.float32)
    shifted = jnp.zeros(key_matrix.shape, jnp.float32)
    match_list = []
    for tap in range(taps):
        first = taps - 1 - tap
        match = (seg_ext[:, first : first + group_len] == owning_segment).astype(jnp.float32)[
            :, :, None
        ]
        match_list.append(match)
        shifted = shifted + kernel[tap] * extended[:, first : first + group_len] * match
    matches = jnp.stack(match_list)
    logdec = -rate / length
    steps = jnp.arange(group_len, dtype=jnp.float32)[:, None, None]
    rising = jnp.exp(steps * logdec)
    falling = jnp.exp(-steps * logdec)
    leading = jnp.exp((steps + 1.0) * logdec)
    trailing = jnp.exp((group_len - 1.0 - steps) * logdec)
    before = seg_ext[:, taps - 2]
    final = owning_segment[:, -1]
    order = jnp.arange(group_len)
    same = (
        (owning_segment[:, :, None] == owning_segment[:, None, :])
        & (order[:, None] >= order[None, :])
    ).astype(jnp.float32)
    gate = (owning_segment == before[:, None]).astype(jnp.float32)[:, :, None, None]
    ends = (owning_segment == final[:, None]).astype(jnp.float32)[:, :, None, None]
    carry_on = (final == before).astype(jnp.float32)[:, None, None]
    query_f = query_matrix.astype(jnp.float32).reshape(rows, group_len, heads, width)
    shift_f = shifted.reshape(rows, group_len, heads, width)
    value_f = value_matrix.astype(jnp.float32).reshape(rows, group_len, heads, width)
    query_up = query_f * rising
    key_down = shift_f * falling
    query_lead = query_f * leading * gate
    key_tail = shift_f * trailing * ends
    mixing = fmul("rthi,rshi->rhts", query_up, key_down) * same[:, None]
    decay = jnp.exp(group_len * logdec)[None] * carry_on
    end_state = fmul("rshi,rshj->rhij", key_tail, value_f)
    identity = (jnp.ones(decay.shape, jnp.float32), jnp.zeros(end_state.shape, jnp.float32))
    entering = prefix((decay, end_state), SEQ, combine_states, identity)[1]
    mixed = fmul("rhts,rshj->rthj", mixing, value_f) + fmul("rthi,rhij->rthj", query_lead, entering)
    out_mix = lower_triangle(
        mixed.reshape(rows, group_len, heads * width) * (1.0 / math.sqrt(width))
    )
    final_result = residual_stream + narrow(bmul("rte,ed->rtd", out_mix, w_o))
    saved_residuals = (
        widened_hidden,
        standardized_input,
        scale_factor,
        extended,
        matches,
        value_f,
        rising,
        falling,
        leading,
        trailing,
        gate,
        ends,
        same,
        query_up,
        key_down,
        query_lead,
        key_tail,
        mixing,
        decay,
        entering,
        identity,
        out_mix,
    )
    return (final_result, saved_residuals)


def mixer_backward(
    grad_stream, saved_residuals, norm_gain_weight, w_q, w_k, w_v, w_o, kernel, rate
):
    (
        widened_hidden,
        standardized_input,
        scale_factor,
        extended,
        matches,
        value_f,
        rising,
        falling,
        leading,
        trailing,
        gate,
        ends,
        same,
        query_up,
        key_down,
        query_lead,
        key_tail,
        mixing,
        decay,
        entering,
        identity,
        out_mix,
    ) = saved_residuals
    rows, group_len = (widened_hidden.shape[0], widened_hidden.shape[1])
    heads, width = rate.shape
    taps = kernel.shape[0]
    length = group_len * lax.axis_size(SEQ)
    grad_wide = widen_grad(grad_stream)
    grad_o = bmul("rte,rtd->ed", out_mix, grad_wide)
    grad_mixed = bmul("rtd,ed->rte", grad_wide, w_o).reshape(rows, group_len, heads, width) * (
        1.0 / math.sqrt(width)
    )
    grad_mixing = fmul("rthj,rshj->rhts", grad_mixed, value_f) * same[:, None]
    grad_qup = fmul("rhts,rshi->rthi", grad_mixing, key_down)
    grad_kdown = fmul("rhts,rthi->rshi", grad_mixing, query_up)
    reach = fmul("rthj,rhij->rthi", grad_mixed, entering)
    local_back = fmul("rthi,rthj->rhij", query_lead, grad_mixed)
    leaving = prefix_2((decay, local_back), SEQ, combine_states, identity)[1]
    spread = fmul("rshj,rhij->rshi", value_f, leaving)
    grad_value = fmul("rhts,rthj->rshj", mixing, grad_mixed) + fmul(
        "rshi,rhij->rshj", key_tail, leaving
    )
    grad_query = grad_qup * rising + reach * leading * gate
    grad_shift = grad_kdown * falling + spread * trailing * ends
    steps = jnp.arange(group_len, dtype=jnp.float32)[:, None, None]
    local_terms = steps * (query_up * grad_qup - key_down * grad_kdown)
    local_terms = (
        local_terms
        + (steps + 1.0) * query_lead * reach
        + (group_len - 1.0 - steps) * key_tail * spread
    )
    grad_log = jnp.sum(local_terms, axis=(0, 1))
    grad_log = grad_log + group_len * jnp.sum(jnp.sum(leaving * entering, axis=3) * decay, axis=0)
    grad_rate = -grad_log / length
    grad_shift = grad_shift.reshape(rows, group_len, heads * width)
    grad_ext = jnp.zeros(extended.shape, jnp.float32)
    kernel_rows = []
    for tap in range(taps):
        first = taps - 1 - tap
        masked = grad_shift * matches[tap]
        kernel_rows.append(jnp.sum(masked * extended[:, first : first + group_len], axis=(0, 1)))
        grad_ext = grad_ext + jnp.pad(
            kernel[tap] * masked, ((0, 0), (first, taps - 1 - first), (0, 0))
        )
    grad_kernel = jnp.stack(kernel_rows)
    returned = passed_along(grad_ext[:, : taps - 1].astype(jnp.bfloat16), SEQ, -1).astype(
        jnp.float32
    )
    grad_keys = grad_ext[:, taps - 1 :] + jnp.pad(
        returned, ((0, 0), (group_len - taps + 1, 0), (0, 0))
    )
    query_low = lower_triangle(grad_query.reshape(rows, group_len, heads * width))
    keys_low = lower_triangle(grad_keys)
    value_low = lower_triangle(grad_value.reshape(rows, group_len, heads * width))
    grad_qw = bmul("rtd,rte->de", widened_hidden, query_low)
    grad_kw = bmul("rtd,rte->de", widened_hidden, keys_low)
    grad_vw = bmul("rtd,rte->de", widened_hidden, value_low)
    partial_value = bmul("rte,de->rtd", query_low, w_q) + bmul("rte,de->rtd", keys_low, w_k)
    partial_value = partial_value + bmul("rte,de->rtd", value_low, w_v)
    normalized_gradient = narrow_grad(partial_value)
    norm_input_gradient, gain_gradient = layer_norm_backward(
        normalized_gradient, standardized_input, scale_factor, norm_gain_weight
    )
    return (
        grad_stream + norm_input_gradient,
        gain_gradient,
        grad_qw,
        grad_kw,
        grad_vw,
        grad_o,
        grad_kernel,
        grad_rate,
    )


def split_heads(value):
    return value.reshape(value.shape[0], value.shape[1] // HEAD_DIM, HEAD_DIM)


def scores_of(query_rows, key_rows, query_places, key_places, query_seg, key_seg):
    raw = bmul("thd,shd->hts", split_heads(query_rows), split_heads(key_rows)) * (
        1.0 / math.sqrt(HEAD_DIM)
    )
    allowed = (query_places[:, None] >= key_places[None, :]) & (
        query_seg[:, None] == key_seg[None, :]
    )
    return jnp.where(allowed[None], raw, masked_score)


def attend_forward(residual_stream, seg_rows, norm_gain_weight, w_q, w_k, w_v, w_o):
    normalized_input, standardized_input, scale_factor = layer_norm_forward(
        residual_stream, norm_gain_weight
    )
    widened_hidden = widen(normalized_input)
    rows, group_len = (widened_hidden.shape[0], widened_hidden.shape[1])
    query_matrix = lower_triangle(bmul("rtd,de->rte", widened_hidden, w_q))
    key_matrix = lower_triangle(bmul("rtd,de->rte", widened_hidden, w_k))
    value_matrix = lower_triangle(bmul("rtd,de->rte", widened_hidden, w_v))
    gathered_key_rows, gathered_value_rows = (
        lax.all_gather(key_matrix, SEQ, axis=1, tiled=True),
        lax.all_gather(value_matrix, SEQ, axis=1, tiled=True),
    )
    length = gathered_key_rows.shape[1]
    start = lax.axis_index(SEQ) * group_len
    owning_segment = lax.dynamic_slice_in_dim(seg_rows, start, group_len, 1)
    query_places = start + jnp.arange(group_len)
    key_places = jnp.arange(length)

    def forward_row(pieces):
        query_row, key_row, value_row, seg_own, seg_all = pieces
        scores = scores_of(query_row, key_row, query_places, key_places, seg_own, seg_all)
        top = jnp.max(scores, axis=-1, keepdims=True)
        expd = jnp.exp(scores - top)
        total = jnp.sum(expd, axis=-1, keepdims=True)
        softened = lower_triangle(expd / total)
        attended = bmul("hts,shd->thd", softened, split_heads(value_row))
        return (
            lower_triangle(attended.reshape(group_len, attended.shape[1] * HEAD_DIM)),
            (top + jnp.log(total))[..., 0],
        )

    attention_output, log_normalizer = lax.map(
        forward_row,
        (query_matrix, gathered_key_rows, gathered_value_rows, owning_segment, seg_rows),
    )
    final_result = residual_stream + narrow(bmul("rte,ed->rtd", attention_output, w_o))
    saved_residuals = (
        widened_hidden,
        standardized_input,
        scale_factor,
        query_matrix,
        key_matrix,
        value_matrix,
        gathered_key_rows,
        gathered_value_rows,
        owning_segment,
        log_normalizer,
        attention_output,
    )
    return (final_result, saved_residuals)


def attend_backward(grad_stream, saved_residuals, seg_rows, norm_gain_weight, w_q, w_k, w_v, w_o):
    (
        widened_hidden,
        standardized_input,
        scale_factor,
        query_matrix,
        key_matrix,
        value_matrix,
        gathered_key_rows,
        gathered_value_rows,
        owning_segment,
        log_normalizer,
        attention_output,
    ) = saved_residuals
    rows, group_len = (widened_hidden.shape[0], widened_hidden.shape[1])
    length = gathered_key_rows.shape[1]
    start = lax.axis_index(SEQ) * group_len
    query_places = start + jnp.arange(group_len)
    key_places = jnp.arange(length)
    scale = 1.0 / math.sqrt(HEAD_DIM)
    grad_wide = widen_grad(grad_stream)
    grad_o = bmul("rte,rtd->ed", attention_output, grad_wide)
    grad_out = lower_triangle(bmul("rtd,ed->rte", grad_wide, w_o))

    def query_common(pieces):
        query_row, key_row, value_row, seg_own, seg_all, total_row, grad_row = pieces
        scores = scores_of(query_row, key_row, query_places, key_places, seg_own, seg_all)
        softened = jnp.exp(scores - total_row[:, :, None])
        grad_soft = bmul("thd,shd->hts", split_heads(grad_row), split_heads(value_row))
        inner = jnp.sum(softened * grad_soft, axis=-1)
        grad_score = lower_triangle(softened * (grad_soft - inner[:, :, None]))
        grad_q = bmul("hts,shd->thd", grad_score, split_heads(key_row)) * scale
        return (softened, grad_score, grad_q.reshape(group_len, -1), inner)

    pieces = (
        query_matrix,
        gathered_key_rows,
        gathered_value_rows,
        owning_segment,
        seg_rows,
        log_normalizer,
        grad_out,
    )

    def query_only(row_pieces):
        _, _, grad_q, inner = query_common(row_pieces)
        return (grad_q, inner)

    grad_query, inner = lax.map(query_only, pieces)
    all_query, all_grad = (
        lax.all_gather(query_matrix, SEQ, axis=1, tiled=True),
        lax.all_gather(grad_out, SEQ, axis=1, tiled=True),
    )
    all_total, all_inner = (
        lax.all_gather(log_normalizer, SEQ, axis=2, tiled=True),
        lax.all_gather(inner, SEQ, axis=2, tiled=True),
    )

    def key_row_fn(row_pieces):
        query_row, key_row, value_row, seg_all, seg_own, total_row, inner_row, grad_row = row_pieces
        scores = scores_of(query_row, key_row, key_places, query_places, seg_all, seg_own)
        softened = jnp.exp(scores - total_row[:, :, None])
        grad_soft = bmul("thd,shd->hts", split_heads(grad_row), split_heads(value_row))
        grad_score = lower_triangle(softened * (grad_soft - inner_row[:, :, None]))
        grad_k = bmul("hts,thd->shd", grad_score, split_heads(query_row)) * scale
        grad_v = bmul("hts,thd->shd", lower_triangle(softened), split_heads(grad_row))
        return (grad_k.reshape(group_len, -1), grad_v.reshape(group_len, -1))

    grad_keys, grad_values = lax.map(
        key_row_fn,
        (
            all_query,
            key_matrix,
            value_matrix,
            seg_rows,
            owning_segment,
            all_total,
            all_inner,
            all_grad,
        ),
    )
    query_low = lower_triangle(grad_query)
    keys_low = lower_triangle(grad_keys)
    value_low = lower_triangle(grad_values)
    grad_qw = bmul("rtd,rte->de", widened_hidden, query_low)
    grad_kw = bmul("rtd,rte->de", widened_hidden, keys_low)
    grad_vw = bmul("rtd,rte->de", widened_hidden, value_low)
    partial_value = bmul("rte,de->rtd", query_low, w_q) + bmul("rte,de->rtd", keys_low, w_k)
    partial_value = partial_value + bmul("rte,de->rtd", value_low, w_v)
    normalized_gradient = narrow_grad(partial_value)
    norm_input_gradient, gain_gradient = layer_norm_backward(
        normalized_gradient, standardized_input, scale_factor, norm_gain_weight
    )
    return (grad_stream + norm_input_gradient, gain_gradient, grad_qw, grad_kw, grad_vw, grad_o)


def shards(
    tokens,
    out_grad,
    segments,
    gain_mix,
    query_mix,
    key_mix,
    value_mix,
    output_mix,
    shift_kernel,
    decay_rate,
    gain_ff1,
    ff_in1,
    ff_out1,
    gain_att,
    query_att,
    key_att,
    value_att,
    output_att,
    gain_ff2,
    ff_in2,
    ff_out2,
):
    stream_one, kept_mix = mixer_forward(
        tokens,
        segments,
        gain_mix,
        query_mix,
        key_mix,
        value_mix,
        output_mix,
        shift_kernel,
        decay_rate,
    )
    stream_two, kept_first = feed_forward(stream_one, gain_ff1, ff_in1, ff_out1)
    stream_three, kept_att = attend_forward(
        stream_two, segments, gain_att, query_att, key_att, value_att, output_att
    )
    stream_four, kept_second = feed_forward(stream_three, gain_ff2, ff_in2, ff_out2)
    back_three, gain_two_grad, in_two_grad, out_two_grad = feed_backward(
        out_grad, kept_second, gain_ff2, ff_in2, ff_out2
    )
    back_two, att_gain_grad, att_q_grad, att_k_grad, att_v_grad, att_o_grad = attend_backward(
        back_three, kept_att, segments, gain_att, query_att, key_att, value_att, output_att
    )
    back_one, gain_one_grad, in_one_grad, out_one_grad = feed_backward(
        back_two, kept_first, gain_ff1, ff_in1, ff_out1
    )
    (
        back_zero,
        mix_gain_grad,
        mix_q_grad,
        mix_k_grad,
        mix_v_grad,
        mix_o_grad,
        kernel_grad,
        rate_grad,
    ) = mixer_backward(
        back_one,
        kept_mix,
        gain_mix,
        query_mix,
        key_mix,
        value_mix,
        output_mix,
        shift_kernel,
        decay_rate,
    )
    summed = lax.psum(
        (
            mix_q_grad,
            mix_k_grad,
            mix_v_grad,
            mix_o_grad,
            kernel_grad,
            in_one_grad,
            out_one_grad,
            att_q_grad,
            att_k_grad,
            att_v_grad,
            att_o_grad,
            in_two_grad,
            out_two_grad,
            rate_grad,
        ),
        (DP, SEQ),
    )
    gains = lax.psum(
        (mix_gain_grad, gain_one_grad, att_gain_grad, gain_two_grad), (DP, SEQ, TENSOR)
    )
    return (
        stream_four,
        back_zero,
        gains[0],
        summed[0],
        summed[1],
        summed[2],
        summed[3],
        summed[4],
        gains[1],
        summed[5],
        summed[6],
        gains[2],
        summed[7],
        summed[8],
        summed[9],
        summed[10],
        gains[3],
        summed[11],
        summed[12],
        summed[13],
    )


CHUNK = 128
LANES = 128
BLOCK = 2 * CHUNK
FF_COLUMNS = 768
MIB = 1024 * 1024


def dot(left, right, over):
    return lax.dot_general(left, right, (over, ((), ())), preferred_element_type=jnp.float32)


over_nn, over_nt = ((1,), (0,)), ((1,), (1,))


def dot_nn(left, right):
    return dot(left, right, over_nn)


def dot_nt(left, right):
    return dot(left, right, over_nt)


def dot_tn(left, right):
    return dot(left, right, ((0,), (0,)))


def low16(value):
    return value.astype(jnp.bfloat16)


def wide32(value):
    return value.astype(jnp.float32)


def made(shape, kind=jnp.bfloat16):
    return jax.ShapeDtypeStruct(shape, kind)


def kernel_call(
    body, outs, scratch=(), grid=(), in_specs=None, out_specs=None, scalars=0, name=None, after=(), cost=0
):
    if in_specs is None:
        in_specs, out_specs = pl.BlockSpec(memory_space=pltpu.VMEM), [pl.BlockSpec(memory_space=pltpu.VMEM)] * len(outs)
    params = pltpu.CompilerParams(vmem_limit_bytes=50 * MIB)
    estimate = pl.CostEstimate(flops=cost * 10**9, bytes_accessed=0, transcendentals=0)

    def call(*arrays):
        count = len(arrays)
        ins = [in_specs] * (count - scalars) if isinstance(in_specs, pl.BlockSpec) else list(in_specs)
        spec = pltpu.PrefetchScalarGridSpec(
            num_scalar_prefetch=scalars,
            grid=grid,
            in_specs=ins + [pl.BlockSpec(memory_space=pl.ANY)] * len(after),
            out_specs=out_specs,
            scratch_shapes=scratch,
        )

        def whole_body(*refs):
            body(*refs[:count], *refs[count + len(after) :])

        return pl.pallas_call(
            whole_body, grid_spec=spec, out_shape=outs, compiler_params=params, cost_estimate=estimate, name=name
        )(*arrays, *after)

    return call


def place_of(n, core, half):
    return pl.multiple_of(((n & 1) ^ core) * half + (n >> 1) * CHUNK, CHUNK)


def lane_heads():
    lane = lax.broadcasted_iota(jnp.int32, (CHUNK, LANES), 1)
    return [lane // HEAD_DIM == head for head in range(LANES // HEAD_DIM)]


def head_diagonal():
    row = lax.broadcasted_iota(jnp.int32, (LANES, LANES), 0)
    lane = lax.broadcasted_iota(jnp.int32, (LANES, LANES), 1)
    return row // HEAD_DIM == lane // HEAD_DIM


def causal_same(seg_rows, seg_lanes):
    row = lax.broadcasted_iota(jnp.int32, (CHUNK, CHUNK), 0)
    lane = lax.broadcasted_iota(jnp.int32, (CHUNK, CHUNK), 1)
    return (seg_rows == seg_lanes) & (row >= lane)


def pick_heads(heads, parts):
    result = parts[0]
    for head in range(1, len(parts)):
        result = jnp.where(heads[head], parts[head], result)
    return result


def decays(logdec):
    steps = wide32(lax.broadcasted_iota(jnp.int32, (CHUNK, LANES), 0))
    rising, falling = jnp.exp(steps * logdec), jnp.exp(-steps * logdec)
    return steps, rising, falling, jnp.exp(logdec), jnp.exp((CHUNK - 1.0) * logdec), jnp.exp(CHUNK * logdec)


def documents(seg_s, n):
    at = pl.multiple_of(n * CHUNK, CHUNK)
    before = jnp.where(n == 0, -1, seg_s[jnp.maximum(at - 1, 0)])
    return at, seg_s[at], seg_s[at + CHUNK - 1], before


def split_columns(ref, tile=0):
    first = 3 * LANES * tile
    return [ref.at[:, first + i * LANES : first + (i + 1) * LANES] for i in range(3)]


def tile_of(tile):
    return slice(tile * LANES, (tile + 1) * LANES)


def h3_forward_body(
    first, tiles, taps, seg_s, qkv_ref, w_ref, logdec_ref, segb_ref, segl_ref,
    out_ref, shift_ref, state_ref, key_f, masked, state,
):
    length = qkv_ref.shape[0]
    chunks, half, core = length // CHUNK, length // 2, seg_s[length]
    tables = [decays(logdec_ref[:, tile_of(first + tile)]) for tile in range(tiles)]
    heads, diagonal = lane_heads(), head_diagonal()
    key_f[0:taps, :] = jnp.zeros((taps, tiles * LANES), jnp.float32)
    state[...] = jnp.zeros_like(state)

    def chunk_step(n, _):
        at, low_doc, high_doc, before = documents(seg_s, n)
        here = pl.ds(place_of(n, core, half), CHUNK)
        for tile in range(tiles):
            key_f[pl.ds(at + taps, CHUNK), tile_of(tile)] = wide32(split_columns(qkv_ref, tile)[1][here, :])
        seg_here = segb_ref[pl.ds(at + taps, CHUNK), :]

        def one_doc(doc, totals):
            window = segb_ref[pl.ds(at, CHUNK + taps), :] == doc
            result = []
            for tile in range(tiles):
                lanes = tile_of(tile)
                masked[:, lanes] = jnp.where(window, key_f[pl.ds(at, CHUNK + taps), lanes], 0.0)
                conv = jnp.zeros((CHUNK, LANES), jnp.float32)
                for b in range(8):
                    part = jnp.zeros((CHUNK + 8, LANES), jnp.float32)
                    for a in range(taps // 8):
                        tap = 8 * a + b
                        seen = masked[taps - 8 - 8 * a : taps + CHUNK - 8 * a, lanes]
                        part = part + w_ref[tap : tap + 1, tile_of(first + tile)] * seen
                    if b:
                        part = pltpu.roll(part, b, 0)
                    conv = conv + part[8:, :]
                result.append(totals[tile] + jnp.where(seg_here == doc, conv, 0.0))
            return tuple(result)

        zero = jnp.zeros((CHUNK, LANES), jnp.float32)
        shifts = lax.fori_loop(low_doc, high_doc + 1, one_doc, (zero,) * tiles)
        gate, ends = wide32(seg_here == before), wide32(seg_here == high_doc)
        carry = jnp.where(high_doc == before, 1.0, 0.0)
        same = causal_same(seg_here, segl_ref[pl.ds(n, 1), :])
        work = []
        for tile in range(tiles):
            _, rising, falling, one, last, whole = tables[tile]
            q_ref, _, v_ref = split_columns(qkv_ref, tile)
            shift_ref[pl.ds(at, CHUNK), tile_of(tile)] = shifts[tile]
            q_up = low16(wide32(q_ref[here, :]) * rising)
            k_down = low16(shifts[tile] * falling)
            work.append((q_up, k_down, v_ref[here, :], state[tile], one, last, whole))
        mixings = [
            [dot_nt(jnp.where(head, q_up, jnp.zeros_like(q_up)), k_down) for head in heads]
            for q_up, k_down, *_ in work
        ]
        for tile, (q_up, k_down, value, entering, one, last, whole) in enumerate(work):
            parts = [dot_nn(low16(jnp.where(same, mixing, 0.0)), value) for mixing in mixings[tile]]
            state_ref[tile, n] = entering
            mixed = pick_heads(heads, parts) + gate * dot_nt(q_up, low16(entering * one))
            out_ref[here, tile_of(tile)] = low16(mixed * (1.0 / math.sqrt(HEAD_DIM)))
            tail = dot_tn(low16(wide32(value) * ends), k_down) * last
            state[tile] = entering * (whole * carry) + jnp.where(diagonal, tail, 0.0)
        return 0

    lax.fori_loop(0, chunks, chunk_step, 0)


def h3_specs(length, taps, wide, chunks):
    whole = lambda *shape: pl.BlockSpec(shape, lambda i, s: (0,) * len(shape))
    tables = [whole(taps, wide), whole(1, wide), whole(length + 2 * taps, LANES), whole(chunks, CHUNK)]
    return whole, tables


def h3_forward_call(first, qkv, seg, kernel, logdec, marks, after=()):
    length, tiles, taps = qkv.shape[0], qkv.shape[1] // (3 * LANES), kernel.shape[0]
    chunks, wide = length // CHUNK, tiles * LANES
    whole, tables = h3_specs(length, taps, kernel.shape[1], chunks)
    return kernel_call(
        functools.partial(h3_forward_body, first, tiles, taps),
        [made((length, wide)), made((length, wide), jnp.float32), made((tiles, chunks, LANES, LANES), jnp.float32)],
        [
            pltpu.VMEM((length + taps, wide), jnp.float32),
            pltpu.VMEM((CHUNK + taps, wide), jnp.float32),
            pltpu.VMEM((tiles, LANES, LANES), jnp.float32),
        ],
        (1,),
        [whole(*qkv.shape)] + tables,
        [whole(length, wide), whole(length, wide), whole(tiles, chunks, LANES, LANES)],
        1,
        "h3_forward",
        after,
        10 * tiles,
    )(seg, qkv, kernel, logdec, *marks)


def h3_backward_body(
    first, tiles, taps, seg_s, qkv_ref, shift_ref, grad_ref, w_ref, logdec_ref, segb_ref, segl_ref,
    state_ref, dqkv_ref, dw_ref, dlog_ref, key_f, grad_f, masked, masked_grad, state, tap_sums, log_sum,
):
    length = qkv_ref.shape[0]
    chunks, half, core = length // CHUNK, length // 2, seg_s[length]
    tables = [decays(logdec_ref[:, tile_of(first + tile)]) for tile in range(tiles)]
    heads, diagonal = lane_heads(), head_diagonal()
    key_f[0:taps, :] = jnp.zeros((taps, tiles * LANES), jnp.float32)

    def copy_keys(n, _):
        at = pl.multiple_of(n * CHUNK, CHUNK)
        for tile in range(tiles):
            keys = split_columns(qkv_ref, tile)[1][pl.ds(place_of(n, core, half), CHUNK), :]
            key_f[pl.ds(at + taps, CHUNK), tile_of(tile)] = wide32(keys)
        return 0

    lax.fori_loop(0, chunks, copy_keys, 0)
    grad_f[length:, :] = jnp.zeros((taps, tiles * LANES), jnp.float32)
    state[...] = jnp.zeros_like(state)
    tap_sums[...] = jnp.zeros_like(tap_sums)
    log_sum[...] = jnp.zeros_like(log_sum)
    masked_grad[CHUNK + taps :, :] = jnp.zeros((8, tiles * LANES), jnp.float32)

    def chunk_step(back, _):
        n = chunks - 1 - back
        at, low_doc, high_doc, before = documents(seg_s, n)
        here = pl.ds(place_of(n, core, half), CHUNK)
        seg_here = segb_ref[pl.ds(at + taps, CHUNK), :]
        gate, ends = wide32(seg_here == before), wide32(seg_here == high_doc)
        carry = jnp.where(high_doc == before, 1.0, 0.0)
        same = causal_same(seg_here, segl_ref[pl.ds(n, 1), :])
        work = []
        for tile in range(tiles):
            _, rising, falling, *_ = tables[tile]
            q_ref, _, v_ref = split_columns(qkv_ref, tile)
            q_up = low16(wide32(q_ref[here, :]) * rising)
            k_down = low16(shift_ref[pl.ds(at, CHUNK), tile_of(tile)] * falling)
            work.append((q_up, k_down, v_ref[here, :], grad_ref[here, tile_of(first + tile)]))
        squares = []
        for q_up, k_down, value, grad in work:
            for head in heads:
                mixing = dot_nt(jnp.where(head, q_up, jnp.zeros_like(q_up)), k_down)
                grad_mixing = dot_nt(jnp.where(head, grad, jnp.zeros_like(grad)), value)
                squares.append([low16(jnp.where(same, square, 0.0)) for square in (mixing, grad_mixing)])
        for tile, (q_up, k_down, value, grad) in enumerate(work):
            steps, rising, falling, one, last, whole = tables[tile]
            lanes = tile_of(tile)
            dqkv = split_columns(dqkv_ref, tile)
            mine = squares[tile * len(heads) : (tile + 1) * len(heads)]
            dq_local = pick_heads(heads, [dot_nn(grad_mixing, k_down) for _, grad_mixing in mine])
            dk_local = pick_heads(heads, [dot_tn(grad_mixing, q_up) for _, grad_mixing in mine])
            dv = pick_heads(heads, [dot_tn(mixing, grad) for mixing, _ in mine])
            entering, leaving = state_ref[tile, n], state[tile]
            leaving_low = low16(leaving)
            reach = dot_nn(grad, low16(entering)) * (one * gate)
            spread = dot_nn(value, leaving_low) * (last * ends)
            q_up_f, k_down_f = wide32(q_up), wide32(k_down)
            dqkv[0][here, :] = low16((dq_local + reach) * rising)
            dqkv[2][here, :] = low16(dv + dot_nt(low16(k_down_f * (last * ends)), leaving_low))
            terms = steps * (q_up_f * dq_local - k_down_f * dk_local)
            terms = terms + (steps + 1.0) * q_up_f * reach + (CHUNK - 1.0 - steps) * k_down_f * spread
            log_sum[:, lanes] += terms + (CHUNK * carry) * (leaving * entering * whole)
            lead = dot_tn(low16(wide32(grad) * gate), q_up) * one
            state[tile] = leaving * (whole * carry) + jnp.where(diagonal, lead, 0.0)
            grad_f[pl.ds(at, CHUNK), lanes] = (dk_local + spread) * falling

        def one_doc(doc, totals):
            after = segb_ref[pl.ds(at + taps, CHUNK + taps), :] == doc
            ahead = segb_ref[pl.ds(at, CHUNK + taps), :] == doc
            result = []
            for tile in range(tiles):
                lanes = tile_of(tile)
                ahead_grad = jnp.where(after, grad_f[pl.ds(at, CHUNK + taps), lanes], 0.0)
                masked_grad[0 : CHUNK + taps, lanes] = ahead_grad
                masked[:, lanes] = jnp.where(ahead, key_f[pl.ds(at, CHUNK + taps), lanes], 0.0)
                own = jnp.concatenate([jnp.zeros((8, LANES), jnp.float32), masked_grad[0:CHUNK, lanes]], axis=0)
                conv = jnp.zeros((CHUNK, LANES), jnp.float32)
                for b in range(8):
                    part = jnp.zeros((CHUNK + 8, LANES), jnp.float32)
                    moved = pltpu.roll(own, CHUNK + 8 - b, 0) if b else own
                    for a in range(taps // 8):
                        tap = 8 * a + b
                        here_grad = masked_grad[8 * a : 8 * a + CHUNK + 8, lanes]
                        part = part + w_ref[tap : tap + 1, tile_of(first + tile)] * here_grad
                        seen = masked[taps - 8 - 8 * a : taps + CHUNK - 8 * a, lanes]
                        tap_sums[tap, :, lanes] += jnp.sum((moved * seen).reshape(-1, 8, LANES), axis=0)
                    if b:
                        part = pltpu.roll(part, CHUNK + 8 - b, 0)
                    conv = conv + part[:CHUNK, :]
                result.append(totals[tile] + jnp.where(seg_here == doc, conv, 0.0))
            return tuple(result)

        zero = jnp.zeros((CHUNK, LANES), jnp.float32)
        dks = lax.fori_loop(low_doc, high_doc + 1, one_doc, (zero,) * tiles)
        for tile in range(tiles):
            split_columns(dqkv_ref, tile)[1][here, :] = low16(dks[tile])
        return 0

    lax.fori_loop(0, chunks, chunk_step, 0)
    dw_ref[...] = jnp.sum(tap_sums[...], axis=1)
    dlog_ref[...] = jnp.sum(log_sum[...], axis=0, keepdims=True)


def h3_backward_call(first, qkv, shifted, grad, states, seg, kernel, logdec, marks, after=()):
    length, tiles, taps = qkv.shape[0], qkv.shape[1] // (3 * LANES), kernel.shape[0]
    chunks, wide = length // CHUNK, tiles * LANES
    whole, tables = h3_specs(length, taps, kernel.shape[1], chunks)
    tall = [pltpu.VMEM((n, wide), jnp.float32) for n in (length + taps, length + taps, CHUNK + taps, CHUNK + taps + 8)]
    return kernel_call(
        functools.partial(h3_backward_body, first, tiles, taps),
        [made(qkv.shape), made((taps, wide), jnp.float32), made((1, wide), jnp.float32)],
        tall
        + [
            pltpu.VMEM((tiles, LANES, LANES), jnp.float32),
            pltpu.VMEM((taps, 8, wide), jnp.float32),
            pltpu.VMEM((CHUNK, wide), jnp.float32),
        ],
        (1,),
        [whole(*qkv.shape), whole(*shifted.shape), whole(*grad.shape)] + tables + [whole(*states.shape)],
        [whole(*qkv.shape), whole(taps, wide), whole(1, wide)],
        1,
        "h3_backward",
        after,
        16 * tiles,
    )(seg, qkv, shifted, grad, kernel, logdec, *marks, states)


score_unit = 1.0 / math.sqrt(HEAD_DIM)


def row_block(ref, i, core, half):
    parts = [ref[pl.ds(place_of(2 * i + step, core, half), CHUNK), :] for step in range(2)]
    return jnp.concatenate(parts, axis=0)


def put_block(ref, i, core, half, block):
    for step in range(2):
        ref[pl.ds(place_of(2 * i + step, core, half), CHUNK), :] = block[step * CHUNK : (step + 1) * CHUNK, :]


def head_rows(block):
    lane, zero = lax.broadcasted_iota(jnp.int32, block.shape, 1), jnp.zeros_like(block)
    parts = [jnp.where(lane // HEAD_DIM == head, block, zero) for head in range(LANES // HEAD_DIM)]
    return jnp.concatenate(parts, axis=0)


def allowed_tile(first, segb_ref, segl_ref, q_block, k_block):
    seg_keys = segb_ref[first + k_block * BLOCK : first + (k_block + 1) * BLOCK, :]
    seg_keys = jnp.concatenate([seg_keys] * (BLOCK // LANES), axis=1)
    allowed = seg_keys == segl_ref[q_block : q_block + 1, :]
    if q_block == k_block:
        row = lax.broadcasted_iota(jnp.int32, (BLOCK, BLOCK), 0)
        lane = lax.broadcasted_iota(jnp.int32, (BLOCK, BLOCK), 1)
        allowed = allowed & (row <= lane)
    return jnp.concatenate([allowed] * (LANES // HEAD_DIM), axis=1)


def picked_rows(tall):
    parts = []
    for head in range(LANES // HEAD_DIM):
        rows = slice(head * HEAD_DIM, (head + 1) * HEAD_DIM)
        parts.append(tall[rows, head * BLOCK : (head + 1) * BLOCK])
    return jnp.concatenate(parts, axis=0)


def att_forward_body(first, seg_s, qkv_ref, segb_ref, segl_ref, out_ref, total_ref, key, value, score):
    length = qkv_ref.shape[0]
    q_ref, k_ref, v_ref = split_columns(qkv_ref)
    blocks, half, core = length // BLOCK, length // 2, seg_s[length]
    for i in range(blocks):
        key[i * BLOCK : (i + 1) * BLOCK, :] = row_block(k_ref, i, core, half)
        value[i * BLOCK : (i + 1) * BLOCK, :] = row_block(v_ref, i, core, half)
    for i in range(blocks):
        query = head_rows(row_block(q_ref, i, core, half) * jnp.bfloat16(score_unit))
        top = jnp.full((1, 2 * BLOCK), masked_score, jnp.float32)
        for j in range(i + 1):
            keys = slice(j * BLOCK, (j + 1) * BLOCK)
            tile = dot_nt(key[keys, :], query)
            tile = jnp.where(allowed_tile(first, segb_ref, segl_ref, i, j), tile, masked_score)
            score[keys, :] = tile
            top = jnp.maximum(top, jnp.max(tile, axis=0, keepdims=True))
        total = jnp.zeros((1, 2 * BLOCK), jnp.float32)
        tall = jnp.zeros((LANES, 2 * BLOCK), jnp.float32)
        for j in range(i + 1):
            keys = slice(j * BLOCK, (j + 1) * BLOCK)
            expd = jnp.exp(score[keys, :] - top)
            total = total + jnp.sum(expd, axis=0, keepdims=True)
            tall = tall + dot_tn(value[keys, :], low16(expd))
        put_block(out_ref, i, core, half, low16(picked_rows(tall / total).T))
        total_ref[i : i + 1, :] = top + jnp.log(total)


def att_backward_body(
    first, seg_s, qkv_ref, grad_ref, total_ref, segb_ref, segl_ref, dqkv_ref,
    key, value, probs, grad_probs, dk_sum, dv_sum,
):
    length = qkv_ref.shape[0]
    q_ref, k_ref, v_ref = split_columns(qkv_ref)
    dq_ref, dk_ref, dv_ref = split_columns(dqkv_ref)
    blocks, half, core = length // BLOCK, length // 2, seg_s[length]
    for i in range(blocks):
        key[i * BLOCK : (i + 1) * BLOCK, :] = row_block(k_ref, i, core, half)
        value[i * BLOCK : (i + 1) * BLOCK, :] = row_block(v_ref, i, core, half)
    for i in range(blocks):
        query = head_rows(row_block(q_ref, i, core, half) * jnp.bfloat16(score_unit))
        grad = head_rows(row_block(grad_ref, i, core, half))
        inner = jnp.zeros((1, 2 * BLOCK), jnp.float32)
        for j in range(i + 1):
            keys = slice(j * BLOCK, (j + 1) * BLOCK)
            tile = dot_nt(key[keys, :], query) - total_ref[i : i + 1, :]
            tile = jnp.exp(jnp.where(allowed_tile(first, segb_ref, segl_ref, i, j), tile, masked_score))
            grad_tile = dot_nt(value[keys, :], grad)
            probs[keys, :] = tile
            grad_probs[keys, :] = grad_tile
            inner = inner + jnp.sum(tile * grad_tile, axis=0, keepdims=True)
        tall = jnp.zeros((LANES, 2 * BLOCK), jnp.float32)
        for j in range(i + 1):
            keys = slice(j * BLOCK, (j + 1) * BLOCK)
            tile = probs[keys, :]
            grad_score = low16(tile * (grad_probs[keys, :] - inner))
            dk, dv = dot_nn(grad_score, query), dot_nn(low16(tile), grad)
            if i == j:
                dk_sum[keys, :], dv_sum[keys, :] = dk, dv
            else:
                dk_sum[keys, :] += dk
                dv_sum[keys, :] += dv
            tall = tall + dot_tn(key[keys, :], grad_score)
        put_block(dq_ref, i, core, half, low16(picked_rows(tall).T * score_unit))
    for i in range(blocks):
        put_block(dk_ref, i, core, half, low16(dk_sum[i * BLOCK : (i + 1) * BLOCK, :]))
        put_block(dv_ref, i, core, half, low16(dv_sum[i * BLOCK : (i + 1) * BLOCK, :]))


def att_specs(length, wide, marks):
    own = lambda columns: pl.BlockSpec((length, columns), lambda i, s: (0, i))
    whole = [pl.BlockSpec(mark.shape, lambda i, s: (0, 0)) for mark in marks]
    totals = pl.BlockSpec((None, length // BLOCK, 2 * BLOCK), lambda i, s: (i, 0, 0))
    return wide // LANES, own, whole, totals


def att_forward_call(first, seg, qkv, marks, *after):
    length, wide = qkv.shape[0], qkv.shape[1] // 3
    tiles, own, whole, totals = att_specs(length, wide, marks)
    return kernel_call(
        functools.partial(att_forward_body, first),
        [made((length, wide)), made((tiles, length // BLOCK, 2 * BLOCK), jnp.float32)],
        [pltpu.VMEM((length, LANES), jnp.bfloat16)] * 2 + [pltpu.VMEM((length, 2 * BLOCK), jnp.float32)],
        (tiles,),
        [own(3 * LANES)] + whole,
        [own(LANES), totals],
        1,
        "att_forward",
        after,
        11,
    )(seg, qkv, *marks)


def att_backward_call(first, seg, qkv, grad, total, marks, *after):
    length, wide = grad.shape
    tiles, own, whole, totals = att_specs(length, wide, marks)
    return kernel_call(
        functools.partial(att_backward_body, first),
        [made(qkv.shape)],
        [pltpu.VMEM((length, LANES), jnp.bfloat16)] * 2
        + [pltpu.VMEM((length, 2 * BLOCK), jnp.float32)] * 2
        + [pltpu.VMEM((length, LANES), jnp.float32)] * 2,
        (tiles,),
        [own(3 * LANES), own(LANES), totals] + whole,
        [own(3 * LANES)],
        1,
        "att_backward",
        after,
        18,
    )(seg, qkv, grad, total, *marks)[0]


def tile_rows(i, quarter, rest):
    found = []
    for kind in range(3):
        for unit in range(2):
            head = (unit * quarter, LANES, kind * LANES)
            tail = (unit * quarter + LANES, rest, 3 * LANES + kind * rest)
            for first, count, row in (head, tail):
                low, high = max(first, i * LANES), min(first + count, (i + 1) * LANES)
                if low < high:
                    found.append((unit, row + low - first, kind * LANES + low - i * LANES, high - low))
    return found


def join_body(first, own_ref, far_ref, out_ref):
    quarter = own_ref.shape[0] // 3
    for i in range(out_ref.shape[0] // (3 * LANES)):
        for unit, row, at, count in tile_rows(first + i, quarter, quarter - LANES):
            at += i * 3 * LANES
            out_ref[at : at + count, :] = (own_ref, far_ref)[unit][row : row + count, :]


def joined_tiles(first, tiles, own, far, *after):
    shape = (tiles * 3 * LANES, own.shape[1])
    body = functools.partial(join_body, first)
    return kernel_call(body, [made(shape)], name="join", after=after)(own, far)[0]


def copy_body(array_ref, out_ref):
    out_ref[...] = array_ref[...]


def copied(array, *after):
    return kernel_call(copy_body, [made(array.shape, array.dtype)], name="copied", after=after)(array)[0]


def stack_body(one_ref, two_ref, out_ref):
    rows = one_ref.shape[0]
    out_ref[:rows, :] = one_ref[...]
    out_ref[rows:, :] = two_ref[...]


def stacked(one, two, *after):
    shape = (one.shape[0] + two.shape[0], one.shape[1])
    return kernel_call(stack_body, [made(shape)], name="stack", after=after)(one, two)[0]


def pack_body(q_ref, k_ref, v_ref, *refs):
    unit_ref, quarter = refs[-1], q_ref.shape[0]
    rest = quarter - LANES
    for kind, ref in enumerate((q_ref, k_ref, v_ref)):
        unit_ref[kind * LANES : (kind + 1) * LANES, :] = ref[:LANES, :]
        unit_ref[3 * LANES + kind * rest : 3 * LANES + (kind + 1) * rest, :] = ref[LANES:, :]
    for ref in refs[:-1]:
        unit_ref[3 * quarter :, :] = ref[...]


def packed(parts, *after):
    shape = (sum(part.shape[0] for part in parts), parts[0].shape[1])
    return kernel_call(pack_body, [made(shape)], name="pack", after=after)(*parts)[0]


def put_grads(first, x_ref, dqkv_ref, units, quarter):
    for i in range(dqkv_ref.shape[1] // (3 * LANES)):
        total = dot_tn(dqkv_ref[:, i * 3 * LANES : (i + 1) * 3 * LANES], x_ref[...])
        for unit, row, at, count in tile_rows(first + i, quarter, quarter - LANES):
            units[unit][row : row + count, :] = low16(total[at : at + count, :])


def far_grads_body(first, x_ref, dqkv_ref, g_ref, *refs):
    outs, unit_ref, far_ref = refs[:-2], refs[-2], refs[-1]
    quarter = unit_ref.shape[0] // 4
    put_grads(first, x_ref, dqkv_ref, (unit_ref, far_ref), quarter)
    at = 3 * quarter
    total = jnp.concatenate([dot_tn(ref[...], g_ref[...]) for ref in outs[: len(outs) - 1 + (first == 0)]], axis=0)
    unit_ref[at:, :] = low16(total[:quarter, :])
    far_ref[at : at + quarter, :] = low16(total[quarter:, :])
    if first:
        far_ref[at + quarter :, :] = outs[-1][...]


def far_grads(first, x, dqkv, g, outs, *small, after=()):
    quarter, width = sum(out.shape[1] for out in outs) // 2, x.shape[1]
    shapes = [(4 * quarter, width), (4 * quarter + sum(rows.shape[0] for rows in small), width)]
    body = functools.partial(far_grads_body, first)
    return kernel_call(body, [made(shape) for shape in shapes], name="far_grads", after=after)(x, dqkv, g, *outs, *small)


def own_grads_body(x_ref, dqkv_ref, rest_ref, small_ref, unit_ref):
    quarter = rest_ref.shape[0] // 4
    put_grads(0, x_ref, dqkv_ref, (unit_ref, unit_ref), quarter)
    unit_ref[3 * LANES : 4 * quarter, :] = rest_ref[3 * LANES :, :]
    unit_ref[4 * quarter :, :] = small_ref[...]


def own_grads(x, dqkv, rest, small, *after):
    shape = (rest.shape[0] + small.shape[0], x.shape[1])
    return kernel_call(own_grads_body, [made(shape)], name="own_grads", after=after)(x, dqkv, rest, small)[0]


def gelu_and_slope(value):
    bell = jnp.exp(value * value * -0.5)
    below = 0.5 + 0.5 * lax.erf(value * math.sqrt(0.5))
    return value * below, below + value * bell * (1.0 / math.sqrt(2.0 * math.pi))


def ff_forward_body(x_ref, in_own, in_far, out_own, out_far, *refs):
    own_ref, other_ref = refs[-2:]
    total = None
    for i, (w_in, w_out) in enumerate(((in_own, out_own), (in_far, out_far))):
        hidden, slope = gelu_and_slope(dot_nn(x_ref[...], w_in[...]))
        hidden = low16(hidden)
        refs[i][...] = hidden
        refs[2 + i][...] = low16(slope)
        part = dot_nn(hidden, w_out[...])
        total = part if total is None else total + part

    @pl.when(pl.program_id(0) == 0)
    def _():
        other_ref[...] = low16(total)

    @pl.when(pl.program_id(0) == 1)
    def _():
        own_ref[...] = total


def ff_forward_call(x, w_in, w_out, far):
    half, width, units = x.shape[0] // 2, x.shape[1], w_in.shape[1]
    flipped = lambda columns: pl.BlockSpec((half, columns), lambda i: (1 - i, 0))
    rows = pl.BlockSpec((half, width), lambda i: (0, 0))
    weight = lambda at: pl.BlockSpec((width, units), lambda i: (at, 0))
    return kernel_call(
        ff_forward_body,
        [made((2 * half, units))] * 4 + [made((half, width), jnp.float32), made((half, width))],
        grid=(2,),
        in_specs=[flipped(width), weight(0), weight(0), weight(0), weight(1)],
        out_specs=[flipped(units)] * 4 + [rows, rows],
        name="ff_forward",
        cost=12,
    )(x, w_in, far, w_out, far)


def standardized(stream):
    centered = stream - jnp.mean(stream, axis=-1, keepdims=True)
    scale = lax.rsqrt(jnp.mean(centered * centered, axis=-1, keepdims=True) + norm_eps)
    return centered * scale, scale


def deal_rows_body(place, array_ref, *refs):
    for by, ref in enumerate(refs):
        ref[...] = low16(array_ref[place[2] ^ by])


def deal_rows(place, array, *after):
    count, *shape = array.shape
    return kernel_call(
        deal_rows_body,
        [made(tuple(shape))] * count,
        grid=(1,),
        in_specs=[pl.BlockSpec(array.shape, lambda i, s: (0, 0, 0))],
        out_specs=[pl.BlockSpec(tuple(shape), lambda i, s: (0, 0))] * count,
        scalars=1,
        name="deal_rows",
        after=after,
    )(place, array)


def collect_rows_body(place, *refs):
    for by, ref in enumerate(refs[:-1]):
        refs[-1][place[2] ^ by] = ref[...].astype(refs[-1].dtype)


def collect_rows(place, parts, kind, *after):
    shape = (len(parts), *parts[0].shape)
    return kernel_call(
        collect_rows_body,
        [made(shape, kind)],
        grid=(1,),
        in_specs=[pl.BlockSpec(parts[0].shape, lambda i, s: (0, 0))] * len(parts),
        out_specs=[pl.BlockSpec(shape, lambda i, s: (0, 0, 0))],
        scalars=1,
        name="collect_rows",
        after=after,
    )(place, *parts)[0]


def first_norm_body(place, *refs):
    *parts, gain_ref, stream_ref, normed_ref = refs
    rows = parts[0].shape[0]
    for by, ref in enumerate(parts):
        here = pl.ds(pl.multiple_of((place[2] ^ by) * rows, rows), rows)
        stream = wide32(ref[...])
        stream_ref[here, :] = stream
        normed_ref[here, :] = low16(standardized(stream)[0] * gain_ref[...])


def first_norm(place, parts, gain, *after):
    rows, width = parts[0].shape
    shape = (rows * len(parts), width)
    whole = lambda shape: pl.BlockSpec(shape, lambda i, s: (0, 0))
    return kernel_call(
        first_norm_body,
        [made(shape, jnp.float32), made(shape)],
        grid=(1,),
        in_specs=[whole(part.shape) for part in parts] + [whole(gain.shape)],
        out_specs=[whole(shape)] * 2,
        scalars=1,
        name="first_norm",
        after=after,
    )(place, *parts, gain)


def touch_body(*refs):
    pass


def touched(arrays, *after):
    anywhere = pl.BlockSpec(memory_space=pl.ANY)
    return pl.pallas_call(
        touch_body,
        in_specs=[anywhere] * (len(arrays) + len(after)),
        out_specs=[anywhere] * len(arrays),
        out_shape=[made(array.shape, array.dtype) for array in arrays],
        input_output_aliases={i: i for i in range(len(arrays))},
        cost_estimate=pl.CostEstimate(flops=0, bytes_accessed=0, transcendentals=0),
        name="touch",
    )(*arrays, *after)


def add_norm_body(stream_ref, own_ref, recv_ref, gain_ref, sum_ref, normed_ref):
    stream = stream_ref[...] + (own_ref[...] + wide32(recv_ref[...]))
    sum_ref[...] = stream
    normed_ref[...] = low16(standardized(stream)[0] * gain_ref[...])


def add_norm(stream, own, recv, gain, *after):
    outs = [made(stream.shape, jnp.float32), made(stream.shape)]
    return kernel_call(add_norm_body, outs, name="add_norm", after=after)(stream, own, recv, gain)


def norm_back_body(grad_ref, own_ref, recv_ref, stream_ref, gain_ref, sum_ref, low_ref):
    xhat, scale = standardized(stream_ref[...])
    e = (own_ref[...] + wide32(recv_ref[...])) * gain_ref[...]
    inner = jnp.mean(e * xhat, axis=-1, keepdims=True)
    back = scale * (e - jnp.mean(e, axis=-1, keepdims=True) - xhat * inner)
    total = grad_ref[...] + back
    sum_ref[...] = total
    low_ref[...] = low16(total)


def norm_back(grad, own, recv, stream, gain, *after):
    outs = [made(grad.shape, jnp.float32), made(grad.shape)]
    return kernel_call(norm_back_body, outs, name="norm_back", after=after)(grad, own, recv, stream, gain)


def fold_body(place, own_keep, recv_keep, own_send, recv_send, keep_ref, send_ref):
    send_ref[...] = low16(wide32(own_send[...]) + wide32(recv_send[...]))
    keep_ref[...] = low16(wide32(own_keep[...]) + wide32(recv_keep[...]))


def fold(place, own, recv, *after):
    shape = (own.shape[0] // 2, own.shape[1])
    keep = pl.BlockSpec(shape, lambda i, s: (s[0], 0))
    send = pl.BlockSpec(shape, lambda i, s: (1 - s[0], 0))
    same = pl.BlockSpec(shape, lambda i, s: (0, 0))
    return kernel_call(
        fold_body,
        [made(shape)] * 2,
        grid=(1,),
        in_specs=[keep, keep, send, send],
        out_specs=[same] * 2,
        scalars=1,
        name="fold",
        after=after,
    )(place, own, recv, own, recv)


def ff_fold_body(place, own_in, recv_in, own_out, recv_out, keep_ref, send_ref):
    both_in = low16(wide32(own_in[...]) + wide32(recv_in[...]))
    both_out = low16(wide32(own_out[...]) + wide32(recv_out[...]))
    keep_ref[...] = jnp.where(place[0] == 0, both_in, both_out)
    send_ref[...] = jnp.where(place[0] == 0, both_out, both_in)


def ff_fold(place, own, recv, *after):
    shape = own[0].shape
    same = pl.BlockSpec(shape, lambda i, s: (0, 0))
    return kernel_call(
        ff_fold_body,
        [made(shape)] * 2,
        grid=(1,),
        in_specs=[same] * 4,
        out_specs=[same] * 2,
        scalars=1,
        name="ff_fold",
        after=after,
    )(place, own[0], recv[0], own[1], recv[1])


def add_two_body(one_ref, two_ref, out_ref):
    out_ref[...] = low16(wide32(one_ref[...]) + wide32(two_ref[...]))


def add_two(one, two, *after):
    return kernel_call(add_two_body, [made(one.shape)], name="add_two", after=after)(one, two)[0]


def sum_parts_body(parts_ref, out_ref):
    total = wide32(parts_ref[0])
    for i in range(1, parts_ref.shape[0]):
        total = total + wide32(parts_ref[i])
    for i in range(out_ref.shape[0]):
        out_ref[i] = low16(total)


def sum_parts(parts, copies, *after):
    shape = (copies, *parts.shape[1:])
    return kernel_call(sum_parts_body, [made(shape)], name="sum_parts", after=after)(parts)[0]


def ff_finish_body(place, half_ref, recv_ref, w_ref, gain_ref, in_ref, out_ref, gain_grad_ref):
    first = place[0] == 0
    out_ref[...] = wide32(jnp.where(first, half_ref[...], recv_ref[...]))
    grad = wide32(jnp.where(first, recv_ref[...], half_ref[...]))
    in_ref[...] = grad
    sums = jnp.sum(grad * wide32(w_ref[...]), axis=1, keepdims=True)
    gain_grad_ref[...] = jnp.broadcast_to(sums, (w_ref.shape[0], LANES)).T[:8, :] / gain_ref[...]


def ff_finish(place, half, recv, w_in, gain, *after):
    whole = lambda shape: pl.BlockSpec(shape, lambda i, s: (0, 0))
    shapes = [w_in.shape, w_in.shape, (8, w_in.shape[0])]
    return kernel_call(
        ff_finish_body,
        [made(shape, jnp.float32) for shape in shapes],
        grid=(1,),
        in_specs=[whole(array.shape) for array in (half, recv, w_in, gain)],
        out_specs=[whole(shape) for shape in shapes],
        scalars=1,
        name="ff_finish",
        after=after,
    )(place, half, recv, w_in, gain)


def whole_finish_body(all_ref, w_ref, gain_ref, in_ref, out_ref, gain_grad_ref):
    width = w_ref.shape[0]
    out_ref[...] = wide32(all_ref[:width, :])
    grad = wide32(all_ref[width:, :])
    in_ref[...] = grad
    sums = jnp.sum(grad * wide32(w_ref[...]), axis=1, keepdims=True)
    gain_grad_ref[...] = jnp.broadcast_to(sums, (width, LANES)).T[:8, :] / gain_ref[...]


def whole_finish(summed, w_in, gain, *after):
    shapes = [w_in.shape, w_in.shape, (8, w_in.shape[0])]
    return kernel_call(whole_finish_body, [made(shape, jnp.float32) for shape in shapes], name="whole_finish", after=after)(
        summed, w_in, gain
    )


def mixer_finish_body(place, half_ref, recv_ref, w_ref, gain_ref, *refs):
    *outs, gain_grad_ref, unit = refs
    rows, quarter = half_ref.shape[0], outs[0].shape[0]
    rest = quarter - LANES
    for by, ref in enumerate((half_ref, recv_ref)):
        unit[pl.ds(pl.multiple_of((place[0] ^ by) * rows, 16), rows), :] = wide32(ref[...])
    for kind in range(3):
        outs[kind][:LANES, :] = unit[kind * LANES : (kind + 1) * LANES, :]
        outs[kind][LANES:, :] = unit[3 * LANES + kind * rest : 3 * LANES + (kind + 1) * rest, :]
    outs[3][...] = unit[3 * quarter : 4 * quarter, :]
    if len(outs) > 4:
        outs[4][...] = unit[4 * quarter :, :]
    sums = jnp.sum(unit[: 3 * quarter, :] * wide32(w_ref[...]), axis=0, keepdims=True)
    gain_grad_ref[...] = jnp.broadcast_to(sums / gain_ref[...], gain_grad_ref.shape)


def mixer_finish(place, half, recv, weights, gain, *after):
    rows, columns = half.shape
    quarter = weights.shape[0] // 3
    whole = lambda *shape: pl.BlockSpec(shape, lambda i, s: (0, 0))
    shapes = [(quarter, columns)] * 4 + [(2 * rows - 4 * quarter, columns)] * (2 * rows > 4 * quarter) + [(8, columns)]
    return kernel_call(
        mixer_finish_body,
        [made(shape, jnp.float32) for shape in shapes],
        [pltpu.VMEM((2 * rows, columns), jnp.float32)],
        (1,),
        [whole(rows, columns)] * 2 + [whole(*weights.shape), whole(*gain.shape)],
        [whole(*shape) for shape in shapes],
        1,
        "mixer_finish",
        after,
    )(place, half, recv, weights, gain)


def share_body(place, in_ref, out_ref, share_ref):
    share_ref[...] = jnp.where(place[0] == 0, in_ref[...], out_ref[...])


def far_share(place, w_in, w_out, count, *after):
    shape = (w_in.shape[0] // count, w_in.shape[1])
    rows = pl.BlockSpec(shape, lambda i, s: (s[1], 0))
    return kernel_call(
        share_body,
        [made(shape)],
        grid=(1,),
        in_specs=[rows, rows],
        out_specs=[pl.BlockSpec(shape, lambda i, s: (0, 0))],
        scalars=1,
        name="far_share",
        after=after,
    )(place, w_in, w_out)[0]


def exchanged(array, axis, by):
    devices = lax.axis_size(axis)
    return lax.ppermute(array, axis, [(i, i ^ by) for i in range(devices)])


def core_swap(array):
    return exchanged(array, TENSOR, 1)


def half_swap(array):
    return exchanged(array, TENSOR, 2)


def chip_place():
    return lax.axis_index(SEQ) * (lax.axis_size(TENSOR) // 2) + lax.axis_index(TENSOR) // 2


def swapped_rows(parts):
    return [parts[0]] + [exchanged(part, (SEQ, TENSOR), 2 * by) for by, part in enumerate(parts) if by]


def nt(left, right):
    return dot_nt(left, right)


def tn(left, right):
    return dot_tn(left, right)


def with_other(own):
    return jnp.concatenate([own, core_swap(own)], axis=0)


def closing_parts(parts):
    half = parts[0][0].shape[0] // 2
    other = sum(dot(left[half:], right, over) for left, right, over in parts)
    own = sum(dot(left[:half], right, over) for left, right, over in parts)
    return own, low16(other)


def closing(parts):
    own, other = closing_parts(parts)
    return own, core_swap(other)


def swapped_parts(parts):
    return lax.all_to_all(parts, DP, 0, 0)


def dealt(half):
    return swapped_parts(half.reshape(lax.axis_size(DP), -1, half.shape[1]))


def row_shards(
    tokens,
    out_grad,
    segments,
    gain_mix,
    query_mix,
    key_mix,
    value_mix,
    output_mix,
    shift_kernel,
    decay_rate,
    gain_ff1,
    ff_in1,
    ff_out1,
    gain_att,
    query_att,
    key_att,
    value_att,
    output_att,
    gain_ff2,
    ff_in2,
    ff_out2,
):
    features = tokens.shape[2]
    taps, quarter = shift_kernel.shape
    length = segments.shape[1]
    place = jnp.stack([lax.axis_index(SEQ), lax.axis_index(DP), chip_place()]).astype(jnp.int32)
    count = lax.axis_size(DP)

    mine = deal_rows(place, tokens)
    share = half_swap(far_share(place, ff_in1, ff_out1, count, mine[0]))
    mix_own = packed([query_mix.T, key_mix.T, value_mix.T], mine[0])
    mine = swapped_rows(mine)
    mix_far = half_swap(mix_own)
    far_one = lax.all_gather(share, (SEQ, DP), axis=0, tiled=True)
    few = jnp.concatenate([shift_kernel, decay_rate.reshape(1, -1) * (-1.0 / length)], axis=0)
    few_far = half_swap(few)
    both = jnp.concatenate([few, few_far], axis=1)

    seg_row = lax.dynamic_index_in_dim(segments, chip_place(), 0, False)
    core = (lax.axis_index(TENSOR) % 2).astype(jnp.int32)
    seg = jnp.concatenate([seg_row, core.reshape(1)])
    padded = jnp.pad(seg_row, (taps, taps), constant_values=-1)
    segb = jnp.broadcast_to(padded[:, None], (padded.shape[0], LANES))
    marks = (segb, seg_row.reshape(-1, CHUNK))
    att_marks = (segb, seg_row.reshape(-1, BLOCK))
    gains = [gain.reshape(1, -1) for gain in (gain_mix, gain_ff1, gain_att, gain_ff2)]
    h3 = [{"seg": seg, "kernel": table[:taps], "logdec": table[taps:], "marks": marks} for table in (few, both)]

    stream0, normed = first_norm(place, mine, gains[0], share, few_far)
    x_mix = with_other(normed)
    mix_w = [mix_own[: 3 * LANES]]
    qkv_mix = [low16(nt(x_mix, mix_w[0]))]
    kept_mix = [h3_forward_call(0, qkv_mix[0], **h3[0])]
    mix_w.append(joined_tiles(1, 2, mix_own, mix_far, kept_mix[0][0]))
    qkv_mix.append(low16(nt(x_mix, mix_w[1])))
    share = half_swap(far_share(place, ff_in2, ff_out2, count, mix_w[1]))
    mix_o = half_swap(copied(output_mix, mix_w[1]))
    kept_mix.append(touched(h3_forward_call(1, qkv_mix[1], **h3[1]), share, mix_o))
    out_mix = [kept[0] for kept in kept_mix]
    mix_o = stacked(output_mix, mix_o, out_mix[1])
    far_two = lax.all_gather(share, (SEQ, DP), axis=0, tiled=True)
    att_own = packed([query_att.T, key_att.T, value_att.T], mix_w[1])
    out_w = [mix_o[:LANES], mix_o[LANES:]]
    sums = closing([(out, weight, over_nn) for out, weight in zip(out_mix, out_w)])
    stream1, normed = add_norm(stream0, *sums, gains[1])
    x_one = with_other(normed)
    att_far = half_swap(att_own)
    kept_one = touched(ff_forward_call(x_one, ff_in1, ff_out1, far_one), att_far)
    att_w = joined_tiles(0, 3, att_own, att_far, kept_one[4])
    stream2, normed = add_norm(stream1, kept_one[4], core_swap(kept_one[5]), gains[2])
    x_att = with_other(normed)
    qkv_att = low16(nt(x_att, att_w))
    back_parts = swapped_rows(deal_rows(place, out_grad, kept_one[4]))
    att_o = half_swap(output_att)
    out_att, total = touched(att_forward_call(taps, seg, qkv_att, att_marks), *back_parts[1:], att_o, far_two)
    att_o = stacked(output_att, att_o, out_att)
    back_low = collect_rows(place, back_parts, jnp.bfloat16, out_att).reshape(-1, features)
    stream3, normed = add_norm(stream2, *closing([(out_att, att_o, over_nn)]), gains[3])
    x_two = with_other(normed)
    kept_two = ff_forward_call(x_two, ff_in2, ff_out2, far_two)
    mixed = stream3 + (kept_two[4] + wide32(core_swap(kept_two[5])))
    mixed_parts = deal_rows(place, mixed.reshape(tokens.shape))

    def ff_back(g, x, kept, w_in, w_out, far):
        far_in, far_out = far[:features], far[features:]
        far_grad = low16(nt(g, far_out) * wide32(kept[3]))
        own_grad = low16(nt(g, w_out) * wide32(kept[2]))
        sums = closing([(far_grad, far_in, over_nt), (own_grad, w_in, over_nt)])
        far_unit = (low16(tn(kept[1], g)), low16(tn(x, far_grad)))
        own_unit = (low16(tn(kept[0], g)), low16(tn(x, own_grad)))
        return sums, own_unit, far_unit

    g_two = with_other(back_low)
    sums, two_own, two_far = ff_back(g_two, x_two, kept_two, ff_in2, ff_out2, far_two)
    back, back_low = norm_back(wide32(back_low), *sums, stream3, gains[3], *two_far)
    two_recv = [half_swap(part) for part in two_far]

    g_att = with_other(back_low)
    dqkv_att = att_backward_call(taps, seg, qkv_att, low16(nt(g_att, att_o)), total, att_marks, mixed_parts[0])
    att_unit, att_far_unit = far_grads(0, x_att, dqkv_att, g_att, [out_att])
    att_recv = half_swap(att_far_unit)
    sums = closing([(dqkv_att, att_w, over_nn)])
    back, back_low = norm_back(back, *sums, stream2, gains[2], att_far_unit, two_recv[0])

    g_one = with_other(back_low)
    sums, one_own, one_far = ff_back(g_one, x_one, kept_one, ff_in1, ff_out1, far_one)
    two = ff_fold(place, two_own, two_recv, one_far[0])
    back, back_low = norm_back(back, *sums, stream1, gains[1], *one_far, two[1])
    one_recv = [half_swap(part) for part in one_far]

    g_mix = with_other(back_low)
    grad_mixed = low16(nt(g_mix, mix_o) * (1.0 / math.sqrt(HEAD_DIM)))
    att = fold(place, att_unit, att_recv, grad_mixed)
    att_got = exchanged(att[1], SEQ, 1)
    two_half = add_two(two[0], exchanged(two[1], SEQ, 1), grad_mixed)
    two_half = lax.psum(two_half, DP)

    def small_rows(kernel_grad, log_grad):
        small = jnp.concatenate([kernel_grad, log_grad * (-1.0 / length)], axis=0)
        return jnp.pad(low16(small), ((0, -small.shape[0] % 512), (0, 0))).reshape(-1, features)

    h3_back = lambda i, *after: h3_backward_call(
        i, qkv_mix[i], kept_mix[i][1], grad_mixed, kept_mix[i][2], **h3[i], after=after
    )
    late = touched(h3_back(1, att[1], *one_own), att_got, *one_recv)
    skip = quarter - LANES
    small = small_rows(late[1][:, skip:], late[2][:, skip:])
    one = ff_fold(place, one_own, one_recv, late[0])
    one_got = exchanged(one[1], SEQ, 1)
    att_half = add_two(att[0], att_got, one[1])
    att_parts = dealt(att_half)
    rest, mix_far_unit = far_grads(1, x_mix, late[0], g_mix, out_mix, small, after=(att_half,))
    mix_recv = half_swap(mix_far_unit)
    att_final = sum_parts(att_parts, count, mix_far_unit)
    att = swapped_parts(att_final)
    two_back = exchanged(two_half, SEQ, 1)
    early = touched(h3_back(0, att_final, two_half), att, one_got)
    small = small_rows(
        jnp.concatenate([early[1], late[1][:, :skip]], axis=1), jnp.concatenate([early[2], late[2][:, :skip]], axis=1)
    )

    mix_unit = own_grads(x_mix, early[0], rest, small)
    mix = fold(place, mix_unit, mix_recv, two_back)
    mix_got = exchanged(mix[1], SEQ, 1)
    one_half = add_two(one[0], one_got, mix[1])
    one_parts = dealt(one_half)
    att = touched([att.reshape(-1, features)], mix[1])[0]
    mix_half = add_two(mix[0], mix_got, att)
    one_final = sum_parts(one_parts, 1, mix_half)[0]
    mix_parts = dealt(touched([mix_half], one_final)[0])
    one = lax.all_gather(one_final, (SEQ, DP), axis=0, tiled=True)
    att_back = exchanged(att, SEQ, 1)
    mixed_parts = swapped_rows(touched(mixed_parts, mix_half))
    own, other = closing_parts([(early[0], mix_w[0], over_nn), (late[0], mix_w[1], over_nn)])
    other = touched([other], one_final)[0]
    back, _ = norm_back(back, own, core_swap(other), stream0, gains[0])
    tokens_parts = deal_rows(place, back.reshape(tokens.shape))
    mix_final = sum_parts(mix_parts, count, tokens_parts[1], att_back)
    mix = swapped_parts(mix_final)
    tokens_parts = swapped_rows(touched(tokens_parts, mix_final))
    mixed_out = collect_rows(place, mixed_parts, jnp.float32, mix_final)
    tokens_grad = collect_rows(place, tokens_parts, jnp.float32, mixed_out)
    in_two, out_two, two_gain = ff_finish(place, two_half, two_back, ff_in2, gains[3], mix_final)
    q_att, k_att, v_att, o_att, att_gain = mixer_finish(place, att, att_back, att_own, gains[2], mix_final)
    mix = touched([mix.reshape(-1, features)], att_gain, tokens_grad, two_gain)[0]
    mix_back = exchanged(mix, SEQ, 1)
    in_one, out_one, one_gain = whole_finish(one, ff_in1, gains[1], mix)
    q_mix, k_mix, v_mix, o_mix, small, mix_gain = mixer_finish(place, mix, mix_back, mix_own, gains[0], one_gain)
    gain_grads = jnp.concatenate([part[:1] for part in (mix_gain, one_gain, att_gain, two_gain)])
    gain_grads = gain_grads + half_swap(gain_grads)
    gain_grads = gain_grads + core_swap(gain_grads)
    small = small.reshape(-1, quarter)
    return (
        mixed_out,
        tokens_grad,
        gain_grads[0],
        q_mix.T,
        k_mix.T,
        v_mix.T,
        o_mix,
        small[:taps],
        gain_grads[1],
        in_one,
        out_one,
        gain_grads[2],
        q_att.T,
        k_att.T,
        v_att.T,
        o_att,
        gain_grads[3],
        in_two,
        out_two,
        small[taps].reshape(decay_rate.shape),
    )


def row_plan_fits(sizes):
    return sizes[SEQ] == 2 and sizes[TENSOR] == 4


def solution(mesh):
    plan = row_shards if row_plan_fits(dict(mesh.shape)) else shards
    return jax.shard_map(
        plan,
        mesh=mesh,
        in_specs=(
            P(DP, (SEQ, TENSOR), None),
            P(DP, (SEQ, TENSOR), None),
            P(DP, None),
            P(),
            P(None, TENSOR),
            P(None, TENSOR),
            P(None, TENSOR),
            P(TENSOR, None),
            P(None, TENSOR),
            P(TENSOR, None),
            P(),
            P(None, TENSOR),
            P(TENSOR, None),
            P(),
            P(None, TENSOR),
            P(None, TENSOR),
            P(None, TENSOR),
            P(TENSOR, None),
            P(),
            P(None, TENSOR),
            P(TENSOR, None),
        ),
        out_specs=(
            P(DP, (SEQ, TENSOR), None),
            P(DP, (SEQ, TENSOR), None),
            P(),
            P(None, TENSOR),
            P(None, TENSOR),
            P(None, TENSOR),
            P(TENSOR, None),
            P(None, TENSOR),
            P(),
            P(None, TENSOR),
            P(TENSOR, None),
            P(),
            P(None, TENSOR),
            P(None, TENSOR),
            P(None, TENSOR),
            P(TENSOR, None),
            P(),
            P(None, TENSOR),
            P(TENSOR, None),
            P(TENSOR, None),
        ),
        check_vma=False,
    )
```

```python
import functools
import math

import jax
import jax.numpy as jnp
from jax import lax
from jax.experimental import pallas as pl
from jax.experimental.pallas import tpu as pltpu
from jax.sharding import PartitionSpec as P

HEAD_DIM = 64
DP, SEQ, TENSOR = "dp", "seq", "tensor"


highest = lax.Precision.HIGHEST
norm_eps = 1e-05
masked_score = -1e30


def passed_along(array, axis, by):
    devices = lax.axis_size(axis)
    pairs = [(i, i + by) for i in range(devices) if 0 <= i + by < devices]
    return lax.ppermute(array, axis, pairs)


def prefix(array, axis, combine, identity):
    devices, here = (lax.axis_size(axis), lax.axis_index(axis))
    everything = jax.tree.map(lambda part: lax.all_gather(part, axis), array)
    start = jax.tree.map(
        lambda part, zero: jnp.broadcast_to(jnp.asarray(zero, part.dtype), part.shape),
        array,
        identity,
    )

    def step(k, before):
        reached = k < here
        new = combine(before, jax.tree.map(lambda part: part[k], everything))
        return jax.tree.map(lambda a, b: jnp.where(reached, a, b), new, before)

    return lax.fori_loop(0, devices, step, start)


def prefix_2(array, axis, join, neutral):
    count = lax.axis_size(axis)
    place = lax.axis_index(axis)
    ahead = count - 1 - place
    gathered = jax.tree.map(
        lambda a, kind: lax.all_gather(a.astype(kind), axis), array, (jnp.bfloat16, jnp.bfloat16)
    )
    state = jax.tree.map(lambda a, e: jnp.zeros_like(a) + jnp.asarray(e, a.dtype), array, neutral)

    def one(step, state):
        source = count - 1 - step
        return join(
            state,
            jax.tree.map(
                lambda a, own: lax.dynamic_index_in_dim(a, source, 0, False).astype(own.dtype),
                gathered,
                array,
            ),
        )

    return lax.fori_loop(0, ahead, one, state)


def lower_triangle(value):
    return value.astype(jnp.bfloat16)


def bmul(form, left, right):
    return jnp.einsum(form, left, right, preferred_element_type=jnp.float32)


def fmul(form, left, right):
    return jnp.einsum(form, left, right, precision=highest, preferred_element_type=jnp.float32)


def layer_norm_forward(residual_stream, norm_gain_weight):
    feature_mean = jnp.mean(residual_stream, axis=-1, keepdims=True)
    mean_centered = residual_stream - feature_mean
    scale_factor = lax.rsqrt(
        jnp.mean(mean_centered * mean_centered, axis=-1, keepdims=True) + norm_eps
    )
    standardized_input = mean_centered * scale_factor
    return (lower_triangle(standardized_input * norm_gain_weight), standardized_input, scale_factor)


def layer_norm_backward(normalized_gradient, standardized_input, scale_factor, norm_gain_weight):
    gain_gradient = jnp.sum(normalized_gradient * standardized_input, axis=(0, 1))
    rescaled_input = normalized_gradient * norm_gain_weight
    mean_centered = rescaled_input - jnp.mean(rescaled_input, axis=-1, keepdims=True)
    return (
        scale_factor
        * (
            mean_centered
            - standardized_input
            * jnp.mean(rescaled_input * standardized_input, axis=-1, keepdims=True)
        ),
        gain_gradient,
    )


def widen(normalized_input):
    return lax.all_gather(normalized_input, TENSOR, axis=1, tiled=True)


def narrow(partial_value):
    return lax.psum_scatter(partial_value, TENSOR, scatter_dimension=1, tiled=True)


def widen_grad(grad_stream):
    return lax.all_gather(lower_triangle(grad_stream), TENSOR, axis=1, tiled=True)


def narrow_grad(partial_value):
    return lax.psum_scatter(partial_value, TENSOR, scatter_dimension=1, tiled=True)


def combine_states(earlier, later):
    return (earlier[0] * later[0], later[1] + later[0][..., None] * earlier[1])


def feed_forward(residual_stream, norm_gain_weight, w_in, w_out):
    normalized_input, standardized_input, scale_factor = layer_norm_forward(
        residual_stream, norm_gain_weight
    )
    widened_hidden = widen(normalized_input)
    hidden_preactivation = bmul("rtd,df->rtf", widened_hidden, w_in)
    hidden_units = lower_triangle(jax.nn.gelu(hidden_preactivation, approximate=False))
    final_result = residual_stream + narrow(bmul("rtf,fd->rtd", hidden_units, w_out))
    return (
        final_result,
        (widened_hidden, standardized_input, scale_factor, hidden_preactivation, hidden_units),
    )


def feed_backward(grad_stream, saved_residuals, norm_gain_weight, w_in, w_out):
    widened_hidden, standardized_input, scale_factor, hidden_preactivation, hidden_units = (
        saved_residuals
    )
    grad_wide = widen_grad(grad_stream)
    grad_out_w = bmul("rtf,rtd->fd", hidden_units, grad_wide)
    grad_hidden = bmul("rtd,fd->rtf", grad_wide, w_out)
    _, gelu_pull = jax.vjp(
        lambda value: jax.nn.gelu(value, approximate=False), hidden_preactivation
    )
    grad_before = lower_triangle(gelu_pull(grad_hidden)[0])
    grad_in_w = bmul("rtd,rtf->df", widened_hidden, grad_before)
    normalized_gradient = narrow_grad(bmul("rtf,df->rtd", grad_before, w_in))
    norm_input_gradient, gain_gradient = layer_norm_backward(
        normalized_gradient, standardized_input, scale_factor, norm_gain_weight
    )
    return (grad_stream + norm_input_gradient, gain_gradient, grad_in_w, grad_out_w)


def mixer_forward(residual_stream, seg_rows, norm_gain_weight, w_q, w_k, w_v, w_o, kernel, rate):
    normalized_input, standardized_input, scale_factor = layer_norm_forward(
        residual_stream, norm_gain_weight
    )
    widened_hidden = widen(normalized_input)
    rows, group_len = (widened_hidden.shape[0], widened_hidden.shape[1])
    heads, width = rate.shape
    query_matrix = lower_triangle(bmul("rtd,de->rte", widened_hidden, w_q))
    key_matrix = lower_triangle(bmul("rtd,de->rte", widened_hidden, w_k))
    value_matrix = lower_triangle(bmul("rtd,de->rte", widened_hidden, w_v))
    taps = kernel.shape[0]
    start = lax.axis_index(SEQ) * group_len
    length = group_len * lax.axis_size(SEQ)
    padded = jnp.concatenate([jnp.full((rows, taps), -1, jnp.int32), seg_rows], axis=1)
    seg_ext = lax.dynamic_slice_in_dim(padded, start + 1, group_len + taps - 1, 1)
    owning_segment = seg_ext[:, taps - 1 :]
    rim = passed_along(key_matrix[:, group_len - taps + 1 :, :], SEQ, 1)
    extended = jnp.concatenate([rim, key_matrix], axis=1).astype(jnp.float32)
    shifted = jnp.zeros(key_matrix.shape, jnp.float32)
    match_list = []
    for tap in range(taps):
        first = taps - 1 - tap
        match = (seg_ext[:, first : first + group_len] == owning_segment).astype(jnp.float32)[
            :, :, None
        ]
        match_list.append(match)
        shifted = shifted + kernel[tap] * extended[:, first : first + group_len] * match
    matches = jnp.stack(match_list)
    logdec = -rate / length
    steps = jnp.arange(group_len, dtype=jnp.float32)[:, None, None]
    rising = jnp.exp(steps * logdec)
    falling = jnp.exp(-steps * logdec)
    leading = jnp.exp((steps + 1.0) * logdec)
    trailing = jnp.exp((group_len - 1.0 - steps) * logdec)
    before = seg_ext[:, taps - 2]
    final = owning_segment[:, -1]
    order = jnp.arange(group_len)
    same = (
        (owning_segment[:, :, None] == owning_segment[:, None, :])
        & (order[:, None] >= order[None, :])
    ).astype(jnp.float32)
    gate = (owning_segment == before[:, None]).astype(jnp.float32)[:, :, None, None]
    ends = (owning_segment == final[:, None]).astype(jnp.float32)[:, :, None, None]
    carry_on = (final == before).astype(jnp.float32)[:, None, None]
    query_f = query_matrix.astype(jnp.float32).reshape(rows, group_len, heads, width)
    shift_f = shifted.reshape(rows, group_len, heads, width)
    value_f = value_matrix.astype(jnp.float32).reshape(rows, group_len, heads, width)
    query_up = query_f * rising
    key_down = shift_f * falling
    query_lead = query_f * leading * gate
    key_tail = shift_f * trailing * ends
    mixing = fmul("rthi,rshi->rhts", query_up, key_down) * same[:, None]
    decay = jnp.exp(group_len * logdec)[None] * carry_on
    end_state = fmul("rshi,rshj->rhij", key_tail, value_f)
    identity = (jnp.ones(decay.shape, jnp.float32), jnp.zeros(end_state.shape, jnp.float32))
    entering = prefix((decay, end_state), SEQ, combine_states, identity)[1]
    mixed = fmul("rhts,rshj->rthj", mixing, value_f) + fmul("rthi,rhij->rthj", query_lead, entering)
    out_mix = lower_triangle(
        mixed.reshape(rows, group_len, heads * width) * (1.0 / math.sqrt(width))
    )
    final_result = residual_stream + narrow(bmul("rte,ed->rtd", out_mix, w_o))
    saved_residuals = (
        widened_hidden,
        standardized_input,
        scale_factor,
        extended,
        matches,
        value_f,
        rising,
        falling,
        leading,
        trailing,
        gate,
        ends,
        same,
        query_up,
        key_down,
        query_lead,
        key_tail,
        mixing,
        decay,
        entering,
        identity,
        out_mix,
    )
    return (final_result, saved_residuals)


def mixer_backward(
    grad_stream, saved_residuals, norm_gain_weight, w_q, w_k, w_v, w_o, kernel, rate
):
    (
        widened_hidden,
        standardized_input,
        scale_factor,
        extended,
        matches,
        value_f,
        rising,
        falling,
        leading,
        trailing,
        gate,
        ends,
        same,
        query_up,
        key_down,
        query_lead,
        key_tail,
        mixing,
        decay,
        entering,
        identity,
        out_mix,
    ) = saved_residuals
    rows, group_len = (widened_hidden.shape[0], widened_hidden.shape[1])
    heads, width = rate.shape
    taps = kernel.shape[0]
    length = group_len * lax.axis_size(SEQ)
    grad_wide = widen_grad(grad_stream)
    grad_o = bmul("rte,rtd->ed", out_mix, grad_wide)
    grad_mixed = bmul("rtd,ed->rte", grad_wide, w_o).reshape(rows, group_len, heads, width) * (
        1.0 / math.sqrt(width)
    )
    grad_mixing = fmul("rthj,rshj->rhts", grad_mixed, value_f) * same[:, None]
    grad_qup = fmul("rhts,rshi->rthi", grad_mixing, key_down)
    grad_kdown = fmul("rhts,rthi->rshi", grad_mixing, query_up)
    reach = fmul("rthj,rhij->rthi", grad_mixed, entering)
    local_back = fmul("rthi,rthj->rhij", query_lead, grad_mixed)
    leaving = prefix_2((decay, local_back), SEQ, combine_states, identity)[1]
    spread = fmul("rshj,rhij->rshi", value_f, leaving)
    grad_value = fmul("rhts,rthj->rshj", mixing, grad_mixed) + fmul(
        "rshi,rhij->rshj", key_tail, leaving
    )
    grad_query = grad_qup * rising + reach * leading * gate
    grad_shift = grad_kdown * falling + spread * trailing * ends
    steps = jnp.arange(group_len, dtype=jnp.float32)[:, None, None]
    local_terms = steps * (query_up * grad_qup - key_down * grad_kdown)
    local_terms = (
        local_terms
        + (steps + 1.0) * query_lead * reach
        + (group_len - 1.0 - steps) * key_tail * spread
    )
    grad_log = jnp.sum(local_terms, axis=(0, 1))
    grad_log = grad_log + group_len * jnp.sum(jnp.sum(leaving * entering, axis=3) * decay, axis=0)
    grad_rate = -grad_log / length
    grad_shift = grad_shift.reshape(rows, group_len, heads * width)
    grad_ext = jnp.zeros(extended.shape, jnp.float32)
    kernel_rows = []
    for tap in range(taps):
        first = taps - 1 - tap
        masked = grad_shift * matches[tap]
        kernel_rows.append(jnp.sum(masked * extended[:, first : first + group_len], axis=(0, 1)))
        grad_ext = grad_ext + jnp.pad(
            kernel[tap] * masked, ((0, 0), (first, taps - 1 - first), (0, 0))
        )
    grad_kernel = jnp.stack(kernel_rows)
    returned = passed_along(grad_ext[:, : taps - 1].astype(jnp.bfloat16), SEQ, -1).astype(
        jnp.float32
    )
    grad_keys = grad_ext[:, taps - 1 :] + jnp.pad(
        returned, ((0, 0), (group_len - taps + 1, 0), (0, 0))
    )
    query_low = lower_triangle(grad_query.reshape(rows, group_len, heads * width))
    keys_low = lower_triangle(grad_keys)
    value_low = lower_triangle(grad_value.reshape(rows, group_len, heads * width))
    grad_qw = bmul("rtd,rte->de", widened_hidden, query_low)
    grad_kw = bmul("rtd,rte->de", widened_hidden, keys_low)
    grad_vw = bmul("rtd,rte->de", widened_hidden, value_low)
    partial_value = bmul("rte,de->rtd", query_low, w_q) + bmul("rte,de->rtd", keys_low, w_k)
    partial_value = partial_value + bmul("rte,de->rtd", value_low, w_v)
    normalized_gradient = narrow_grad(partial_value)
    norm_input_gradient, gain_gradient = layer_norm_backward(
        normalized_gradient, standardized_input, scale_factor, norm_gain_weight
    )
    return (
        grad_stream + norm_input_gradient,
        gain_gradient,
        grad_qw,
        grad_kw,
        grad_vw,
        grad_o,
        grad_kernel,
        grad_rate,
    )


def split_heads(value):
    return value.reshape(value.shape[0], value.shape[1] // HEAD_DIM, HEAD_DIM)


def scores_of(query_rows, key_rows, query_places, key_places, query_seg, key_seg):
    raw = bmul("thd,shd->hts", split_heads(query_rows), split_heads(key_rows)) * (
        1.0 / math.sqrt(HEAD_DIM)
    )
    allowed = (query_places[:, None] >= key_places[None, :]) & (
        query_seg[:, None] == key_seg[None, :]
    )
    return jnp.where(allowed[None], raw, masked_score)


def attend_forward(residual_stream, seg_rows, norm_gain_weight, w_q, w_k, w_v, w_o):
    normalized_input, standardized_input, scale_factor = layer_norm_forward(
        residual_stream, norm_gain_weight
    )
    widened_hidden = widen(normalized_input)
    rows, group_len = (widened_hidden.shape[0], widened_hidden.shape[1])
    query_matrix = lower_triangle(bmul("rtd,de->rte", widened_hidden, w_q))
    key_matrix = lower_triangle(bmul("rtd,de->rte", widened_hidden, w_k))
    value_matrix = lower_triangle(bmul("rtd,de->rte", widened_hidden, w_v))
    gathered_key_rows, gathered_value_rows = (
        lax.all_gather(key_matrix, SEQ, axis=1, tiled=True),
        lax.all_gather(value_matrix, SEQ, axis=1, tiled=True),
    )
    length = gathered_key_rows.shape[1]
    start = lax.axis_index(SEQ) * group_len
    owning_segment = lax.dynamic_slice_in_dim(seg_rows, start, group_len, 1)
    query_places = start + jnp.arange(group_len)
    key_places = jnp.arange(length)

    def forward_row(pieces):
        query_row, key_row, value_row, seg_own, seg_all = pieces
        scores = scores_of(query_row, key_row, query_places, key_places, seg_own, seg_all)
        top = jnp.max(scores, axis=-1, keepdims=True)
        expd = jnp.exp(scores - top)
        total = jnp.sum(expd, axis=-1, keepdims=True)
        softened = lower_triangle(expd / total)
        attended = bmul("hts,shd->thd", softened, split_heads(value_row))
        return (
            lower_triangle(attended.reshape(group_len, attended.shape[1] * HEAD_DIM)),
            (top + jnp.log(total))[..., 0],
        )

    attention_output, log_normalizer = lax.map(
        forward_row,
        (query_matrix, gathered_key_rows, gathered_value_rows, owning_segment, seg_rows),
    )
    final_result = residual_stream + narrow(bmul("rte,ed->rtd", attention_output, w_o))
    saved_residuals = (
        widened_hidden,
        standardized_input,
        scale_factor,
        query_matrix,
        key_matrix,
        value_matrix,
        gathered_key_rows,
        gathered_value_rows,
        owning_segment,
        log_normalizer,
        attention_output,
    )
    return (final_result, saved_residuals)


def attend_backward(grad_stream, saved_residuals, seg_rows, norm_gain_weight, w_q, w_k, w_v, w_o):
    (
        widened_hidden,
        standardized_input,
        scale_factor,
        query_matrix,
        key_matrix,
        value_matrix,
        gathered_key_rows,
        gathered_value_rows,
        owning_segment,
        log_normalizer,
        attention_output,
    ) = saved_residuals
    rows, group_len = (widened_hidden.shape[0], widened_hidden.shape[1])
    length = gathered_key_rows.shape[1]
    start = lax.axis_index(SEQ) * group_len
    query_places = start + jnp.arange(group_len)
    key_places = jnp.arange(length)
    scale = 1.0 / math.sqrt(HEAD_DIM)
    grad_wide = widen_grad(grad_stream)
    grad_o = bmul("rte,rtd->ed", attention_output, grad_wide)
    grad_out = lower_triangle(bmul("rtd,ed->rte", grad_wide, w_o))

    def query_common(pieces):
        query_row, key_row, value_row, seg_own, seg_all, total_row, grad_row = pieces
        scores = scores_of(query_row, key_row, query_places, key_places, seg_own, seg_all)
        softened = jnp.exp(scores - total_row[:, :, None])
        grad_soft = bmul("thd,shd->hts", split_heads(grad_row), split_heads(value_row))
        inner = jnp.sum(softened * grad_soft, axis=-1)
        grad_score = lower_triangle(softened * (grad_soft - inner[:, :, None]))
        grad_q = bmul("hts,shd->thd", grad_score, split_heads(key_row)) * scale
        return (softened, grad_score, grad_q.reshape(group_len, -1), inner)

    pieces = (
        query_matrix,
        gathered_key_rows,
        gathered_value_rows,
        owning_segment,
        seg_rows,
        log_normalizer,
        grad_out,
    )

    def query_only(row_pieces):
        _, _, grad_q, inner = query_common(row_pieces)
        return (grad_q, inner)

    grad_query, inner = lax.map(query_only, pieces)
    all_query, all_grad = (
        lax.all_gather(query_matrix, SEQ, axis=1, tiled=True),
        lax.all_gather(grad_out, SEQ, axis=1, tiled=True),
    )
    all_total, all_inner = (
        lax.all_gather(log_normalizer, SEQ, axis=2, tiled=True),
        lax.all_gather(inner, SEQ, axis=2, tiled=True),
    )

    def key_row_fn(row_pieces):
        query_row, key_row, value_row, seg_all, seg_own, total_row, inner_row, grad_row = row_pieces
        scores = scores_of(query_row, key_row, key_places, query_places, seg_all, seg_own)
        softened = jnp.exp(scores - total_row[:, :, None])
        grad_soft = bmul("thd,shd->hts", split_heads(grad_row), split_heads(value_row))
        grad_score = lower_triangle(softened * (grad_soft - inner_row[:, :, None]))
        grad_k = bmul("hts,thd->shd", grad_score, split_heads(query_row)) * scale
        grad_v = bmul("hts,thd->shd", lower_triangle(softened), split_heads(grad_row))
        return (grad_k.reshape(group_len, -1), grad_v.reshape(group_len, -1))

    grad_keys, grad_values = lax.map(
        key_row_fn,
        (
            all_query,
            key_matrix,
            value_matrix,
            seg_rows,
            owning_segment,
            all_total,
            all_inner,
            all_grad,
        ),
    )
    query_low = lower_triangle(grad_query)
    keys_low = lower_triangle(grad_keys)
    value_low = lower_triangle(grad_values)
    grad_qw = bmul("rtd,rte->de", widened_hidden, query_low)
    grad_kw = bmul("rtd,rte->de", widened_hidden, keys_low)
    grad_vw = bmul("rtd,rte->de", widened_hidden, value_low)
    partial_value = bmul("rte,de->rtd", query_low, w_q) + bmul("rte,de->rtd", keys_low, w_k)
    partial_value = partial_value + bmul("rte,de->rtd", value_low, w_v)
    normalized_gradient = narrow_grad(partial_value)
    norm_input_gradient, gain_gradient = layer_norm_backward(
        normalized_gradient, standardized_input, scale_factor, norm_gain_weight
    )
    return (grad_stream + norm_input_gradient, gain_gradient, grad_qw, grad_kw, grad_vw, grad_o)


def shards(
    tokens,
    out_grad,
    segments,
    gain_mix,
    query_mix,
    key_mix,
    value_mix,
    output_mix,
    shift_kernel,
    decay_rate,
    gain_ff1,
    ff_in1,
    ff_out1,
    gain_att,
    query_att,
    key_att,
    value_att,
    output_att,
    gain_ff2,
    ff_in2,
    ff_out2,
):
    stream_one, kept_mix = mixer_forward(
        tokens,
        segments,
        gain_mix,
        query_mix,
        key_mix,
        value_mix,
        output_mix,
        shift_kernel,
        decay_rate,
    )
    stream_two, kept_first = feed_forward(stream_one, gain_ff1, ff_in1, ff_out1)
    stream_three, kept_att = attend_forward(
        stream_two, segments, gain_att, query_att, key_att, value_att, output_att
    )
    stream_four, kept_second = feed_forward(stream_three, gain_ff2, ff_in2, ff_out2)
    back_three, gain_two_grad, in_two_grad, out_two_grad = feed_backward(
        out_grad, kept_second, gain_ff2, ff_in2, ff_out2
    )
    back_two, att_gain_grad, att_q_grad, att_k_grad, att_v_grad, att_o_grad = attend_backward(
        back_three, kept_att, segments, gain_att, query_att, key_att, value_att, output_att
    )
    back_one, gain_one_grad, in_one_grad, out_one_grad = feed_backward(
        back_two, kept_first, gain_ff1, ff_in1, ff_out1
    )
    (
        back_zero,
        mix_gain_grad,
        mix_q_grad,
        mix_k_grad,
        mix_v_grad,
        mix_o_grad,
        kernel_grad,
        rate_grad,
    ) = mixer_backward(
        back_one,
        kept_mix,
        gain_mix,
        query_mix,
        key_mix,
        value_mix,
        output_mix,
        shift_kernel,
        decay_rate,
    )
    summed = lax.psum(
        (
            mix_q_grad,
            mix_k_grad,
            mix_v_grad,
            mix_o_grad,
            kernel_grad,
            in_one_grad,
            out_one_grad,
            att_q_grad,
            att_k_grad,
            att_v_grad,
            att_o_grad,
            in_two_grad,
            out_two_grad,
            rate_grad,
        ),
        (DP, SEQ),
    )
    gains = lax.psum(
        (mix_gain_grad, gain_one_grad, att_gain_grad, gain_two_grad), (DP, SEQ, TENSOR)
    )
    return (
        stream_four,
        back_zero,
        gains[0],
        summed[0],
        summed[1],
        summed[2],
        summed[3],
        summed[4],
        gains[1],
        summed[5],
        summed[6],
        gains[2],
        summed[7],
        summed[8],
        summed[9],
        summed[10],
        gains[3],
        summed[11],
        summed[12],
        summed[13],
    )


CHUNK = 128
LANES = 128
BLOCK = 2 * CHUNK
FF_COLUMNS = 768
MIB = 1024 * 1024


def dot(left, right, over):
    return lax.dot_general(left, right, (over, ((), ())), preferred_element_type=jnp.float32)


over_nn, over_nt = ((1,), (0,)), ((1,), (1,))


def dot_nn(left, right):
    return dot(left, right, over_nn)


def dot_nt(left, right):
    return dot(left, right, over_nt)


def dot_tn(left, right):
    return dot(left, right, ((0,), (0,)))


def low16(value):
    return value.astype(jnp.bfloat16)


def wide32(value):
    return value.astype(jnp.float32)


def made(shape, kind=jnp.bfloat16):
    return jax.ShapeDtypeStruct(shape, kind)


def kernel_call(
    body, outs, scratch=(), grid=(), in_specs=None, out_specs=None, scalars=0, name=None, after=(), cost=0
):
    if in_specs is None:
        in_specs, out_specs = pl.BlockSpec(memory_space=pltpu.VMEM), [pl.BlockSpec(memory_space=pltpu.VMEM)] * len(outs)
    params = pltpu.CompilerParams(vmem_limit_bytes=50 * MIB)
    estimate = pl.CostEstimate(flops=cost * 10**9, bytes_accessed=0, transcendentals=0)

    def call(*arrays):
        count = len(arrays)
        ins = [in_specs] * (count - scalars) if isinstance(in_specs, pl.BlockSpec) else list(in_specs)
        spec = pltpu.PrefetchScalarGridSpec(
            num_scalar_prefetch=scalars,
            grid=grid,
            in_specs=ins + [pl.BlockSpec(memory_space=pl.ANY)] * len(after),
            out_specs=out_specs,
            scratch_shapes=scratch,
        )

        def whole_body(*refs):
            body(*refs[:count], *refs[count + len(after) :])

        return pl.pallas_call(
            whole_body, grid_spec=spec, out_shape=outs, compiler_params=params, cost_estimate=estimate, name=name
        )(*arrays, *after)

    return call


def place_of(n, core, half):
    return pl.multiple_of(((n & 1) ^ core) * half + (n >> 1) * CHUNK, CHUNK)


def lane_heads():
    lane = lax.broadcasted_iota(jnp.int32, (CHUNK, LANES), 1)
    return [lane // HEAD_DIM == head for head in range(LANES // HEAD_DIM)]


def head_diagonal():
    row = lax.broadcasted_iota(jnp.int32, (LANES, LANES), 0)
    lane = lax.broadcasted_iota(jnp.int32, (LANES, LANES), 1)
    return row // HEAD_DIM == lane // HEAD_DIM


def causal_same(seg_rows, seg_lanes):
    row = lax.broadcasted_iota(jnp.int32, (CHUNK, CHUNK), 0)
    lane = lax.broadcasted_iota(jnp.int32, (CHUNK, CHUNK), 1)
    return (seg_rows == seg_lanes) & (row >= lane)


def pick_heads(heads, parts):
    result = parts[0]
    for head in range(1, len(parts)):
        result = jnp.where(heads[head], parts[head], result)
    return result


def decays(logdec):
    steps = wide32(lax.broadcasted_iota(jnp.int32, (CHUNK, LANES), 0))
    rising, falling = jnp.exp(steps * logdec), jnp.exp(-steps * logdec)
    return steps, rising, falling, jnp.exp(logdec), jnp.exp((CHUNK - 1.0) * logdec), jnp.exp(CHUNK * logdec)


def documents(seg_s, n):
    at = pl.multiple_of(n * CHUNK, CHUNK)
    before = jnp.where(n == 0, -1, seg_s[jnp.maximum(at - 1, 0)])
    return at, seg_s[at], seg_s[at + CHUNK - 1], before


def split_columns(ref, tile=0):
    first = 3 * LANES * tile
    return [ref.at[:, first + i * LANES : first + (i + 1) * LANES] for i in range(3)]


def tile_of(tile):
    return slice(tile * LANES, (tile + 1) * LANES)


def h3_forward_body(
    first, tiles, taps, seg_s, qkv_ref, w_ref, logdec_ref, segb_ref, segl_ref,
    out_ref, shift_ref, state_ref, key_f, masked, state,
):
    length = qkv_ref.shape[0]
    chunks, half, core = length // CHUNK, length // 2, seg_s[length]
    tables = [decays(logdec_ref[:, tile_of(first + tile)]) for tile in range(tiles)]
    heads, diagonal = lane_heads(), head_diagonal()
    key_f[0:taps, :] = jnp.zeros((taps, tiles * LANES), jnp.float32)
    state[...] = jnp.zeros_like(state)

    def chunk_step(n, _):
        at, low_doc, high_doc, before = documents(seg_s, n)
        here = pl.ds(place_of(n, core, half), CHUNK)
        for tile in range(tiles):
            key_f[pl.ds(at + taps, CHUNK), tile_of(tile)] = wide32(split_columns(qkv_ref, tile)[1][here, :])
        seg_here = segb_ref[pl.ds(at + taps, CHUNK), :]

        def one_doc(doc, totals):
            window = segb_ref[pl.ds(at, CHUNK + taps), :] == doc
            result = []
            for tile in range(tiles):
                lanes = tile_of(tile)
                masked[:, lanes] = jnp.where(window, key_f[pl.ds(at, CHUNK + taps), lanes], 0.0)
                conv = jnp.zeros((CHUNK, LANES), jnp.float32)
                for b in range(8):
                    part = jnp.zeros((CHUNK + 8, LANES), jnp.float32)
                    for a in range(taps // 8):
                        tap = 8 * a + b
                        seen = masked[taps - 8 - 8 * a : taps + CHUNK - 8 * a, lanes]
                        part = part + w_ref[tap : tap + 1, tile_of(first + tile)] * seen
                    if b:
                        part = pltpu.roll(part, b, 0)
                    conv = conv + part[8:, :]
                result.append(totals[tile] + jnp.where(seg_here == doc, conv, 0.0))
            return tuple(result)

        zero = jnp.zeros((CHUNK, LANES), jnp.float32)
        shifts = lax.fori_loop(low_doc, high_doc + 1, one_doc, (zero,) * tiles)
        gate, ends = wide32(seg_here == before), wide32(seg_here == high_doc)
        carry = jnp.where(high_doc == before, 1.0, 0.0)
        same = causal_same(seg_here, segl_ref[pl.ds(n, 1), :])
        work = []
        for tile in range(tiles):
            _, rising, falling, one, last, whole = tables[tile]
            q_ref, _, v_ref = split_columns(qkv_ref, tile)
            shift_ref[pl.ds(at, CHUNK), tile_of(tile)] = shifts[tile]
            q_up = low16(wide32(q_ref[here, :]) * rising)
            k_down = low16(shifts[tile] * falling)
            work.append((q_up, k_down, v_ref[here, :], state[tile], one, last, whole))
        mixings = [
            [dot_nt(jnp.where(head, q_up, jnp.zeros_like(q_up)), k_down) for head in heads]
            for q_up, k_down, *_ in work
        ]
        for tile, (q_up, k_down, value, entering, one, last, whole) in enumerate(work):
            parts = [dot_nn(low16(jnp.where(same, mixing, 0.0)), value) for mixing in mixings[tile]]
            state_ref[tile, n] = entering
            mixed = pick_heads(heads, parts) + gate * dot_nt(q_up, low16(entering * one))
            out_ref[here, tile_of(tile)] = low16(mixed * (1.0 / math.sqrt(HEAD_DIM)))
            tail = dot_tn(low16(wide32(value) * ends), k_down) * last
            state[tile] = entering * (whole * carry) + jnp.where(diagonal, tail, 0.0)
        return 0

    lax.fori_loop(0, chunks, chunk_step, 0)


def h3_specs(length, taps, wide, chunks):
    whole = lambda *shape: pl.BlockSpec(shape, lambda i, s: (0,) * len(shape))
    tables = [whole(taps, wide), whole(1, wide), whole(length + 2 * taps, LANES), whole(chunks, CHUNK)]
    return whole, tables


def h3_forward_call(first, qkv, seg, kernel, logdec, marks, after=()):
    length, tiles, taps = qkv.shape[0], qkv.shape[1] // (3 * LANES), kernel.shape[0]
    chunks, wide = length // CHUNK, tiles * LANES
    whole, tables = h3_specs(length, taps, kernel.shape[1], chunks)
    return kernel_call(
        functools.partial(h3_forward_body, first, tiles, taps),
        [made((length, wide)), made((length, wide), jnp.float32), made((tiles, chunks, LANES, LANES), jnp.float32)],
        [
            pltpu.VMEM((length + taps, wide), jnp.float32),
            pltpu.VMEM((CHUNK + taps, wide), jnp.float32),
            pltpu.VMEM((tiles, LANES, LANES), jnp.float32),
        ],
        (1,),
        [whole(*qkv.shape)] + tables,
        [whole(length, wide), whole(length, wide), whole(tiles, chunks, LANES, LANES)],
        1,
        "h3_forward",
        after,
        10 * tiles,
    )(seg, qkv, kernel, logdec, *marks)


def h3_backward_body(
    first, tiles, taps, seg_s, qkv_ref, shift_ref, grad_ref, w_ref, logdec_ref, segb_ref, segl_ref,
    state_ref, dqkv_ref, dw_ref, dlog_ref, key_f, grad_f, masked, masked_grad, state, tap_sums, log_sum,
):
    length = qkv_ref.shape[0]
    chunks, half, core = length // CHUNK, length // 2, seg_s[length]
    tables = [decays(logdec_ref[:, tile_of(first + tile)]) for tile in range(tiles)]
    heads, diagonal = lane_heads(), head_diagonal()
    key_f[0:taps, :] = jnp.zeros((taps, tiles * LANES), jnp.float32)

    def copy_keys(n, _):
        at = pl.multiple_of(n * CHUNK, CHUNK)
        for tile in range(tiles):
            keys = split_columns(qkv_ref, tile)[1][pl.ds(place_of(n, core, half), CHUNK), :]
            key_f[pl.ds(at + taps, CHUNK), tile_of(tile)] = wide32(keys)
        return 0

    lax.fori_loop(0, chunks, copy_keys, 0)
    grad_f[length:, :] = jnp.zeros((taps, tiles * LANES), jnp.float32)
    state[...] = jnp.zeros_like(state)
    tap_sums[...] = jnp.zeros_like(tap_sums)
    log_sum[...] = jnp.zeros_like(log_sum)
    masked_grad[CHUNK + taps :, :] = jnp.zeros((8, tiles * LANES), jnp.float32)

    def chunk_step(back, _):
        n = chunks - 1 - back
        at, low_doc, high_doc, before = documents(seg_s, n)
        here = pl.ds(place_of(n, core, half), CHUNK)
        seg_here = segb_ref[pl.ds(at + taps, CHUNK), :]
        gate, ends = wide32(seg_here == before), wide32(seg_here == high_doc)
        carry = jnp.where(high_doc == before, 1.0, 0.0)
        same = causal_same(seg_here, segl_ref[pl.ds(n, 1), :])
        work = []
        for tile in range(tiles):
            _, rising, falling, *_ = tables[tile]
            q_ref, _, v_ref = split_columns(qkv_ref, tile)
            q_up = low16(wide32(q_ref[here, :]) * rising)
            k_down = low16(shift_ref[pl.ds(at, CHUNK), tile_of(tile)] * falling)
            work.append((q_up, k_down, v_ref[here, :], grad_ref[here, tile_of(first + tile)]))
        squares = []
        for q_up, k_down, value, grad in work:
            for head in heads:
                mixing = dot_nt(jnp.where(head, q_up, jnp.zeros_like(q_up)), k_down)
                grad_mixing = dot_nt(jnp.where(head, grad, jnp.zeros_like(grad)), value)
                squares.append([low16(jnp.where(same, square, 0.0)) for square in (mixing, grad_mixing)])
        for tile, (q_up, k_down, value, grad) in enumerate(work):
            steps, rising, falling, one, last, whole = tables[tile]
            lanes = tile_of(tile)
            dqkv = split_columns(dqkv_ref, tile)
            mine = squares[tile * len(heads) : (tile + 1) * len(heads)]
            dq_local = pick_heads(heads, [dot_nn(grad_mixing, k_down) for _, grad_mixing in mine])
            dk_local = pick_heads(heads, [dot_tn(grad_mixing, q_up) for _, grad_mixing in mine])
            dv = pick_heads(heads, [dot_tn(mixing, grad) for mixing, _ in mine])
            entering, leaving = state_ref[tile, n], state[tile]
            leaving_low = low16(leaving)
            reach = dot_nn(grad, low16(entering)) * (one * gate)
            spread = dot_nn(value, leaving_low) * (last * ends)
            q_up_f, k_down_f = wide32(q_up), wide32(k_down)
            dqkv[0][here, :] = low16((dq_local + reach) * rising)
            dqkv[2][here, :] = low16(dv + dot_nt(low16(k_down_f * (last * ends)), leaving_low))
            terms = steps * (q_up_f * dq_local - k_down_f * dk_local)
            terms = terms + (steps + 1.0) * q_up_f * reach + (CHUNK - 1.0 - steps) * k_down_f * spread
            log_sum[:, lanes] += terms + (CHUNK * carry) * (leaving * entering * whole)
            lead = dot_tn(low16(wide32(grad) * gate), q_up) * one
            state[tile] = leaving * (whole * carry) + jnp.where(diagonal, lead, 0.0)
            grad_f[pl.ds(at, CHUNK), lanes] = (dk_local + spread) * falling

        def one_doc(doc, totals):
            after = segb_ref[pl.ds(at + taps, CHUNK + taps), :] == doc
            ahead = segb_ref[pl.ds(at, CHUNK + taps), :] == doc
            result = []
            for tile in range(tiles):
                lanes = tile_of(tile)
                ahead_grad = jnp.where(after, grad_f[pl.ds(at, CHUNK + taps), lanes], 0.0)
                masked_grad[0 : CHUNK + taps, lanes] = ahead_grad
                masked[:, lanes] = jnp.where(ahead, key_f[pl.ds(at, CHUNK + taps), lanes], 0.0)
                own = jnp.concatenate([jnp.zeros((8, LANES), jnp.float32), masked_grad[0:CHUNK, lanes]], axis=0)
                conv = jnp.zeros((CHUNK, LANES), jnp.float32)
                for b in range(8):
                    part = jnp.zeros((CHUNK + 8, LANES), jnp.float32)
                    moved = pltpu.roll(own, CHUNK + 8 - b, 0) if b else own
                    for a in range(taps // 8):
                        tap = 8 * a + b
                        here_grad = masked_grad[8 * a : 8 * a + CHUNK + 8, lanes]
                        part = part + w_ref[tap : tap + 1, tile_of(first + tile)] * here_grad
                        seen = masked[taps - 8 - 8 * a : taps + CHUNK - 8 * a, lanes]
                        tap_sums[tap, :, lanes] += jnp.sum((moved * seen).reshape(-1, 8, LANES), axis=0)
                    if b:
                        part = pltpu.roll(part, CHUNK + 8 - b, 0)
                    conv = conv + part[:CHUNK, :]
                result.append(totals[tile] + jnp.where(seg_here == doc, conv, 0.0))
            return tuple(result)

        zero = jnp.zeros((CHUNK, LANES), jnp.float32)
        dks = lax.fori_loop(low_doc, high_doc + 1, one_doc, (zero,) * tiles)
        for tile in range(tiles):
            split_columns(dqkv_ref, tile)[1][here, :] = low16(dks[tile])
        return 0

    lax.fori_loop(0, chunks, chunk_step, 0)
    dw_ref[...] = jnp.sum(tap_sums[...], axis=1)
    dlog_ref[...] = jnp.sum(log_sum[...], axis=0, keepdims=True)


def h3_backward_call(first, qkv, shifted, grad, states, seg, kernel, logdec, marks, after=()):
    length, tiles, taps = qkv.shape[0], qkv.shape[1] // (3 * LANES), kernel.shape[0]
    chunks, wide = length // CHUNK, tiles * LANES
    whole, tables = h3_specs(length, taps, kernel.shape[1], chunks)
    tall = [pltpu.VMEM((n, wide), jnp.float32) for n in (length + taps, length + taps, CHUNK + taps, CHUNK + taps + 8)]
    return kernel_call(
        functools.partial(h3_backward_body, first, tiles, taps),
        [made(qkv.shape), made((taps, wide), jnp.float32), made((1, wide), jnp.float32)],
        tall
        + [
            pltpu.VMEM((tiles, LANES, LANES), jnp.float32),
            pltpu.VMEM((taps, 8, wide), jnp.float32),
            pltpu.VMEM((CHUNK, wide), jnp.float32),
        ],
        (1,),
        [whole(*qkv.shape), whole(*shifted.shape), whole(*grad.shape)] + tables + [whole(*states.shape)],
        [whole(*qkv.shape), whole(taps, wide), whole(1, wide)],
        1,
        "h3_backward",
        after,
        16 * tiles,
    )(seg, qkv, shifted, grad, kernel, logdec, *marks, states)


score_unit = 1.0 / math.sqrt(HEAD_DIM)


def row_block(ref, i, core, half):
    parts = [ref[pl.ds(place_of(2 * i + step, core, half), CHUNK), :] for step in range(2)]
    return jnp.concatenate(parts, axis=0)


def put_block(ref, i, core, half, block):
    for step in range(2):
        ref[pl.ds(place_of(2 * i + step, core, half), CHUNK), :] = block[step * CHUNK : (step + 1) * CHUNK, :]


def head_rows(block):
    lane, zero = lax.broadcasted_iota(jnp.int32, block.shape, 1), jnp.zeros_like(block)
    parts = [jnp.where(lane // HEAD_DIM == head, block, zero) for head in range(LANES // HEAD_DIM)]
    return jnp.concatenate(parts, axis=0)


def allowed_tile(first, segb_ref, segl_ref, q_block, k_block):
    seg_keys = segb_ref[first + k_block * BLOCK : first + (k_block + 1) * BLOCK, :]
    seg_keys = jnp.concatenate([seg_keys] * (BLOCK // LANES), axis=1)
    allowed = seg_keys == segl_ref[q_block : q_block + 1, :]
    if q_block == k_block:
        row = lax.broadcasted_iota(jnp.int32, (BLOCK, BLOCK), 0)
        lane = lax.broadcasted_iota(jnp.int32, (BLOCK, BLOCK), 1)
        allowed = allowed & (row <= lane)
    return jnp.concatenate([allowed] * (LANES // HEAD_DIM), axis=1)


def picked_rows(tall):
    parts = []
    for head in range(LANES // HEAD_DIM):
        rows = slice(head * HEAD_DIM, (head + 1) * HEAD_DIM)
        parts.append(tall[rows, head * BLOCK : (head + 1) * BLOCK])
    return jnp.concatenate(parts, axis=0)


def att_forward_body(first, seg_s, qkv_ref, segb_ref, segl_ref, out_ref, total_ref, key, value, score):
    length = qkv_ref.shape[0]
    q_ref, k_ref, v_ref = split_columns(qkv_ref)
    blocks, half, core = length // BLOCK, length // 2, seg_s[length]
    for i in range(blocks):
        key[i * BLOCK : (i + 1) * BLOCK, :] = row_block(k_ref, i, core, half)
        value[i * BLOCK : (i + 1) * BLOCK, :] = row_block(v_ref, i, core, half)
    for i in range(blocks):
        query = head_rows(row_block(q_ref, i, core, half) * jnp.bfloat16(score_unit))
        top = jnp.full((1, 2 * BLOCK), masked_score, jnp.float32)
        for j in range(i + 1):
            keys = slice(j * BLOCK, (j + 1) * BLOCK)
            tile = dot_nt(key[keys, :], query)
            tile = jnp.where(allowed_tile(first, segb_ref, segl_ref, i, j), tile, masked_score)
            score[keys, :] = tile
            top = jnp.maximum(top, jnp.max(tile, axis=0, keepdims=True))
        total = jnp.zeros((1, 2 * BLOCK), jnp.float32)
        tall = jnp.zeros((LANES, 2 * BLOCK), jnp.float32)
        for j in range(i + 1):
            keys = slice(j * BLOCK, (j + 1) * BLOCK)
            expd = jnp.exp(score[keys, :] - top)
            total = total + jnp.sum(expd, axis=0, keepdims=True)
            tall = tall + dot_tn(value[keys, :], low16(expd))
        put_block(out_ref, i, core, half, low16(picked_rows(tall / total).T))
        total_ref[i : i + 1, :] = top + jnp.log(total)


def att_backward_body(
    first, seg_s, qkv_ref, grad_ref, total_ref, segb_ref, segl_ref, dqkv_ref,
    key, value, probs, grad_probs, dk_sum, dv_sum,
):
    length = qkv_ref.shape[0]
    q_ref, k_ref, v_ref = split_columns(qkv_ref)
    dq_ref, dk_ref, dv_ref = split_columns(dqkv_ref)
    blocks, half, core = length // BLOCK, length // 2, seg_s[length]
    for i in range(blocks):
        key[i * BLOCK : (i + 1) * BLOCK, :] = row_block(k_ref, i, core, half)
        value[i * BLOCK : (i + 1) * BLOCK, :] = row_block(v_ref, i, core, half)
    for i in range(blocks):
        query = head_rows(row_block(q_ref, i, core, half) * jnp.bfloat16(score_unit))
        grad = head_rows(row_block(grad_ref, i, core, half))
        inner = jnp.zeros((1, 2 * BLOCK), jnp.float32)
        for j in range(i + 1):
            keys = slice(j * BLOCK, (j + 1) * BLOCK)
            tile = dot_nt(key[keys, :], query) - total_ref[i : i + 1, :]
            tile = jnp.exp(jnp.where(allowed_tile(first, segb_ref, segl_ref, i, j), tile, masked_score))
            grad_tile = dot_nt(value[keys, :], grad)
            probs[keys, :] = tile
            grad_probs[keys, :] = grad_tile
            inner = inner + jnp.sum(tile * grad_tile, axis=0, keepdims=True)
        tall = jnp.zeros((LANES, 2 * BLOCK), jnp.float32)
        for j in range(i + 1):
            keys = slice(j * BLOCK, (j + 1) * BLOCK)
            tile = probs[keys, :]
            grad_score = low16(tile * (grad_probs[keys, :] - inner))
            dk, dv = dot_nn(grad_score, query), dot_nn(low16(tile), grad)
            if i == j:
                dk_sum[keys, :], dv_sum[keys, :] = dk, dv
            else:
                dk_sum[keys, :] += dk
                dv_sum[keys, :] += dv
            tall = tall + dot_tn(key[keys, :], grad_score)
        put_block(dq_ref, i, core, half, low16(picked_rows(tall).T * score_unit))
    for i in range(blocks):
        put_block(dk_ref, i, core, half, low16(dk_sum[i * BLOCK : (i + 1) * BLOCK, :]))
        put_block(dv_ref, i, core, half, low16(dv_sum[i * BLOCK : (i + 1) * BLOCK, :]))


def att_specs(length, wide, marks):
    own = lambda columns: pl.BlockSpec((length, columns), lambda i, s: (0, i))
    whole = [pl.BlockSpec(mark.shape, lambda i, s: (0, 0)) for mark in marks]
    totals = pl.BlockSpec((None, length // BLOCK, 2 * BLOCK), lambda i, s: (i, 0, 0))
    return wide // LANES, own, whole, totals


def att_forward_call(first, seg, qkv, marks, *after):
    length, wide = qkv.shape[0], qkv.shape[1] // 3
    tiles, own, whole, totals = att_specs(length, wide, marks)
    return kernel_call(
        functools.partial(att_forward_body, first),
        [made((length, wide)), made((tiles, length // BLOCK, 2 * BLOCK), jnp.float32)],
        [pltpu.VMEM((length, LANES), jnp.bfloat16)] * 2 + [pltpu.VMEM((length, 2 * BLOCK), jnp.float32)],
        (tiles,),
        [own(3 * LANES)] + whole,
        [own(LANES), totals],
        1,
        "att_forward",
        after,
        11,
    )(seg, qkv, *marks)


def att_backward_call(first, seg, qkv, grad, total, marks, *after):
    length, wide = grad.shape
    tiles, own, whole, totals = att_specs(length, wide, marks)
    return kernel_call(
        functools.partial(att_backward_body, first),
        [made(qkv.shape)],
        [pltpu.VMEM((length, LANES), jnp.bfloat16)] * 2
        + [pltpu.VMEM((length, 2 * BLOCK), jnp.float32)] * 2
        + [pltpu.VMEM((length, LANES), jnp.float32)] * 2,
        (tiles,),
        [own(3 * LANES), own(LANES), totals] + whole,
        [own(3 * LANES)],
        1,
        "att_backward",
        after,
        18,
    )(seg, qkv, grad, total, *marks)[0]


def tile_rows(i, quarter, rest):
    found = []
    for kind in range(3):
        for unit in range(2):
            head = (unit * quarter, LANES, kind * LANES)
            tail = (unit * quarter + LANES, rest, 3 * LANES + kind * rest)
            for first, count, row in (head, tail):
                low, high = max(first, i * LANES), min(first + count, (i + 1) * LANES)
                if low < high:
                    found.append((unit, row + low - first, kind * LANES + low - i * LANES, high - low))
    return found


def join_body(first, own_ref, far_ref, out_ref):
    quarter = own_ref.shape[0] // 3
    for i in range(out_ref.shape[0] // (3 * LANES)):
        for unit, row, at, count in tile_rows(first + i, quarter, quarter - LANES):
            at += i * 3 * LANES
            out_ref[at : at + count, :] = (own_ref, far_ref)[unit][row : row + count, :]


def joined_tiles(first, tiles, own, far, *after):
    shape = (tiles * 3 * LANES, own.shape[1])
    body = functools.partial(join_body, first)
    return kernel_call(body, [made(shape)], name="join", after=after)(own, far)[0]


def copy_body(array_ref, out_ref):
    out_ref[...] = array_ref[...]


def copied(array, *after):
    return kernel_call(copy_body, [made(array.shape, array.dtype)], name="copied", after=after)(array)[0]


def stack_body(one_ref, two_ref, out_ref):
    rows = one_ref.shape[0]
    out_ref[:rows, :] = one_ref[...]
    out_ref[rows:, :] = two_ref[...]


def stacked(one, two, *after):
    shape = (one.shape[0] + two.shape[0], one.shape[1])
    return kernel_call(stack_body, [made(shape)], name="stack", after=after)(one, two)[0]


def pack_body(q_ref, k_ref, v_ref, *refs):
    unit_ref, quarter = refs[-1], q_ref.shape[0]
    rest = quarter - LANES
    for kind, ref in enumerate((q_ref, k_ref, v_ref)):
        unit_ref[kind * LANES : (kind + 1) * LANES, :] = ref[:LANES, :]
        unit_ref[3 * LANES + kind * rest : 3 * LANES + (kind + 1) * rest, :] = ref[LANES:, :]
    for ref in refs[:-1]:
        unit_ref[3 * quarter :, :] = ref[...]


def packed(parts, *after):
    shape = (sum(part.shape[0] for part in parts), parts[0].shape[1])
    return kernel_call(pack_body, [made(shape)], name="pack", after=after)(*parts)[0]


def put_grads(first, x_ref, dqkv_ref, units, quarter):
    for i in range(dqkv_ref.shape[1] // (3 * LANES)):
        total = dot_tn(dqkv_ref[:, i * 3 * LANES : (i + 1) * 3 * LANES], x_ref[...])
        for unit, row, at, count in tile_rows(first + i, quarter, quarter - LANES):
            units[unit][row : row + count, :] = low16(total[at : at + count, :])


def far_grads_body(first, x_ref, dqkv_ref, g_ref, *refs):
    outs, unit_ref, far_ref = refs[:-2], refs[-2], refs[-1]
    quarter = unit_ref.shape[0] // 4
    put_grads(first, x_ref, dqkv_ref, (unit_ref, far_ref), quarter)
    at = 3 * quarter
    total = jnp.concatenate([dot_tn(ref[...], g_ref[...]) for ref in outs[: len(outs) - 1 + (first == 0)]], axis=0)
    unit_ref[at:, :] = low16(total[:quarter, :])
    far_ref[at : at + quarter, :] = low16(total[quarter:, :])
    if first:
        far_ref[at + quarter :, :] = outs[-1][...]


def far_grads(first, x, dqkv, g, outs, *small, after=()):
    quarter, width = sum(out.shape[1] for out in outs) // 2, x.shape[1]
    shapes = [(4 * quarter, width), (4 * quarter + sum(rows.shape[0] for rows in small), width)]
    body = functools.partial(far_grads_body, first)
    return kernel_call(body, [made(shape) for shape in shapes], name="far_grads", after=after)(x, dqkv, g, *outs, *small)


def own_grads_body(x_ref, dqkv_ref, rest_ref, small_ref, unit_ref):
    quarter = rest_ref.shape[0] // 4
    put_grads(0, x_ref, dqkv_ref, (unit_ref, unit_ref), quarter)
    unit_ref[3 * LANES : 4 * quarter, :] = rest_ref[3 * LANES :, :]
    unit_ref[4 * quarter :, :] = small_ref[...]


def own_grads(x, dqkv, rest, small, *after):
    shape = (rest.shape[0] + small.shape[0], x.shape[1])
    return kernel_call(own_grads_body, [made(shape)], name="own_grads", after=after)(x, dqkv, rest, small)[0]


def gelu_and_slope(value):
    bell = jnp.exp(value * value * -0.5)
    below = 0.5 + 0.5 * lax.erf(value * math.sqrt(0.5))
    return value * below, below + value * bell * (1.0 / math.sqrt(2.0 * math.pi))


def ff_forward_body(x_ref, in_own, in_far, out_own, out_far, *refs):
    own_ref, other_ref = refs[-2:]
    total = None
    for i, (w_in, w_out) in enumerate(((in_own, out_own), (in_far, out_far))):
        hidden, slope = gelu_and_slope(dot_nn(x_ref[...], w_in[...]))
        hidden = low16(hidden)
        refs[i][...] = hidden
        refs[2 + i][...] = low16(slope)
        part = dot_nn(hidden, w_out[...])
        total = part if total is None else total + part

    @pl.when(pl.program_id(0) == 0)
    def _():
        other_ref[...] = low16(total)

    @pl.when(pl.program_id(0) == 1)
    def _():
        own_ref[...] = total


def ff_forward_call(x, w_in, w_out, far):
    half, width, units = x.shape[0] // 2, x.shape[1], w_in.shape[1]
    flipped = lambda columns: pl.BlockSpec((half, columns), lambda i: (1 - i, 0))
    rows = pl.BlockSpec((half, width), lambda i: (0, 0))
    weight = lambda at: pl.BlockSpec((width, units), lambda i: (at, 0))
    return kernel_call(
        ff_forward_body,
        [made((2 * half, units))] * 4 + [made((half, width), jnp.float32), made((half, width))],
        grid=(2,),
        in_specs=[flipped(width), weight(0), weight(0), weight(0), weight(1)],
        out_specs=[flipped(units)] * 4 + [rows, rows],
        name="ff_forward",
        cost=12,
    )(x, w_in, far, w_out, far)


def standardized(stream):
    centered = stream - jnp.mean(stream, axis=-1, keepdims=True)
    scale = lax.rsqrt(jnp.mean(centered * centered, axis=-1, keepdims=True) + norm_eps)
    return centered * scale, scale


def deal_rows_body(place, array_ref, *refs):
    for by, ref in enumerate(refs):
        ref[...] = low16(array_ref[place[2] ^ by])


def deal_rows(place, array, *after):
    count, *shape = array.shape
    return kernel_call(
        deal_rows_body,
        [made(tuple(shape))] * count,
        grid=(1,),
        in_specs=[pl.BlockSpec(array.shape, lambda i, s: (0, 0, 0))],
        out_specs=[pl.BlockSpec(tuple(shape), lambda i, s: (0, 0))] * count,
        scalars=1,
        name="deal_rows",
        after=after,
    )(place, array)


def collect_rows_body(place, *refs):
    for by, ref in enumerate(refs[:-1]):
        refs[-1][place[2] ^ by] = ref[...].astype(refs[-1].dtype)


def collect_rows(place, parts, kind, *after):
    shape = (len(parts), *parts[0].shape)
    return kernel_call(
        collect_rows_body,
        [made(shape, kind)],
        grid=(1,),
        in_specs=[pl.BlockSpec(parts[0].shape, lambda i, s: (0, 0))] * len(parts),
        out_specs=[pl.BlockSpec(shape, lambda i, s: (0, 0, 0))],
        scalars=1,
        name="collect_rows",
        after=after,
    )(place, *parts)[0]


def first_norm_body(place, *refs):
    *parts, gain_ref, stream_ref, normed_ref = refs
    rows = parts[0].shape[0]
    for by, ref in enumerate(parts):
        here = pl.ds(pl.multiple_of((place[2] ^ by) * rows, rows), rows)
        stream = wide32(ref[...])
        stream_ref[here, :] = stream
        normed_ref[here, :] = low16(standardized(stream)[0] * gain_ref[...])


def first_norm(place, parts, gain, *after):
    rows, width = parts[0].shape
    shape = (rows * len(parts), width)
    whole = lambda shape: pl.BlockSpec(shape, lambda i, s: (0, 0))
    return kernel_call(
        first_norm_body,
        [made(shape, jnp.float32), made(shape)],
        grid=(1,),
        in_specs=[whole(part.shape) for part in parts] + [whole(gain.shape)],
        out_specs=[whole(shape)] * 2,
        scalars=1,
        name="first_norm",
        after=after,
    )(place, *parts, gain)


def touch_body(*refs):
    pass


def touched(arrays, *after):
    anywhere = pl.BlockSpec(memory_space=pl.ANY)
    return pl.pallas_call(
        touch_body,
        in_specs=[anywhere] * (len(arrays) + len(after)),
        out_specs=[anywhere] * len(arrays),
        out_shape=[made(array.shape, array.dtype) for array in arrays],
        input_output_aliases={i: i for i in range(len(arrays))},
        cost_estimate=pl.CostEstimate(flops=0, bytes_accessed=0, transcendentals=0),
        name="touch",
    )(*arrays, *after)


def add_norm_body(stream_ref, own_ref, recv_ref, gain_ref, sum_ref, normed_ref):
    stream = stream_ref[...] + (own_ref[...] + wide32(recv_ref[...]))
    sum_ref[...] = stream
    normed_ref[...] = low16(standardized(stream)[0] * gain_ref[...])


def add_norm(stream, own, recv, gain, *after):
    outs = [made(stream.shape, jnp.float32), made(stream.shape)]
    return kernel_call(add_norm_body, outs, name="add_norm", after=after)(stream, own, recv, gain)


def norm_back_body(grad_ref, own_ref, recv_ref, stream_ref, gain_ref, sum_ref, low_ref):
    xhat, scale = standardized(stream_ref[...])
    e = (own_ref[...] + wide32(recv_ref[...])) * gain_ref[...]
    inner = jnp.mean(e * xhat, axis=-1, keepdims=True)
    back = scale * (e - jnp.mean(e, axis=-1, keepdims=True) - xhat * inner)
    total = grad_ref[...] + back
    sum_ref[...] = total
    low_ref[...] = low16(total)


def norm_back(grad, own, recv, stream, gain, *after):
    outs = [made(grad.shape, jnp.float32), made(grad.shape)]
    return kernel_call(norm_back_body, outs, name="norm_back", after=after)(grad, own, recv, stream, gain)


def fold_body(place, own_keep, recv_keep, own_send, recv_send, keep_ref, send_ref):
    send_ref[...] = low16(wide32(own_send[...]) + wide32(recv_send[...]))
    keep_ref[...] = low16(wide32(own_keep[...]) + wide32(recv_keep[...]))


def fold(place, own, recv, *after):
    shape = (own.shape[0] // 2, own.shape[1])
    keep = pl.BlockSpec(shape, lambda i, s: (s[0], 0))
    send = pl.BlockSpec(shape, lambda i, s: (1 - s[0], 0))
    same = pl.BlockSpec(shape, lambda i, s: (0, 0))
    return kernel_call(
        fold_body,
        [made(shape)] * 2,
        grid=(1,),
        in_specs=[keep, keep, send, send],
        out_specs=[same] * 2,
        scalars=1,
        name="fold",
        after=after,
    )(place, own, recv, own, recv)


def ff_fold_body(place, own_in, recv_in, own_out, recv_out, keep_ref, send_ref):
    both_in = low16(wide32(own_in[...]) + wide32(recv_in[...]))
    both_out = low16(wide32(own_out[...]) + wide32(recv_out[...]))
    keep_ref[...] = jnp.where(place[0] == 0, both_in, both_out)
    send_ref[...] = jnp.where(place[0] == 0, both_out, both_in)


def ff_fold(place, own, recv, *after):
    shape = own[0].shape
    same = pl.BlockSpec(shape, lambda i, s: (0, 0))
    return kernel_call(
        ff_fold_body,
        [made(shape)] * 2,
        grid=(1,),
        in_specs=[same] * 4,
        out_specs=[same] * 2,
        scalars=1,
        name="ff_fold",
        after=after,
    )(place, own[0], recv[0], own[1], recv[1])


def add_two_body(one_ref, two_ref, out_ref):
    out_ref[...] = low16(wide32(one_ref[...]) + wide32(two_ref[...]))


def add_two(one, two, *after):
    return kernel_call(add_two_body, [made(one.shape)], name="add_two", after=after)(one, two)[0]


def sum_parts_body(parts_ref, out_ref):
    total = wide32(parts_ref[0])
    for i in range(1, parts_ref.shape[0]):
        total = total + wide32(parts_ref[i])
    for i in range(out_ref.shape[0]):
        out_ref[i] = low16(total)


def sum_parts(parts, copies, *after):
    shape = (copies, *parts.shape[1:])
    return kernel_call(sum_parts_body, [made(shape)], name="sum_parts", after=after)(parts)[0]


def ff_finish_body(place, half_ref, recv_ref, w_ref, gain_ref, in_ref, out_ref, gain_grad_ref):
    first = place[0] == 0
    out_ref[...] = wide32(jnp.where(first, half_ref[...], recv_ref[...]))
    grad = wide32(jnp.where(first, recv_ref[...], half_ref[...]))
    in_ref[...] = grad
    sums = jnp.sum(grad * wide32(w_ref[...]), axis=1, keepdims=True)
    gain_grad_ref[...] = jnp.broadcast_to(sums, (w_ref.shape[0], LANES)).T[:8, :] / gain_ref[...]


def ff_finish(place, half, recv, w_in, gain, *after):
    whole = lambda shape: pl.BlockSpec(shape, lambda i, s: (0, 0))
    shapes = [w_in.shape, w_in.shape, (8, w_in.shape[0])]
    return kernel_call(
        ff_finish_body,
        [made(shape, jnp.float32) for shape in shapes],
        grid=(1,),
        in_specs=[whole(array.shape) for array in (half, recv, w_in, gain)],
        out_specs=[whole(shape) for shape in shapes],
        scalars=1,
        name="ff_finish",
        after=after,
    )(place, half, recv, w_in, gain)


def whole_finish_body(all_ref, w_ref, gain_ref, in_ref, out_ref, gain_grad_ref):
    width = w_ref.shape[0]
    out_ref[...] = wide32(all_ref[:width, :])
    grad = wide32(all_ref[width:, :])
    in_ref[...] = grad
    sums = jnp.sum(grad * wide32(w_ref[...]), axis=1, keepdims=True)
    gain_grad_ref[...] = jnp.broadcast_to(sums, (width, LANES)).T[:8, :] / gain_ref[...]


def whole_finish(summed, w_in, gain, *after):
    shapes = [w_in.shape, w_in.shape, (8, w_in.shape[0])]
    return kernel_call(whole_finish_body, [made(shape, jnp.float32) for shape in shapes], name="whole_finish", after=after)(
        summed, w_in, gain
    )


def mixer_finish_body(place, half_ref, recv_ref, w_ref, gain_ref, *refs):
    *outs, gain_grad_ref, unit = refs
    rows, quarter = half_ref.shape[0], outs[0].shape[0]
    rest = quarter - LANES
    for by, ref in enumerate((half_ref, recv_ref)):
        unit[pl.ds(pl.multiple_of((place[0] ^ by) * rows, 16), rows), :] = wide32(ref[...])
    for kind in range(3):
        outs[kind][:LANES, :] = unit[kind * LANES : (kind + 1) * LANES, :]
        outs[kind][LANES:, :] = unit[3 * LANES + kind * rest : 3 * LANES + (kind + 1) * rest, :]
    outs[3][...] = unit[3 * quarter : 4 * quarter, :]
    if len(outs) > 4:
        outs[4][...] = unit[4 * quarter :, :]
    sums = jnp.sum(unit[: 3 * quarter, :] * wide32(w_ref[...]), axis=0, keepdims=True)
    gain_grad_ref[...] = jnp.broadcast_to(sums / gain_ref[...], gain_grad_ref.shape)


def mixer_finish(place, half, recv, weights, gain, *after):
    rows, columns = half.shape
    quarter = weights.shape[0] // 3
    whole = lambda *shape: pl.BlockSpec(shape, lambda i, s: (0, 0))
    shapes = [(quarter, columns)] * 4 + [(2 * rows - 4 * quarter, columns)] * (2 * rows > 4 * quarter) + [(8, columns)]
    return kernel_call(
        mixer_finish_body,
        [made(shape, jnp.float32) for shape in shapes],
        [pltpu.VMEM((2 * rows, columns), jnp.float32)],
        (1,),
        [whole(rows, columns)] * 2 + [whole(*weights.shape), whole(*gain.shape)],
        [whole(*shape) for shape in shapes],
        1,
        "mixer_finish",
        after,
    )(place, half, recv, weights, gain)


def share_body(place, in_ref, out_ref, share_ref):
    share_ref[...] = jnp.where(place[0] == 0, in_ref[...], out_ref[...])


def far_share(place, w_in, w_out, count, *after):
    shape = (w_in.shape[0] // count, w_in.shape[1])
    rows = pl.BlockSpec(shape, lambda i, s: (s[1], 0))
    return kernel_call(
        share_body,
        [made(shape)],
        grid=(1,),
        in_specs=[rows, rows],
        out_specs=[pl.BlockSpec(shape, lambda i, s: (0, 0))],
        scalars=1,
        name="far_share",
        after=after,
    )(place, w_in, w_out)[0]


def exchanged(array, axis, by):
    devices = lax.axis_size(axis)
    return lax.ppermute(array, axis, [(i, i ^ by) for i in range(devices)])


def core_swap(array):
    return exchanged(array, TENSOR, 1)


def half_swap(array):
    return exchanged(array, TENSOR, 2)


def chip_place():
    return lax.axis_index(SEQ) * (lax.axis_size(TENSOR) // 2) + lax.axis_index(TENSOR) // 2


def swapped_rows(parts):
    return [parts[0]] + [exchanged(part, (SEQ, TENSOR), 2 * by) for by, part in enumerate(parts) if by]


def nt(left, right):
    return dot_nt(left, right)


def tn(left, right):
    return dot_tn(left, right)


def with_other(own):
    return jnp.concatenate([own, core_swap(own)], axis=0)


def closing_parts(parts):
    half = parts[0][0].shape[0] // 2
    other = sum(dot(left[half:], right, over) for left, right, over in parts)
    own = sum(dot(left[:half], right, over) for left, right, over in parts)
    return own, low16(other)


def closing(parts):
    own, other = closing_parts(parts)
    return own, core_swap(other)


def swapped_parts(parts):
    return lax.all_to_all(parts, DP, 0, 0)


def dealt(half):
    return swapped_parts(half.reshape(lax.axis_size(DP), -1, half.shape[1]))


def row_shards(
    tokens,
    out_grad,
    segments,
    gain_mix,
    query_mix,
    key_mix,
    value_mix,
    output_mix,
    shift_kernel,
    decay_rate,
    gain_ff1,
    ff_in1,
    ff_out1,
    gain_att,
    query_att,
    key_att,
    value_att,
    output_att,
    gain_ff2,
    ff_in2,
    ff_out2,
):
    features = tokens.shape[2]
    taps, quarter = shift_kernel.shape
    length = segments.shape[1]
    place = jnp.stack([lax.axis_index(SEQ), lax.axis_index(DP), chip_place()]).astype(jnp.int32)
    count = lax.axis_size(DP)

    mine = deal_rows(place, tokens)
    share = half_swap(far_share(place, ff_in1, ff_out1, count, mine[0]))
    mix_own = packed([query_mix.T, key_mix.T, value_mix.T], mine[0])
    mine = swapped_rows(mine)
    mix_far = half_swap(mix_own)
    far_one = lax.all_gather(share, (SEQ, DP), axis=0, tiled=True)
    few = jnp.concatenate([shift_kernel, decay_rate.reshape(1, -1) * (-1.0 / length)], axis=0)
    few_far = half_swap(few)
    both = jnp.concatenate([few, few_far], axis=1)

    seg_row = lax.dynamic_index_in_dim(segments, chip_place(), 0, False)
    core = (lax.axis_index(TENSOR) % 2).astype(jnp.int32)
    seg = jnp.concatenate([seg_row, core.reshape(1)])
    padded = jnp.pad(seg_row, (taps, taps), constant_values=-1)
    segb = jnp.broadcast_to(padded[:, None], (padded.shape[0], LANES))
    marks = (segb, seg_row.reshape(-1, CHUNK))
    att_marks = (segb, seg_row.reshape(-1, BLOCK))
    gains = [gain.reshape(1, -1) for gain in (gain_mix, gain_ff1, gain_att, gain_ff2)]
    h3 = [{"seg": seg, "kernel": table[:taps], "logdec": table[taps:], "marks": marks} for table in (few, both)]

    stream0, normed = first_norm(place, mine, gains[0], share, few_far)
    x_mix = with_other(normed)
    mix_w = [mix_own[: 3 * LANES]]
    qkv_mix = [low16(nt(x_mix, mix_w[0]))]
    kept_mix = [h3_forward_call(0, qkv_mix[0], **h3[0])]
    mix_w.append(joined_tiles(1, 2, mix_own, mix_far, kept_mix[0][0]))
    qkv_mix.append(low16(nt(x_mix, mix_w[1])))
    share = half_swap(far_share(place, ff_in2, ff_out2, count, mix_w[1]))
    mix_o = half_swap(copied(output_mix, mix_w[1]))
    kept_mix.append(touched(h3_forward_call(1, qkv_mix[1], **h3[1]), share, mix_o))
    out_mix = [kept[0] for kept in kept_mix]
    mix_o = stacked(output_mix, mix_o, out_mix[1])
    far_two = lax.all_gather(share, (SEQ, DP), axis=0, tiled=True)
    att_own = packed([query_att.T, key_att.T, value_att.T], mix_w[1])
    out_w = [mix_o[:LANES], mix_o[LANES:]]
    sums = closing([(out, weight, over_nn) for out, weight in zip(out_mix, out_w)])
    stream1, normed = add_norm(stream0, *sums, gains[1])
    x_one = with_other(normed)
    att_far = half_swap(att_own)
    kept_one = touched(ff_forward_call(x_one, ff_in1, ff_out1, far_one), att_far)
    att_w = joined_tiles(0, 3, att_own, att_far, kept_one[4])
    stream2, normed = add_norm(stream1, kept_one[4], core_swap(kept_one[5]), gains[2])
    x_att = with_other(normed)
    qkv_att = low16(nt(x_att, att_w))
    back_parts = swapped_rows(deal_rows(place, out_grad, kept_one[4]))
    att_o = half_swap(output_att)
    out_att, total = touched(att_forward_call(taps, seg, qkv_att, att_marks), *back_parts[1:], att_o, far_two)
    att_o = stacked(output_att, att_o, out_att)
    back_low = collect_rows(place, back_parts, jnp.bfloat16, out_att).reshape(-1, features)
    stream3, normed = add_norm(stream2, *closing([(out_att, att_o, over_nn)]), gains[3])
    x_two = with_other(normed)
    kept_two = ff_forward_call(x_two, ff_in2, ff_out2, far_two)
    mixed = stream3 + (kept_two[4] + wide32(core_swap(kept_two[5])))
    mixed_parts = deal_rows(place, mixed.reshape(tokens.shape))

    def ff_back(g, x, kept, w_in, w_out, far):
        far_in, far_out = far[:features], far[features:]
        far_grad = low16(nt(g, far_out) * wide32(kept[3]))
        own_grad = low16(nt(g, w_out) * wide32(kept[2]))
        sums = closing([(far_grad, far_in, over_nt), (own_grad, w_in, over_nt)])
        far_unit = (low16(tn(kept[1], g)), low16(tn(x, far_grad)))
        own_unit = (low16(tn(kept[0], g)), low16(tn(x, own_grad)))
        return sums, own_unit, far_unit

    g_two = with_other(back_low)
    sums, two_own, two_far = ff_back(g_two, x_two, kept_two, ff_in2, ff_out2, far_two)
    back, back_low = norm_back(wide32(back_low), *sums, stream3, gains[3], *two_far)
    two_recv = [half_swap(part) for part in two_far]

    g_att = with_other(back_low)
    dqkv_att = att_backward_call(taps, seg, qkv_att, low16(nt(g_att, att_o)), total, att_marks, mixed_parts[0])
    att_unit, att_far_unit = far_grads(0, x_att, dqkv_att, g_att, [out_att])
    att_recv = half_swap(att_far_unit)
    sums = closing([(dqkv_att, att_w, over_nn)])
    back, back_low = norm_back(back, *sums, stream2, gains[2], att_far_unit, two_recv[0])

    g_one = with_other(back_low)
    sums, one_own, one_far = ff_back(g_one, x_one, kept_one, ff_in1, ff_out1, far_one)
    two = ff_fold(place, two_own, two_recv, one_far[0])
    back, back_low = norm_back(back, *sums, stream1, gains[1], *one_far, two[1])
    one_recv = [half_swap(part) for part in one_far]

    g_mix = with_other(back_low)
    grad_mixed = low16(nt(g_mix, mix_o) * (1.0 / math.sqrt(HEAD_DIM)))
    att = fold(place, att_unit, att_recv, grad_mixed)
    att_got = exchanged(att[1], SEQ, 1)
    two_half = add_two(two[0], exchanged(two[1], SEQ, 1), grad_mixed)
    two_half = lax.psum(two_half, DP)

    def small_rows(kernel_grad, log_grad):
        small = jnp.concatenate([kernel_grad, log_grad * (-1.0 / length)], axis=0)
        return jnp.pad(low16(small), ((0, -small.shape[0] % 512), (0, 0))).reshape(-1, features)

    h3_back = lambda i, *after: h3_backward_call(
        i, qkv_mix[i], kept_mix[i][1], grad_mixed, kept_mix[i][2], **h3[i], after=after
    )
    late = touched(h3_back(1, att[1], *one_own), att_got, *one_recv)
    skip = quarter - LANES
    small = small_rows(late[1][:, skip:], late[2][:, skip:])
    one = ff_fold(place, one_own, one_recv, late[0])
    one_got = exchanged(one[1], SEQ, 1)
    att_half = add_two(att[0], att_got, one[1])
    att_parts = dealt(att_half)
    rest, mix_far_unit = far_grads(1, x_mix, late[0], g_mix, out_mix, small, after=(att_half,))
    mix_recv = half_swap(mix_far_unit)
    att_final = sum_parts(att_parts, count, mix_far_unit)
    att = swapped_parts(att_final)
    two_back = exchanged(two_half, SEQ, 1)
    early = touched(h3_back(0, att_final, two_half), att, one_got)
    small = small_rows(
        jnp.concatenate([early[1], late[1][:, :skip]], axis=1), jnp.concatenate([early[2], late[2][:, :skip]], axis=1)
    )

    one_half = add_two(one[0], one_got, early[0])
    one_parts = dealt(one_half)
    mix_unit = own_grads(x_mix, early[0], rest, small, one_half)
    mix = fold(place, mix_unit, mix_recv, two_back)
    mix_got = exchanged(mix[1], SEQ, 1)
    att = touched([att.reshape(-1, features)], mix[1])[0]
    mix_half = add_two(mix[0], mix_got, att)
    one_final = sum_parts(one_parts, 1, mix_half)[0]
    mix_parts = dealt(touched([mix_half], one_final)[0])
    one = lax.all_gather(one_final, (SEQ, DP), axis=0, tiled=True)
    att_back = exchanged(att, SEQ, 1)
    mixed_parts = swapped_rows(touched(mixed_parts, mix_half))
    own, other = closing_parts([(early[0], mix_w[0], over_nn), (late[0], mix_w[1], over_nn)])
    other = touched([other], one_final)[0]
    back, _ = norm_back(back, own, core_swap(other), stream0, gains[0])
    tokens_parts = deal_rows(place, back.reshape(tokens.shape))
    mix_final = sum_parts(mix_parts, count, tokens_parts[1], att_back)
    mix = swapped_parts(mix_final)
    tokens_parts = swapped_rows(touched(tokens_parts, mix_final))
    mixed_out = collect_rows(place, mixed_parts, jnp.float32, mix_final)
    tokens_grad = collect_rows(place, tokens_parts, jnp.float32, mixed_out)
    in_two, out_two, two_gain = ff_finish(place, two_half, two_back, ff_in2, gains[3], mix_final)
    q_att, k_att, v_att, o_att, att_gain = mixer_finish(place, att, att_back, att_own, gains[2], mix_final)
    mix = touched([mix.reshape(-1, features)], att_gain, tokens_grad, two_gain)[0]
    mix_back = exchanged(mix, SEQ, 1)
    in_one, out_one, one_gain = whole_finish(one, ff_in1, gains[1], mix)
    q_mix, k_mix, v_mix, o_mix, small, mix_gain = mixer_finish(place, mix, mix_back, mix_own, gains[0], one_gain)
    gain_grads = jnp.concatenate([part[:1] for part in (mix_gain, one_gain, att_gain, two_gain)])
    gain_far = half_swap(gain_grads) + exchanged(gain_grads, TENSOR, 3)
    gain_grads = (gain_grads + core_swap(gain_grads)) + gain_far
    small = small.reshape(-1, quarter)
    return (
        mixed_out,
        tokens_grad,
        gain_grads[0],
        q_mix.T,
        k_mix.T,
        v_mix.T,
        o_mix,
        small[:taps],
        gain_grads[1],
        in_one,
        out_one,
        gain_grads[2],
        q_att.T,
        k_att.T,
        v_att.T,
        o_att,
        gain_grads[3],
        in_two,
        out_two,
        small[taps].reshape(decay_rate.shape),
    )


def row_plan_fits(sizes):
    return sizes[SEQ] == 2 and sizes[TENSOR] == 4


def solution(mesh):
    plan = row_shards if row_plan_fits(dict(mesh.shape)) else shards
    return jax.shard_map(
        plan,
        mesh=mesh,
        in_specs=(
            P(DP, (SEQ, TENSOR), None),
            P(DP, (SEQ, TENSOR), None),
            P(DP, None),
            P(),
            P(None, TENSOR),
            P(None, TENSOR),
            P(None, TENSOR),
            P(TENSOR, None),
            P(None, TENSOR),
            P(TENSOR, None),
            P(),
            P(None, TENSOR),
            P(TENSOR, None),
            P(),
            P(None, TENSOR),
            P(None, TENSOR),
            P(None, TENSOR),
            P(TENSOR, None),
            P(),
            P(None, TENSOR),
            P(TENSOR, None),
        ),
        out_specs=(
            P(DP, (SEQ, TENSOR), None),
            P(DP, (SEQ, TENSOR), None),
            P(),
            P(None, TENSOR),
            P(None, TENSOR),
            P(None, TENSOR),
            P(TENSOR, None),
            P(None, TENSOR),
            P(),
            P(None, TENSOR),
            P(TENSOR, None),
            P(),
            P(None, TENSOR),
            P(None, TENSOR),
            P(None, TENSOR),
            P(TENSOR, None),
            P(),
            P(None, TENSOR),
            P(TENSOR, None),
            P(TENSOR, None),
        ),
        check_vma=False,
    )
```

```python
import functools
import math

import jax
import jax.numpy as jnp
from jax import lax
from jax.experimental import pallas as pl
from jax.experimental.pallas import tpu as pltpu
from jax.sharding import PartitionSpec as P

HEAD_DIM = 64
DP, SEQ, TENSOR = "dp", "seq", "tensor"


highest = lax.Precision.HIGHEST
norm_eps = 1e-05
masked_score = -1e30


def passed_along(array, axis, by):
    devices = lax.axis_size(axis)
    pairs = [(i, i + by) for i in range(devices) if 0 <= i + by < devices]
    return lax.ppermute(array, axis, pairs)


def prefix(array, axis, combine, identity):
    devices, here = (lax.axis_size(axis), lax.axis_index(axis))
    everything = jax.tree.map(lambda part: lax.all_gather(part, axis), array)
    start = jax.tree.map(
        lambda part, zero: jnp.broadcast_to(jnp.asarray(zero, part.dtype), part.shape),
        array,
        identity,
    )

    def step(k, before):
        reached = k < here
        new = combine(before, jax.tree.map(lambda part: part[k], everything))
        return jax.tree.map(lambda a, b: jnp.where(reached, a, b), new, before)

    return lax.fori_loop(0, devices, step, start)


def prefix_2(array, axis, join, neutral):
    count = lax.axis_size(axis)
    place = lax.axis_index(axis)
    ahead = count - 1 - place
    gathered = jax.tree.map(
        lambda a, kind: lax.all_gather(a.astype(kind), axis), array, (jnp.bfloat16, jnp.bfloat16)
    )
    state = jax.tree.map(lambda a, e: jnp.zeros_like(a) + jnp.asarray(e, a.dtype), array, neutral)

    def one(step, state):
        source = count - 1 - step
        return join(
            state,
            jax.tree.map(
                lambda a, own: lax.dynamic_index_in_dim(a, source, 0, False).astype(own.dtype),
                gathered,
                array,
            ),
        )

    return lax.fori_loop(0, ahead, one, state)


def lower_triangle(value):
    return value.astype(jnp.bfloat16)


def bmul(form, left, right):
    return jnp.einsum(form, left, right, preferred_element_type=jnp.float32)


def fmul(form, left, right):
    return jnp.einsum(form, left, right, precision=highest, preferred_element_type=jnp.float32)


def layer_norm_forward(residual_stream, norm_gain_weight):
    feature_mean = jnp.mean(residual_stream, axis=-1, keepdims=True)
    mean_centered = residual_stream - feature_mean
    scale_factor = lax.rsqrt(
        jnp.mean(mean_centered * mean_centered, axis=-1, keepdims=True) + norm_eps
    )
    standardized_input = mean_centered * scale_factor
    return (lower_triangle(standardized_input * norm_gain_weight), standardized_input, scale_factor)


def layer_norm_backward(normalized_gradient, standardized_input, scale_factor, norm_gain_weight):
    gain_gradient = jnp.sum(normalized_gradient * standardized_input, axis=(0, 1))
    rescaled_input = normalized_gradient * norm_gain_weight
    mean_centered = rescaled_input - jnp.mean(rescaled_input, axis=-1, keepdims=True)
    return (
        scale_factor
        * (
            mean_centered
            - standardized_input
            * jnp.mean(rescaled_input * standardized_input, axis=-1, keepdims=True)
        ),
        gain_gradient,
    )


def widen(normalized_input):
    return lax.all_gather(normalized_input, TENSOR, axis=1, tiled=True)


def narrow(partial_value):
    return lax.psum_scatter(partial_value, TENSOR, scatter_dimension=1, tiled=True)


def widen_grad(grad_stream):
    return lax.all_gather(lower_triangle(grad_stream), TENSOR, axis=1, tiled=True)


def narrow_grad(partial_value):
    return lax.psum_scatter(partial_value, TENSOR, scatter_dimension=1, tiled=True)


def combine_states(earlier, later):
    return (earlier[0] * later[0], later[1] + later[0][..., None] * earlier[1])


def feed_forward(residual_stream, norm_gain_weight, w_in, w_out):
    normalized_input, standardized_input, scale_factor = layer_norm_forward(
        residual_stream, norm_gain_weight
    )
    widened_hidden = widen(normalized_input)
    hidden_preactivation = bmul("rtd,df->rtf", widened_hidden, w_in)
    hidden_units = lower_triangle(jax.nn.gelu(hidden_preactivation, approximate=False))
    final_result = residual_stream + narrow(bmul("rtf,fd->rtd", hidden_units, w_out))
    return (
        final_result,
        (widened_hidden, standardized_input, scale_factor, hidden_preactivation, hidden_units),
    )


def feed_backward(grad_stream, saved_residuals, norm_gain_weight, w_in, w_out):
    widened_hidden, standardized_input, scale_factor, hidden_preactivation, hidden_units = (
        saved_residuals
    )
    grad_wide = widen_grad(grad_stream)
    grad_out_w = bmul("rtf,rtd->fd", hidden_units, grad_wide)
    grad_hidden = bmul("rtd,fd->rtf", grad_wide, w_out)
    _, gelu_pull = jax.vjp(
        lambda value: jax.nn.gelu(value, approximate=False), hidden_preactivation
    )
    grad_before = lower_triangle(gelu_pull(grad_hidden)[0])
    grad_in_w = bmul("rtd,rtf->df", widened_hidden, grad_before)
    normalized_gradient = narrow_grad(bmul("rtf,df->rtd", grad_before, w_in))
    norm_input_gradient, gain_gradient = layer_norm_backward(
        normalized_gradient, standardized_input, scale_factor, norm_gain_weight
    )
    return (grad_stream + norm_input_gradient, gain_gradient, grad_in_w, grad_out_w)


def mixer_forward(residual_stream, seg_rows, norm_gain_weight, w_q, w_k, w_v, w_o, kernel, rate):
    normalized_input, standardized_input, scale_factor = layer_norm_forward(
        residual_stream, norm_gain_weight
    )
    widened_hidden = widen(normalized_input)
    rows, group_len = (widened_hidden.shape[0], widened_hidden.shape[1])
    heads, width = rate.shape
    query_matrix = lower_triangle(bmul("rtd,de->rte", widened_hidden, w_q))
    key_matrix = lower_triangle(bmul("rtd,de->rte", widened_hidden, w_k))
    value_matrix = lower_triangle(bmul("rtd,de->rte", widened_hidden, w_v))
    taps = kernel.shape[0]
    start = lax.axis_index(SEQ) * group_len
    length = group_len * lax.axis_size(SEQ)
    padded = jnp.concatenate([jnp.full((rows, taps), -1, jnp.int32), seg_rows], axis=1)
    seg_ext = lax.dynamic_slice_in_dim(padded, start + 1, group_len + taps - 1, 1)
    owning_segment = seg_ext[:, taps - 1 :]
    rim = passed_along(key_matrix[:, group_len - taps + 1 :, :], SEQ, 1)
    extended = jnp.concatenate([rim, key_matrix], axis=1).astype(jnp.float32)
    shifted = jnp.zeros(key_matrix.shape, jnp.float32)
    match_list = []
    for tap in range(taps):
        first = taps - 1 - tap
        match = (seg_ext[:, first : first + group_len] == owning_segment).astype(jnp.float32)[
            :, :, None
        ]
        match_list.append(match)
        shifted = shifted + kernel[tap] * extended[:, first : first + group_len] * match
    matches = jnp.stack(match_list)
    logdec = -rate / length
    steps = jnp.arange(group_len, dtype=jnp.float32)[:, None, None]
    rising = jnp.exp(steps * logdec)
    falling = jnp.exp(-steps * logdec)
    leading = jnp.exp((steps + 1.0) * logdec)
    trailing = jnp.exp((group_len - 1.0 - steps) * logdec)
    before = seg_ext[:, taps - 2]
    final = owning_segment[:, -1]
    order = jnp.arange(group_len)
    same = (
        (owning_segment[:, :, None] == owning_segment[:, None, :])
        & (order[:, None] >= order[None, :])
    ).astype(jnp.float32)
    gate = (owning_segment == before[:, None]).astype(jnp.float32)[:, :, None, None]
    ends = (owning_segment == final[:, None]).astype(jnp.float32)[:, :, None, None]
    carry_on = (final == before).astype(jnp.float32)[:, None, None]
    query_f = query_matrix.astype(jnp.float32).reshape(rows, group_len, heads, width)
    shift_f = shifted.reshape(rows, group_len, heads, width)
    value_f = value_matrix.astype(jnp.float32).reshape(rows, group_len, heads, width)
    query_up = query_f * rising
    key_down = shift_f * falling
    query_lead = query_f * leading * gate
    key_tail = shift_f * trailing * ends
    mixing = fmul("rthi,rshi->rhts", query_up, key_down) * same[:, None]
    decay = jnp.exp(group_len * logdec)[None] * carry_on
    end_state = fmul("rshi,rshj->rhij", key_tail, value_f)
    identity = (jnp.ones(decay.shape, jnp.float32), jnp.zeros(end_state.shape, jnp.float32))
    entering = prefix((decay, end_state), SEQ, combine_states, identity)[1]
    mixed = fmul("rhts,rshj->rthj", mixing, value_f) + fmul("rthi,rhij->rthj", query_lead, entering)
    out_mix = lower_triangle(
        mixed.reshape(rows, group_len, heads * width) * (1.0 / math.sqrt(width))
    )
    final_result = residual_stream + narrow(bmul("rte,ed->rtd", out_mix, w_o))
    saved_residuals = (
        widened_hidden,
        standardized_input,
        scale_factor,
        extended,
        matches,
        value_f,
        rising,
        falling,
        leading,
        trailing,
        gate,
        ends,
        same,
        query_up,
        key_down,
        query_lead,
        key_tail,
        mixing,
        decay,
        entering,
        identity,
        out_mix,
    )
    return (final_result, saved_residuals)


def mixer_backward(
    grad_stream, saved_residuals, norm_gain_weight, w_q, w_k, w_v, w_o, kernel, rate
):
    (
        widened_hidden,
        standardized_input,
        scale_factor,
        extended,
        matches,
        value_f,
        rising,
        falling,
        leading,
        trailing,
        gate,
        ends,
        same,
        query_up,
        key_down,
        query_lead,
        key_tail,
        mixing,
        decay,
        entering,
        identity,
        out_mix,
    ) = saved_residuals
    rows, group_len = (widened_hidden.shape[0], widened_hidden.shape[1])
    heads, width = rate.shape
    taps = kernel.shape[0]
    length = group_len * lax.axis_size(SEQ)
    grad_wide = widen_grad(grad_stream)
    grad_o = bmul("rte,rtd->ed", out_mix, grad_wide)
    grad_mixed = bmul("rtd,ed->rte", grad_wide, w_o).reshape(rows, group_len, heads, width) * (
        1.0 / math.sqrt(width)
    )
    grad_mixing = fmul("rthj,rshj->rhts", grad_mixed, value_f) * same[:, None]
    grad_qup = fmul("rhts,rshi->rthi", grad_mixing, key_down)
    grad_kdown = fmul("rhts,rthi->rshi", grad_mixing, query_up)
    reach = fmul("rthj,rhij->rthi", grad_mixed, entering)
    local_back = fmul("rthi,rthj->rhij", query_lead, grad_mixed)
    leaving = prefix_2((decay, local_back), SEQ, combine_states, identity)[1]
    spread = fmul("rshj,rhij->rshi", value_f, leaving)
    grad_value = fmul("rhts,rthj->rshj", mixing, grad_mixed) + fmul(
        "rshi,rhij->rshj", key_tail, leaving
    )
    grad_query = grad_qup * rising + reach * leading * gate
    grad_shift = grad_kdown * falling + spread * trailing * ends
    steps = jnp.arange(group_len, dtype=jnp.float32)[:, None, None]
    local_terms = steps * (query_up * grad_qup - key_down * grad_kdown)
    local_terms = (
        local_terms
        + (steps + 1.0) * query_lead * reach
        + (group_len - 1.0 - steps) * key_tail * spread
    )
    grad_log = jnp.sum(local_terms, axis=(0, 1))
    grad_log = grad_log + group_len * jnp.sum(jnp.sum(leaving * entering, axis=3) * decay, axis=0)
    grad_rate = -grad_log / length
    grad_shift = grad_shift.reshape(rows, group_len, heads * width)
    grad_ext = jnp.zeros(extended.shape, jnp.float32)
    kernel_rows = []
    for tap in range(taps):
        first = taps - 1 - tap
        masked = grad_shift * matches[tap]
        kernel_rows.append(jnp.sum(masked * extended[:, first : first + group_len], axis=(0, 1)))
        grad_ext = grad_ext + jnp.pad(
            kernel[tap] * masked, ((0, 0), (first, taps - 1 - first), (0, 0))
        )
    grad_kernel = jnp.stack(kernel_rows)
    returned = passed_along(grad_ext[:, : taps - 1].astype(jnp.bfloat16), SEQ, -1).astype(
        jnp.float32
    )
    grad_keys = grad_ext[:, taps - 1 :] + jnp.pad(
        returned, ((0, 0), (group_len - taps + 1, 0), (0, 0))
    )
    query_low = lower_triangle(grad_query.reshape(rows, group_len, heads * width))
    keys_low = lower_triangle(grad_keys)
    value_low = lower_triangle(grad_value.reshape(rows, group_len, heads * width))
    grad_qw = bmul("rtd,rte->de", widened_hidden, query_low)
    grad_kw = bmul("rtd,rte->de", widened_hidden, keys_low)
    grad_vw = bmul("rtd,rte->de", widened_hidden, value_low)
    partial_value = bmul("rte,de->rtd", query_low, w_q) + bmul("rte,de->rtd", keys_low, w_k)
    partial_value = partial_value + bmul("rte,de->rtd", value_low, w_v)
    normalized_gradient = narrow_grad(partial_value)
    norm_input_gradient, gain_gradient = layer_norm_backward(
        normalized_gradient, standardized_input, scale_factor, norm_gain_weight
    )
    return (
        grad_stream + norm_input_gradient,
        gain_gradient,
        grad_qw,
        grad_kw,
        grad_vw,
        grad_o,
        grad_kernel,
        grad_rate,
    )


def split_heads(value):
    return value.reshape(value.shape[0], value.shape[1] // HEAD_DIM, HEAD_DIM)


def scores_of(query_rows, key_rows, query_places, key_places, query_seg, key_seg):
    raw = bmul("thd,shd->hts", split_heads(query_rows), split_heads(key_rows)) * (
        1.0 / math.sqrt(HEAD_DIM)
    )
    allowed = (query_places[:, None] >= key_places[None, :]) & (
        query_seg[:, None] == key_seg[None, :]
    )
    return jnp.where(allowed[None], raw, masked_score)


def attend_forward(residual_stream, seg_rows, norm_gain_weight, w_q, w_k, w_v, w_o):
    normalized_input, standardized_input, scale_factor = layer_norm_forward(
        residual_stream, norm_gain_weight
    )
    widened_hidden = widen(normalized_input)
    rows, group_len = (widened_hidden.shape[0], widened_hidden.shape[1])
    query_matrix = lower_triangle(bmul("rtd,de->rte", widened_hidden, w_q))
    key_matrix = lower_triangle(bmul("rtd,de->rte", widened_hidden, w_k))
    value_matrix = lower_triangle(bmul("rtd,de->rte", widened_hidden, w_v))
    gathered_key_rows, gathered_value_rows = (
        lax.all_gather(key_matrix, SEQ, axis=1, tiled=True),
        lax.all_gather(value_matrix, SEQ, axis=1, tiled=True),
    )
    length = gathered_key_rows.shape[1]
    start = lax.axis_index(SEQ) * group_len
    owning_segment = lax.dynamic_slice_in_dim(seg_rows, start, group_len, 1)
    query_places = start + jnp.arange(group_len)
    key_places = jnp.arange(length)

    def forward_row(pieces):
        query_row, key_row, value_row, seg_own, seg_all = pieces
        scores = scores_of(query_row, key_row, query_places, key_places, seg_own, seg_all)
        top = jnp.max(scores, axis=-1, keepdims=True)
        expd = jnp.exp(scores - top)
        total = jnp.sum(expd, axis=-1, keepdims=True)
        softened = lower_triangle(expd / total)
        attended = bmul("hts,shd->thd", softened, split_heads(value_row))
        return (
            lower_triangle(attended.reshape(group_len, attended.shape[1] * HEAD_DIM)),
            (top + jnp.log(total))[..., 0],
        )

    attention_output, log_normalizer = lax.map(
        forward_row,
        (query_matrix, gathered_key_rows, gathered_value_rows, owning_segment, seg_rows),
    )
    final_result = residual_stream + narrow(bmul("rte,ed->rtd", attention_output, w_o))
    saved_residuals = (
        widened_hidden,
        standardized_input,
        scale_factor,
        query_matrix,
        key_matrix,
        value_matrix,
        gathered_key_rows,
        gathered_value_rows,
        owning_segment,
        log_normalizer,
        attention_output,
    )
    return (final_result, saved_residuals)


def attend_backward(grad_stream, saved_residuals, seg_rows, norm_gain_weight, w_q, w_k, w_v, w_o):
    (
        widened_hidden,
        standardized_input,
        scale_factor,
        query_matrix,
        key_matrix,
        value_matrix,
        gathered_key_rows,
        gathered_value_rows,
        owning_segment,
        log_normalizer,
        attention_output,
    ) = saved_residuals
    rows, group_len = (widened_hidden.shape[0], widened_hidden.shape[1])
    length = gathered_key_rows.shape[1]
    start = lax.axis_index(SEQ) * group_len
    query_places = start + jnp.arange(group_len)
    key_places = jnp.arange(length)
    scale = 1.0 / math.sqrt(HEAD_DIM)
    grad_wide = widen_grad(grad_stream)
    grad_o = bmul("rte,rtd->ed", attention_output, grad_wide)
    grad_out = lower_triangle(bmul("rtd,ed->rte", grad_wide, w_o))

    def query_common(pieces):
        query_row, key_row, value_row, seg_own, seg_all, total_row, grad_row = pieces
        scores = scores_of(query_row, key_row, query_places, key_places, seg_own, seg_all)
        softened = jnp.exp(scores - total_row[:, :, None])
        grad_soft = bmul("thd,shd->hts", split_heads(grad_row), split_heads(value_row))
        inner = jnp.sum(softened * grad_soft, axis=-1)
        grad_score = lower_triangle(softened * (grad_soft - inner[:, :, None]))
        grad_q = bmul("hts,shd->thd", grad_score, split_heads(key_row)) * scale
        return (softened, grad_score, grad_q.reshape(group_len, -1), inner)

    pieces = (
        query_matrix,
        gathered_key_rows,
        gathered_value_rows,
        owning_segment,
        seg_rows,
        log_normalizer,
        grad_out,
    )

    def query_only(row_pieces):
        _, _, grad_q, inner = query_common(row_pieces)
        return (grad_q, inner)

    grad_query, inner = lax.map(query_only, pieces)
    all_query, all_grad = (
        lax.all_gather(query_matrix, SEQ, axis=1, tiled=True),
        lax.all_gather(grad_out, SEQ, axis=1, tiled=True),
    )
    all_total, all_inner = (
        lax.all_gather(log_normalizer, SEQ, axis=2, tiled=True),
        lax.all_gather(inner, SEQ, axis=2, tiled=True),
    )

    def key_row_fn(row_pieces):
        query_row, key_row, value_row, seg_all, seg_own, total_row, inner_row, grad_row = row_pieces
        scores = scores_of(query_row, key_row, key_places, query_places, seg_all, seg_own)
        softened = jnp.exp(scores - total_row[:, :, None])
        grad_soft = bmul("thd,shd->hts", split_heads(grad_row), split_heads(value_row))
        grad_score = lower_triangle(softened * (grad_soft - inner_row[:, :, None]))
        grad_k = bmul("hts,thd->shd", grad_score, split_heads(query_row)) * scale
        grad_v = bmul("hts,thd->shd", lower_triangle(softened), split_heads(grad_row))
        return (grad_k.reshape(group_len, -1), grad_v.reshape(group_len, -1))

    grad_keys, grad_values = lax.map(
        key_row_fn,
        (
            all_query,
            key_matrix,
            value_matrix,
            seg_rows,
            owning_segment,
            all_total,
            all_inner,
            all_grad,
        ),
    )
    query_low = lower_triangle(grad_query)
    keys_low = lower_triangle(grad_keys)
    value_low = lower_triangle(grad_values)
    grad_qw = bmul("rtd,rte->de", widened_hidden, query_low)
    grad_kw = bmul("rtd,rte->de", widened_hidden, keys_low)
    grad_vw = bmul("rtd,rte->de", widened_hidden, value_low)
    partial_value = bmul("rte,de->rtd", query_low, w_q) + bmul("rte,de->rtd", keys_low, w_k)
    partial_value = partial_value + bmul("rte,de->rtd", value_low, w_v)
    normalized_gradient = narrow_grad(partial_value)
    norm_input_gradient, gain_gradient = layer_norm_backward(
        normalized_gradient, standardized_input, scale_factor, norm_gain_weight
    )
    return (grad_stream + norm_input_gradient, gain_gradient, grad_qw, grad_kw, grad_vw, grad_o)


def shards(
    tokens,
    out_grad,
    segments,
    gain_mix,
    query_mix,
    key_mix,
    value_mix,
    output_mix,
    shift_kernel,
    decay_rate,
    gain_ff1,
    ff_in1,
    ff_out1,
    gain_att,
    query_att,
    key_att,
    value_att,
    output_att,
    gain_ff2,
    ff_in2,
    ff_out2,
):
    stream_one, kept_mix = mixer_forward(
        tokens,
        segments,
        gain_mix,
        query_mix,
        key_mix,
        value_mix,
        output_mix,
        shift_kernel,
        decay_rate,
    )
    stream_two, kept_first = feed_forward(stream_one, gain_ff1, ff_in1, ff_out1)
    stream_three, kept_att = attend_forward(
        stream_two, segments, gain_att, query_att, key_att, value_att, output_att
    )
    stream_four, kept_second = feed_forward(stream_three, gain_ff2, ff_in2, ff_out2)
    back_three, gain_two_grad, in_two_grad, out_two_grad = feed_backward(
        out_grad, kept_second, gain_ff2, ff_in2, ff_out2
    )
    back_two, att_gain_grad, att_q_grad, att_k_grad, att_v_grad, att_o_grad = attend_backward(
        back_three, kept_att, segments, gain_att, query_att, key_att, value_att, output_att
    )
    back_one, gain_one_grad, in_one_grad, out_one_grad = feed_backward(
        back_two, kept_first, gain_ff1, ff_in1, ff_out1
    )
    (
        back_zero,
        mix_gain_grad,
        mix_q_grad,
        mix_k_grad,
        mix_v_grad,
        mix_o_grad,
        kernel_grad,
        rate_grad,
    ) = mixer_backward(
        back_one,
        kept_mix,
        gain_mix,
        query_mix,
        key_mix,
        value_mix,
        output_mix,
        shift_kernel,
        decay_rate,
    )
    summed = lax.psum(
        (
            mix_q_grad,
            mix_k_grad,
            mix_v_grad,
            mix_o_grad,
            kernel_grad,
            in_one_grad,
            out_one_grad,
            att_q_grad,
            att_k_grad,
            att_v_grad,
            att_o_grad,
            in_two_grad,
            out_two_grad,
            rate_grad,
        ),
        (DP, SEQ),
    )
    gains = lax.psum(
        (mix_gain_grad, gain_one_grad, att_gain_grad, gain_two_grad), (DP, SEQ, TENSOR)
    )
    return (
        stream_four,
        back_zero,
        gains[0],
        summed[0],
        summed[1],
        summed[2],
        summed[3],
        summed[4],
        gains[1],
        summed[5],
        summed[6],
        gains[2],
        summed[7],
        summed[8],
        summed[9],
        summed[10],
        gains[3],
        summed[11],
        summed[12],
        summed[13],
    )


CHUNK = 128
LANES = 128
BLOCK = 2 * CHUNK
FF_COLUMNS = 768
MIB = 1024 * 1024


def dot(left, right, over):
    return lax.dot_general(left, right, (over, ((), ())), preferred_element_type=jnp.float32)


over_nn, over_nt = ((1,), (0,)), ((1,), (1,))


def dot_nn(left, right):
    return dot(left, right, over_nn)


def dot_nt(left, right):
    return dot(left, right, over_nt)


def dot_tn(left, right):
    return dot(left, right, ((0,), (0,)))


def low16(value):
    return value.astype(jnp.bfloat16)


def wide32(value):
    return value.astype(jnp.float32)


def made(shape, kind=jnp.bfloat16):
    return jax.ShapeDtypeStruct(shape, kind)


def kernel_call(
    body, outs, scratch=(), grid=(), in_specs=None, out_specs=None, scalars=0, name=None, after=(), cost=0
):
    if in_specs is None:
        in_specs, out_specs = pl.BlockSpec(memory_space=pltpu.VMEM), [pl.BlockSpec(memory_space=pltpu.VMEM)] * len(outs)
    params = pltpu.CompilerParams(vmem_limit_bytes=50 * MIB)
    estimate = pl.CostEstimate(flops=cost * 10**9, bytes_accessed=0, transcendentals=0)

    def call(*arrays):
        count = len(arrays)
        ins = [in_specs] * (count - scalars) if isinstance(in_specs, pl.BlockSpec) else list(in_specs)
        spec = pltpu.PrefetchScalarGridSpec(
            num_scalar_prefetch=scalars,
            grid=grid,
            in_specs=ins + [pl.BlockSpec(memory_space=pl.ANY)] * len(after),
            out_specs=out_specs,
            scratch_shapes=scratch,
        )

        def whole_body(*refs):
            body(*refs[:count], *refs[count + len(after) :])

        return pl.pallas_call(
            whole_body, grid_spec=spec, out_shape=outs, compiler_params=params, cost_estimate=estimate, name=name
        )(*arrays, *after)

    return call


def place_of(n, core, half):
    return pl.multiple_of(((n & 1) ^ core) * half + (n >> 1) * CHUNK, CHUNK)


def lane_heads():
    lane = lax.broadcasted_iota(jnp.int32, (CHUNK, LANES), 1)
    return [lane // HEAD_DIM == head for head in range(LANES // HEAD_DIM)]


def head_diagonal():
    row = lax.broadcasted_iota(jnp.int32, (LANES, LANES), 0)
    lane = lax.broadcasted_iota(jnp.int32, (LANES, LANES), 1)
    return row // HEAD_DIM == lane // HEAD_DIM


def causal_same(seg_rows, seg_lanes):
    row = lax.broadcasted_iota(jnp.int32, (CHUNK, CHUNK), 0)
    lane = lax.broadcasted_iota(jnp.int32, (CHUNK, CHUNK), 1)
    return (seg_rows == seg_lanes) & (row >= lane)


def pick_heads(heads, parts):
    result = parts[0]
    for head in range(1, len(parts)):
        result = jnp.where(heads[head], parts[head], result)
    return result


def decays(logdec):
    steps = wide32(lax.broadcasted_iota(jnp.int32, (CHUNK, LANES), 0))
    rising, falling = jnp.exp(steps * logdec), jnp.exp(-steps * logdec)
    return steps, rising, falling, jnp.exp(logdec), jnp.exp((CHUNK - 1.0) * logdec), jnp.exp(CHUNK * logdec)


def documents(seg_s, n):
    at = pl.multiple_of(n * CHUNK, CHUNK)
    before = jnp.where(n == 0, -1, seg_s[jnp.maximum(at - 1, 0)])
    return at, seg_s[at], seg_s[at + CHUNK - 1], before


def split_columns(ref, tile=0):
    first = 3 * LANES * tile
    return [ref.at[:, first + i * LANES : first + (i + 1) * LANES] for i in range(3)]


def tile_of(tile):
    return slice(tile * LANES, (tile + 1) * LANES)


def h3_forward_body(
    first, tiles, taps, seg_s, qkv_ref, w_ref, logdec_ref, segb_ref, segl_ref,
    out_ref, shift_ref, state_ref, key_f, masked, state,
):
    length = qkv_ref.shape[0]
    chunks, half, core = length // CHUNK, length // 2, seg_s[length]
    tables = [decays(logdec_ref[:, tile_of(first + tile)]) for tile in range(tiles)]
    heads, diagonal = lane_heads(), head_diagonal()
    key_f[0:taps, :] = jnp.zeros((taps, tiles * LANES), jnp.float32)
    state[...] = jnp.zeros_like(state)

    def chunk_step(n, _):
        at, low_doc, high_doc, before = documents(seg_s, n)
        here = pl.ds(place_of(n, core, half), CHUNK)
        for tile in range(tiles):
            key_f[pl.ds(at + taps, CHUNK), tile_of(tile)] = wide32(split_columns(qkv_ref, tile)[1][here, :])
        seg_here = segb_ref[pl.ds(at + taps, CHUNK), :]

        def one_doc(doc, totals):
            window = segb_ref[pl.ds(at, CHUNK + taps), :] == doc
            result = []
            for tile in range(tiles):
                lanes = tile_of(tile)
                masked[:, lanes] = jnp.where(window, key_f[pl.ds(at, CHUNK + taps), lanes], 0.0)
                conv = jnp.zeros((CHUNK, LANES), jnp.float32)
                for b in range(8):
                    part = jnp.zeros((CHUNK + 8, LANES), jnp.float32)
                    for a in range(taps // 8):
                        tap = 8 * a + b
                        seen = masked[taps - 8 - 8 * a : taps + CHUNK - 8 * a, lanes]
                        part = part + w_ref[tap : tap + 1, tile_of(first + tile)] * seen
                    if b:
                        part = pltpu.roll(part, b, 0)
                    conv = conv + part[8:, :]
                result.append(totals[tile] + jnp.where(seg_here == doc, conv, 0.0))
            return tuple(result)

        zero = jnp.zeros((CHUNK, LANES), jnp.float32)
        shifts = lax.fori_loop(low_doc, high_doc + 1, one_doc, (zero,) * tiles)
        gate, ends = wide32(seg_here == before), wide32(seg_here == high_doc)
        carry = jnp.where(high_doc == before, 1.0, 0.0)
        same = causal_same(seg_here, segl_ref[pl.ds(n, 1), :])
        work = []
        for tile in range(tiles):
            _, rising, falling, one, last, whole = tables[tile]
            q_ref, _, v_ref = split_columns(qkv_ref, tile)
            shift_ref[pl.ds(at, CHUNK), tile_of(tile)] = shifts[tile]
            q_up = low16(wide32(q_ref[here, :]) * rising)
            k_down = low16(shifts[tile] * falling)
            work.append((q_up, k_down, v_ref[here, :], state[tile], one, last, whole))
        mixings = [
            [dot_nt(jnp.where(head, q_up, jnp.zeros_like(q_up)), k_down) for head in heads]
            for q_up, k_down, *_ in work
        ]
        for tile, (q_up, k_down, value, entering, one, last, whole) in enumerate(work):
            parts = [dot_nn(low16(jnp.where(same, mixing, 0.0)), value) for mixing in mixings[tile]]
            state_ref[tile, n] = entering
            mixed = pick_heads(heads, parts) + gate * dot_nt(q_up, low16(entering * one))
            out_ref[here, tile_of(tile)] = low16(mixed * (1.0 / math.sqrt(HEAD_DIM)))
            tail = dot_tn(low16(wide32(value) * ends), k_down) * last
            state[tile] = entering * (whole * carry) + jnp.where(diagonal, tail, 0.0)
        return 0

    lax.fori_loop(0, chunks, chunk_step, 0)


def h3_specs(length, taps, wide, chunks):
    whole = lambda *shape: pl.BlockSpec(shape, lambda i, s: (0,) * len(shape))
    tables = [whole(taps, wide), whole(1, wide), whole(length + 2 * taps, LANES), whole(chunks, CHUNK)]
    return whole, tables


def h3_forward_call(first, qkv, seg, kernel, logdec, marks, after=()):
    length, tiles, taps = qkv.shape[0], qkv.shape[1] // (3 * LANES), kernel.shape[0]
    chunks, wide = length // CHUNK, tiles * LANES
    whole, tables = h3_specs(length, taps, kernel.shape[1], chunks)
    return kernel_call(
        functools.partial(h3_forward_body, first, tiles, taps),
        [made((length, wide)), made((length, wide), jnp.float32), made((tiles, chunks, LANES, LANES), jnp.float32)],
        [
            pltpu.VMEM((length + taps, wide), jnp.float32),
            pltpu.VMEM((CHUNK + taps, wide), jnp.float32),
            pltpu.VMEM((tiles, LANES, LANES), jnp.float32),
        ],
        (1,),
        [whole(*qkv.shape)] + tables,
        [whole(length, wide), whole(length, wide), whole(tiles, chunks, LANES, LANES)],
        1,
        "h3_forward",
        after,
        10 * tiles,
    )(seg, qkv, kernel, logdec, *marks)


def h3_backward_body(
    first, tiles, taps, seg_s, qkv_ref, shift_ref, grad_ref, w_ref, logdec_ref, segb_ref, segl_ref,
    state_ref, dqkv_ref, dw_ref, dlog_ref, key_f, grad_f, masked, masked_grad, state, tap_sums, log_sum,
):
    length = qkv_ref.shape[0]
    chunks, half, core = length // CHUNK, length // 2, seg_s[length]
    tables = [decays(logdec_ref[:, tile_of(first + tile)]) for tile in range(tiles)]
    heads, diagonal = lane_heads(), head_diagonal()
    key_f[0:taps, :] = jnp.zeros((taps, tiles * LANES), jnp.float32)

    def copy_keys(n, _):
        at = pl.multiple_of(n * CHUNK, CHUNK)
        for tile in range(tiles):
            keys = split_columns(qkv_ref, tile)[1][pl.ds(place_of(n, core, half), CHUNK), :]
            key_f[pl.ds(at + taps, CHUNK), tile_of(tile)] = wide32(keys)
        return 0

    lax.fori_loop(0, chunks, copy_keys, 0)
    grad_f[length:, :] = jnp.zeros((taps, tiles * LANES), jnp.float32)
    state[...] = jnp.zeros_like(state)
    tap_sums[...] = jnp.zeros_like(tap_sums)
    log_sum[...] = jnp.zeros_like(log_sum)
    masked_grad[CHUNK + taps :, :] = jnp.zeros((8, tiles * LANES), jnp.float32)

    def chunk_step(back, _):
        n = chunks - 1 - back
        at, low_doc, high_doc, before = documents(seg_s, n)
        here = pl.ds(place_of(n, core, half), CHUNK)
        seg_here = segb_ref[pl.ds(at + taps, CHUNK), :]
        gate, ends = wide32(seg_here == before), wide32(seg_here == high_doc)
        carry = jnp.where(high_doc == before, 1.0, 0.0)
        same = causal_same(seg_here, segl_ref[pl.ds(n, 1), :])
        work = []
        for tile in range(tiles):
            _, rising, falling, *_ = tables[tile]
            q_ref, _, v_ref = split_columns(qkv_ref, tile)
            q_up = low16(wide32(q_ref[here, :]) * rising)
            k_down = low16(shift_ref[pl.ds(at, CHUNK), tile_of(tile)] * falling)
            work.append((q_up, k_down, v_ref[here, :], grad_ref[here, tile_of(first + tile)]))
        squares = []
        for q_up, k_down, value, grad in work:
            for head in heads:
                mixing = dot_nt(jnp.where(head, q_up, jnp.zeros_like(q_up)), k_down)
                grad_mixing = dot_nt(jnp.where(head, grad, jnp.zeros_like(grad)), value)
                squares.append([low16(jnp.where(same, square, 0.0)) for square in (mixing, grad_mixing)])
        for tile, (q_up, k_down, value, grad) in enumerate(work):
            steps, rising, falling, one, last, whole = tables[tile]
            lanes = tile_of(tile)
            dqkv = split_columns(dqkv_ref, tile)
            mine = squares[tile * len(heads) : (tile + 1) * len(heads)]
            dq_local = pick_heads(heads, [dot_nn(grad_mixing, k_down) for _, grad_mixing in mine])
            dk_local = pick_heads(heads, [dot_tn(grad_mixing, q_up) for _, grad_mixing in mine])
            dv = pick_heads(heads, [dot_tn(mixing, grad) for mixing, _ in mine])
            entering, leaving = state_ref[tile, n], state[tile]
            leaving_low = low16(leaving)
            reach = dot_nn(grad, low16(entering)) * (one * gate)
            spread = dot_nn(value, leaving_low) * (last * ends)
            q_up_f, k_down_f = wide32(q_up), wide32(k_down)
            dqkv[0][here, :] = low16((dq_local + reach) * rising)
            dqkv[2][here, :] = low16(dv + dot_nt(low16(k_down_f * (last * ends)), leaving_low))
            terms = steps * (q_up_f * dq_local - k_down_f * dk_local)
            terms = terms + (steps + 1.0) * q_up_f * reach + (CHUNK - 1.0 - steps) * k_down_f * spread
            log_sum[:, lanes] += terms + (CHUNK * carry) * (leaving * entering * whole)
            lead = dot_tn(low16(wide32(grad) * gate), q_up) * one
            state[tile] = leaving * (whole * carry) + jnp.where(diagonal, lead, 0.0)
            grad_f[pl.ds(at, CHUNK), lanes] = (dk_local + spread) * falling

        def one_doc(doc, totals):
            after = segb_ref[pl.ds(at + taps, CHUNK + taps), :] == doc
            ahead = segb_ref[pl.ds(at, CHUNK + taps), :] == doc
            result = []
            for tile in range(tiles):
                lanes = tile_of(tile)
                ahead_grad = jnp.where(after, grad_f[pl.ds(at, CHUNK + taps), lanes], 0.0)
                masked_grad[0 : CHUNK + taps, lanes] = ahead_grad
                masked[:, lanes] = jnp.where(ahead, key_f[pl.ds(at, CHUNK + taps), lanes], 0.0)
                own = jnp.concatenate([jnp.zeros((8, LANES), jnp.float32), masked_grad[0:CHUNK, lanes]], axis=0)
                conv = jnp.zeros((CHUNK, LANES), jnp.float32)
                for b in range(8):
                    part = jnp.zeros((CHUNK + 8, LANES), jnp.float32)
                    moved = pltpu.roll(own, CHUNK + 8 - b, 0) if b else own
                    for a in range(taps // 8):
                        tap = 8 * a + b
                        here_grad = masked_grad[8 * a : 8 * a + CHUNK + 8, lanes]
                        part = part + w_ref[tap : tap + 1, tile_of(first + tile)] * here_grad
                        seen = masked[taps - 8 - 8 * a : taps + CHUNK - 8 * a, lanes]
                        tap_sums[tap, :, lanes] += jnp.sum((moved * seen).reshape(-1, 8, LANES), axis=0)
                    if b:
                        part = pltpu.roll(part, CHUNK + 8 - b, 0)
                    conv = conv + part[:CHUNK, :]
                result.append(totals[tile] + jnp.where(seg_here == doc, conv, 0.0))
            return tuple(result)

        zero = jnp.zeros((CHUNK, LANES), jnp.float32)
        dks = lax.fori_loop(low_doc, high_doc + 1, one_doc, (zero,) * tiles)
        for tile in range(tiles):
            split_columns(dqkv_ref, tile)[1][here, :] = low16(dks[tile])
        return 0

    lax.fori_loop(0, chunks, chunk_step, 0)
    dw_ref[...] = jnp.sum(tap_sums[...], axis=1)
    dlog_ref[...] = jnp.sum(log_sum[...], axis=0, keepdims=True)


def h3_backward_call(first, qkv, shifted, grad, states, seg, kernel, logdec, marks, after=()):
    length, tiles, taps = qkv.shape[0], qkv.shape[1] // (3 * LANES), kernel.shape[0]
    chunks, wide = length // CHUNK, tiles * LANES
    whole, tables = h3_specs(length, taps, kernel.shape[1], chunks)
    tall = [pltpu.VMEM((n, wide), jnp.float32) for n in (length + taps, length + taps, CHUNK + taps, CHUNK + taps + 8)]
    return kernel_call(
        functools.partial(h3_backward_body, first, tiles, taps),
        [made(qkv.shape), made((taps, wide), jnp.float32), made((1, wide), jnp.float32)],
        tall
        + [
            pltpu.VMEM((tiles, LANES, LANES), jnp.float32),
            pltpu.VMEM((taps, 8, wide), jnp.float32),
            pltpu.VMEM((CHUNK, wide), jnp.float32),
        ],
        (1,),
        [whole(*qkv.shape), whole(*shifted.shape), whole(*grad.shape)] + tables + [whole(*states.shape)],
        [whole(*qkv.shape), whole(taps, wide), whole(1, wide)],
        1,
        "h3_backward",
        after,
        16 * tiles,
    )(seg, qkv, shifted, grad, kernel, logdec, *marks, states)


score_unit = 1.0 / math.sqrt(HEAD_DIM)


def row_block(ref, i, core, half):
    parts = [ref[pl.ds(place_of(2 * i + step, core, half), CHUNK), :] for step in range(2)]
    return jnp.concatenate(parts, axis=0)


def put_block(ref, i, core, half, block):
    for step in range(2):
        ref[pl.ds(place_of(2 * i + step, core, half), CHUNK), :] = block[step * CHUNK : (step + 1) * CHUNK, :]


def head_rows(block):
    lane, zero = lax.broadcasted_iota(jnp.int32, block.shape, 1), jnp.zeros_like(block)
    parts = [jnp.where(lane // HEAD_DIM == head, block, zero) for head in range(LANES // HEAD_DIM)]
    return jnp.concatenate(parts, axis=0)


def allowed_tile(first, segb_ref, segl_ref, q_block, k_block):
    seg_keys = segb_ref[first + k_block * BLOCK : first + (k_block + 1) * BLOCK, :]
    seg_keys = jnp.concatenate([seg_keys] * (BLOCK // LANES), axis=1)
    allowed = seg_keys == segl_ref[q_block : q_block + 1, :]
    if q_block == k_block:
        row = lax.broadcasted_iota(jnp.int32, (BLOCK, BLOCK), 0)
        lane = lax.broadcasted_iota(jnp.int32, (BLOCK, BLOCK), 1)
        allowed = allowed & (row <= lane)
    return jnp.concatenate([allowed] * (LANES // HEAD_DIM), axis=1)


def picked_rows(tall):
    parts = []
    for head in range(LANES // HEAD_DIM):
        rows = slice(head * HEAD_DIM, (head + 1) * HEAD_DIM)
        parts.append(tall[rows, head * BLOCK : (head + 1) * BLOCK])
    return jnp.concatenate(parts, axis=0)


def att_forward_body(first, seg_s, qkv_ref, segb_ref, segl_ref, out_ref, total_ref, key, value, score):
    length = qkv_ref.shape[0]
    q_ref, k_ref, v_ref = split_columns(qkv_ref)
    blocks, half, core = length // BLOCK, length // 2, seg_s[length]
    for i in range(blocks):
        key[i * BLOCK : (i + 1) * BLOCK, :] = row_block(k_ref, i, core, half)
        value[i * BLOCK : (i + 1) * BLOCK, :] = row_block(v_ref, i, core, half)
    for i in range(blocks):
        query = head_rows(row_block(q_ref, i, core, half) * jnp.bfloat16(score_unit))
        top = jnp.full((1, 2 * BLOCK), masked_score, jnp.float32)
        for j in range(i + 1):
            keys = slice(j * BLOCK, (j + 1) * BLOCK)
            tile = dot_nt(key[keys, :], query)
            tile = jnp.where(allowed_tile(first, segb_ref, segl_ref, i, j), tile, masked_score)
            score[keys, :] = tile
            top = jnp.maximum(top, jnp.max(tile, axis=0, keepdims=True))
        total = jnp.zeros((1, 2 * BLOCK), jnp.float32)
        tall = jnp.zeros((LANES, 2 * BLOCK), jnp.float32)
        for j in range(i + 1):
            keys = slice(j * BLOCK, (j + 1) * BLOCK)
            expd = jnp.exp(score[keys, :] - top)
            total = total + jnp.sum(expd, axis=0, keepdims=True)
            tall = tall + dot_tn(value[keys, :], low16(expd))
        put_block(out_ref, i, core, half, low16(picked_rows(tall / total).T))
        total_ref[i : i + 1, :] = top + jnp.log(total)


def att_backward_body(
    first, seg_s, qkv_ref, grad_ref, total_ref, segb_ref, segl_ref, dqkv_ref,
    key, value, probs, grad_probs, dk_sum, dv_sum,
):
    length = qkv_ref.shape[0]
    q_ref, k_ref, v_ref = split_columns(qkv_ref)
    dq_ref, dk_ref, dv_ref = split_columns(dqkv_ref)
    blocks, half, core = length // BLOCK, length // 2, seg_s[length]
    for i in range(blocks):
        key[i * BLOCK : (i + 1) * BLOCK, :] = row_block(k_ref, i, core, half)
        value[i * BLOCK : (i + 1) * BLOCK, :] = row_block(v_ref, i, core, half)
    for i in range(blocks):
        query = head_rows(row_block(q_ref, i, core, half) * jnp.bfloat16(score_unit))
        grad = head_rows(row_block(grad_ref, i, core, half))
        inner = jnp.zeros((1, 2 * BLOCK), jnp.float32)
        for j in range(i + 1):
            keys = slice(j * BLOCK, (j + 1) * BLOCK)
            tile = dot_nt(key[keys, :], query) - total_ref[i : i + 1, :]
            tile = jnp.exp(jnp.where(allowed_tile(first, segb_ref, segl_ref, i, j), tile, masked_score))
            grad_tile = dot_nt(value[keys, :], grad)
            probs[keys, :] = tile
            grad_probs[keys, :] = grad_tile
            inner = inner + jnp.sum(tile * grad_tile, axis=0, keepdims=True)
        tall = jnp.zeros((LANES, 2 * BLOCK), jnp.float32)
        for j in range(i + 1):
            keys = slice(j * BLOCK, (j + 1) * BLOCK)
            tile = probs[keys, :]
            grad_score = low16(tile * (grad_probs[keys, :] - inner))
            dk, dv = dot_nn(grad_score, query), dot_nn(low16(tile), grad)
            if i == j:
                dk_sum[keys, :], dv_sum[keys, :] = dk, dv
            else:
                dk_sum[keys, :] += dk
                dv_sum[keys, :] += dv
            tall = tall + dot_tn(key[keys, :], grad_score)
        put_block(dq_ref, i, core, half, low16(picked_rows(tall).T * score_unit))
    for i in range(blocks):
        put_block(dk_ref, i, core, half, low16(dk_sum[i * BLOCK : (i + 1) * BLOCK, :]))
        put_block(dv_ref, i, core, half, low16(dv_sum[i * BLOCK : (i + 1) * BLOCK, :]))


def att_specs(length, wide, marks):
    own = lambda columns: pl.BlockSpec((length, columns), lambda i, s: (0, i))
    whole = [pl.BlockSpec(mark.shape, lambda i, s: (0, 0)) for mark in marks]
    totals = pl.BlockSpec((None, length // BLOCK, 2 * BLOCK), lambda i, s: (i, 0, 0))
    return wide // LANES, own, whole, totals


def att_forward_call(first, seg, qkv, marks, *after):
    length, wide = qkv.shape[0], qkv.shape[1] // 3
    tiles, own, whole, totals = att_specs(length, wide, marks)
    return kernel_call(
        functools.partial(att_forward_body, first),
        [made((length, wide)), made((tiles, length // BLOCK, 2 * BLOCK), jnp.float32)],
        [pltpu.VMEM((length, LANES), jnp.bfloat16)] * 2 + [pltpu.VMEM((length, 2 * BLOCK), jnp.float32)],
        (tiles,),
        [own(3 * LANES)] + whole,
        [own(LANES), totals],
        1,
        "att_forward",
        after,
        11,
    )(seg, qkv, *marks)


def att_backward_call(first, seg, qkv, grad, total, marks, *after):
    length, wide = grad.shape
    tiles, own, whole, totals = att_specs(length, wide, marks)
    return kernel_call(
        functools.partial(att_backward_body, first),
        [made(qkv.shape)],
        [pltpu.VMEM((length, LANES), jnp.bfloat16)] * 2
        + [pltpu.VMEM((length, 2 * BLOCK), jnp.float32)] * 2
        + [pltpu.VMEM((length, LANES), jnp.float32)] * 2,
        (tiles,),
        [own(3 * LANES), own(LANES), totals] + whole,
        [own(3 * LANES)],
        1,
        "att_backward",
        after,
        18,
    )(seg, qkv, grad, total, *marks)[0]


def tile_rows(i, quarter, rest):
    found = []
    for kind in range(3):
        for unit in range(2):
            head = (unit * quarter, LANES, kind * LANES)
            tail = (unit * quarter + LANES, rest, 3 * LANES + kind * rest)
            for first, count, row in (head, tail):
                low, high = max(first, i * LANES), min(first + count, (i + 1) * LANES)
                if low < high:
                    found.append((unit, row + low - first, kind * LANES + low - i * LANES, high - low))
    return found


def join_body(first, own_ref, far_ref, out_ref):
    quarter = own_ref.shape[0] // 3
    for i in range(out_ref.shape[0] // (3 * LANES)):
        for unit, row, at, count in tile_rows(first + i, quarter, quarter - LANES):
            at += i * 3 * LANES
            out_ref[at : at + count, :] = (own_ref, far_ref)[unit][row : row + count, :]


def joined_tiles(first, tiles, own, far, *after):
    shape = (tiles * 3 * LANES, own.shape[1])
    body = functools.partial(join_body, first)
    return kernel_call(body, [made(shape)], name="join", after=after)(own, far)[0]


def copy_body(array_ref, out_ref):
    out_ref[...] = array_ref[...]


def copied(array, *after):
    return kernel_call(copy_body, [made(array.shape, array.dtype)], name="copied", after=after)(array)[0]


def stack_body(one_ref, two_ref, out_ref):
    rows = one_ref.shape[0]
    out_ref[:rows, :] = one_ref[...]
    out_ref[rows:, :] = two_ref[...]


def stacked(one, two, *after):
    shape = (one.shape[0] + two.shape[0], one.shape[1])
    return kernel_call(stack_body, [made(shape)], name="stack", after=after)(one, two)[0]


def pack_body(q_ref, k_ref, v_ref, *refs):
    unit_ref, quarter = refs[-1], q_ref.shape[0]
    rest = quarter - LANES
    for kind, ref in enumerate((q_ref, k_ref, v_ref)):
        unit_ref[kind * LANES : (kind + 1) * LANES, :] = ref[:LANES, :]
        unit_ref[3 * LANES + kind * rest : 3 * LANES + (kind + 1) * rest, :] = ref[LANES:, :]
    for ref in refs[:-1]:
        unit_ref[3 * quarter :, :] = ref[...]


def packed(parts, *after):
    shape = (sum(part.shape[0] for part in parts), parts[0].shape[1])
    return kernel_call(pack_body, [made(shape)], name="pack", after=after)(*parts)[0]


def put_grads(first, x_ref, dqkv_ref, units, quarter):
    for i in range(dqkv_ref.shape[1] // (3 * LANES)):
        total = dot_tn(dqkv_ref[:, i * 3 * LANES : (i + 1) * 3 * LANES], x_ref[...])
        for unit, row, at, count in tile_rows(first + i, quarter, quarter - LANES):
            units[unit][row : row + count, :] = low16(total[at : at + count, :])


def far_grads_body(first, x_ref, dqkv_ref, g_ref, *refs):
    outs, unit_ref, far_ref = refs[:-2], refs[-2], refs[-1]
    quarter = unit_ref.shape[0] // 4
    put_grads(first, x_ref, dqkv_ref, (unit_ref, far_ref), quarter)
    at = 3 * quarter
    total = jnp.concatenate([dot_tn(ref[...], g_ref[...]) for ref in outs[: len(outs) - 1 + (first == 0)]], axis=0)
    unit_ref[at:, :] = low16(total[:quarter, :])
    far_ref[at : at + quarter, :] = low16(total[quarter:, :])
    if first:
        far_ref[at + quarter :, :] = outs[-1][...]


def far_grads(first, x, dqkv, g, outs, *small, after=()):
    quarter, width = sum(out.shape[1] for out in outs) // 2, x.shape[1]
    shapes = [(4 * quarter, width), (4 * quarter + sum(rows.shape[0] for rows in small), width)]
    body = functools.partial(far_grads_body, first)
    return kernel_call(body, [made(shape) for shape in shapes], name="far_grads", after=after)(x, dqkv, g, *outs, *small)


def own_grads_body(x_ref, dqkv_ref, rest_ref, small_ref, unit_ref):
    quarter = rest_ref.shape[0] // 4
    put_grads(0, x_ref, dqkv_ref, (unit_ref, unit_ref), quarter)
    unit_ref[3 * LANES : 4 * quarter, :] = rest_ref[3 * LANES :, :]
    unit_ref[4 * quarter :, :] = small_ref[...]


def own_grads(x, dqkv, rest, small, *after):
    shape = (rest.shape[0] + small.shape[0], x.shape[1])
    return kernel_call(own_grads_body, [made(shape)], name="own_grads", after=after)(x, dqkv, rest, small)[0]


def gelu_and_slope(value):
    bell = jnp.exp(value * value * -0.5)
    below = 0.5 + 0.5 * lax.erf(value * math.sqrt(0.5))
    return value * below, below + value * bell * (1.0 / math.sqrt(2.0 * math.pi))


def ff_forward_body(x_ref, in_own, in_far, out_own, out_far, *refs):
    own_ref, other_ref = refs[-2:]
    total = None
    for i, (w_in, w_out) in enumerate(((in_own, out_own), (in_far, out_far))):
        hidden, slope = gelu_and_slope(dot_nn(x_ref[...], w_in[...]))
        hidden = low16(hidden)
        refs[i][...] = hidden
        refs[2 + i][...] = low16(slope)
        part = dot_nn(hidden, w_out[...])
        total = part if total is None else total + part

    @pl.when(pl.program_id(0) == 0)
    def _():
        other_ref[...] = low16(total)

    @pl.when(pl.program_id(0) == 1)
    def _():
        own_ref[...] = total


def ff_forward_call(x, w_in, w_out, far):
    half, width, units = x.shape[0] // 2, x.shape[1], w_in.shape[1]
    flipped = lambda columns: pl.BlockSpec((half, columns), lambda i: (1 - i, 0))
    rows = pl.BlockSpec((half, width), lambda i: (0, 0))
    weight = lambda at: pl.BlockSpec((width, units), lambda i: (at, 0))
    return kernel_call(
        ff_forward_body,
        [made((2 * half, units))] * 4 + [made((half, width), jnp.float32), made((half, width))],
        grid=(2,),
        in_specs=[flipped(width), weight(0), weight(0), weight(0), weight(1)],
        out_specs=[flipped(units)] * 4 + [rows, rows],
        name="ff_forward",
        cost=12,
    )(x, w_in, far, w_out, far)


def standardized(stream):
    centered = stream - jnp.mean(stream, axis=-1, keepdims=True)
    scale = lax.rsqrt(jnp.mean(centered * centered, axis=-1, keepdims=True) + norm_eps)
    return centered * scale, scale


def deal_rows_body(place, array_ref, *refs):
    for by, ref in enumerate(refs):
        ref[...] = low16(array_ref[place[2] ^ by])


def deal_rows(place, array, *after):
    count, *shape = array.shape
    return kernel_call(
        deal_rows_body,
        [made(tuple(shape))] * count,
        grid=(1,),
        in_specs=[pl.BlockSpec(array.shape, lambda i, s: (0, 0, 0))],
        out_specs=[pl.BlockSpec(tuple(shape), lambda i, s: (0, 0))] * count,
        scalars=1,
        name="deal_rows",
        after=after,
    )(place, array)


def collect_rows_body(place, *refs):
    for by, ref in enumerate(refs[:-1]):
        refs[-1][place[2] ^ by] = ref[...].astype(refs[-1].dtype)


def collect_rows(place, parts, kind, *after):
    shape = (len(parts), *parts[0].shape)
    return kernel_call(
        collect_rows_body,
        [made(shape, kind)],
        grid=(1,),
        in_specs=[pl.BlockSpec(parts[0].shape, lambda i, s: (0, 0))] * len(parts),
        out_specs=[pl.BlockSpec(shape, lambda i, s: (0, 0, 0))],
        scalars=1,
        name="collect_rows",
        after=after,
    )(place, *parts)[0]


def first_norm_body(place, *refs):
    *parts, gain_ref, stream_ref, normed_ref = refs
    rows = parts[0].shape[0]
    for by, ref in enumerate(parts):
        here = pl.ds(pl.multiple_of((place[2] ^ by) * rows, rows), rows)
        stream = wide32(ref[...])
        stream_ref[here, :] = stream
        normed_ref[here, :] = low16(standardized(stream)[0] * gain_ref[...])


def first_norm(place, parts, gain, *after):
    rows, width = parts[0].shape
    shape = (rows * len(parts), width)
    whole = lambda shape: pl.BlockSpec(shape, lambda i, s: (0, 0))
    return kernel_call(
        first_norm_body,
        [made(shape, jnp.float32), made(shape)],
        grid=(1,),
        in_specs=[whole(part.shape) for part in parts] + [whole(gain.shape)],
        out_specs=[whole(shape)] * 2,
        scalars=1,
        name="first_norm",
        after=after,
    )(place, *parts, gain)


def touch_body(*refs):
    pass


def touched(arrays, *after):
    anywhere = pl.BlockSpec(memory_space=pl.ANY)
    return pl.pallas_call(
        touch_body,
        in_specs=[anywhere] * (len(arrays) + len(after)),
        out_specs=[anywhere] * len(arrays),
        out_shape=[made(array.shape, array.dtype) for array in arrays],
        input_output_aliases={i: i for i in range(len(arrays))},
        cost_estimate=pl.CostEstimate(flops=0, bytes_accessed=0, transcendentals=0),
        name="touch",
    )(*arrays, *after)


def add_norm_body(stream_ref, own_ref, recv_ref, gain_ref, sum_ref, normed_ref):
    stream = stream_ref[...] + (own_ref[...] + wide32(recv_ref[...]))
    sum_ref[...] = stream
    normed_ref[...] = low16(standardized(stream)[0] * gain_ref[...])


def add_norm(stream, own, recv, gain, *after):
    outs = [made(stream.shape, jnp.float32), made(stream.shape)]
    return kernel_call(add_norm_body, outs, name="add_norm", after=after)(stream, own, recv, gain)


def norm_back_body(grad_ref, own_ref, recv_ref, stream_ref, gain_ref, sum_ref, low_ref):
    xhat, scale = standardized(stream_ref[...])
    e = (own_ref[...] + wide32(recv_ref[...])) * gain_ref[...]
    inner = jnp.mean(e * xhat, axis=-1, keepdims=True)
    back = scale * (e - jnp.mean(e, axis=-1, keepdims=True) - xhat * inner)
    total = grad_ref[...] + back
    sum_ref[...] = total
    low_ref[...] = low16(total)


def norm_back(grad, own, recv, stream, gain, *after):
    outs = [made(grad.shape, jnp.float32), made(grad.shape)]
    return kernel_call(norm_back_body, outs, name="norm_back", after=after)(grad, own, recv, stream, gain)


def fold_body(place, own_keep, recv_keep, own_send, recv_send, keep_ref, send_ref):
    send_ref[...] = low16(wide32(own_send[...]) + wide32(recv_send[...]))
    keep_ref[...] = low16(wide32(own_keep[...]) + wide32(recv_keep[...]))


def fold(place, own, recv, *after):
    shape = (own.shape[0] // 2, own.shape[1])
    keep = pl.BlockSpec(shape, lambda i, s: (s[0], 0))
    send = pl.BlockSpec(shape, lambda i, s: (1 - s[0], 0))
    same = pl.BlockSpec(shape, lambda i, s: (0, 0))
    return kernel_call(
        fold_body,
        [made(shape)] * 2,
        grid=(1,),
        in_specs=[keep, keep, send, send],
        out_specs=[same] * 2,
        scalars=1,
        name="fold",
        after=after,
    )(place, own, recv, own, recv)


def ff_fold_body(place, own_in, recv_in, own_out, recv_out, keep_ref, send_ref):
    both_in = low16(wide32(own_in[...]) + wide32(recv_in[...]))
    both_out = low16(wide32(own_out[...]) + wide32(recv_out[...]))
    keep_ref[...] = jnp.where(place[0] == 0, both_in, both_out)
    send_ref[...] = jnp.where(place[0] == 0, both_out, both_in)


def ff_fold(place, own, recv, *after):
    shape = own[0].shape
    same = pl.BlockSpec(shape, lambda i, s: (0, 0))
    return kernel_call(
        ff_fold_body,
        [made(shape)] * 2,
        grid=(1,),
        in_specs=[same] * 4,
        out_specs=[same] * 2,
        scalars=1,
        name="ff_fold",
        after=after,
    )(place, own[0], recv[0], own[1], recv[1])


def add_two_body(one_ref, two_ref, out_ref):
    out_ref[...] = low16(wide32(one_ref[...]) + wide32(two_ref[...]))


def add_two(one, two, *after):
    return kernel_call(add_two_body, [made(one.shape)], name="add_two", after=after)(one, two)[0]


def sum_parts_body(parts_ref, out_ref):
    total = wide32(parts_ref[0])
    for i in range(1, parts_ref.shape[0]):
        total = total + wide32(parts_ref[i])
    for i in range(out_ref.shape[0]):
        out_ref[i] = low16(total)


def sum_parts(parts, copies, *after):
    shape = (copies, *parts.shape[1:])
    return kernel_call(sum_parts_body, [made(shape)], name="sum_parts", after=after)(parts)[0]


def ff_finish_body(place, half_ref, recv_ref, w_ref, gain_ref, in_ref, out_ref, gain_grad_ref):
    first = place[0] == 0
    out_ref[...] = wide32(jnp.where(first, half_ref[...], recv_ref[...]))
    grad = wide32(jnp.where(first, recv_ref[...], half_ref[...]))
    in_ref[...] = grad
    sums = jnp.sum(grad * wide32(w_ref[...]), axis=1, keepdims=True)
    gain_grad_ref[...] = jnp.broadcast_to(sums, (w_ref.shape[0], LANES)).T[:8, :] / gain_ref[...]


def ff_finish(place, half, recv, w_in, gain, *after):
    whole = lambda shape: pl.BlockSpec(shape, lambda i, s: (0, 0))
    shapes = [w_in.shape, w_in.shape, (8, w_in.shape[0])]
    return kernel_call(
        ff_finish_body,
        [made(shape, jnp.float32) for shape in shapes],
        grid=(1,),
        in_specs=[whole(array.shape) for array in (half, recv, w_in, gain)],
        out_specs=[whole(shape) for shape in shapes],
        scalars=1,
        name="ff_finish",
        after=after,
    )(place, half, recv, w_in, gain)


def whole_finish_body(all_ref, w_ref, gain_ref, in_ref, out_ref, gain_grad_ref):
    width = w_ref.shape[0]
    out_ref[...] = wide32(all_ref[:width, :])
    grad = wide32(all_ref[width:, :])
    in_ref[...] = grad
    sums = jnp.sum(grad * wide32(w_ref[...]), axis=1, keepdims=True)
    gain_grad_ref[...] = jnp.broadcast_to(sums, (width, LANES)).T[:8, :] / gain_ref[...]


def whole_finish(summed, w_in, gain, *after):
    shapes = [w_in.shape, w_in.shape, (8, w_in.shape[0])]
    return kernel_call(whole_finish_body, [made(shape, jnp.float32) for shape in shapes], name="whole_finish", after=after)(
        summed, w_in, gain
    )


def mixer_finish_body(place, half_ref, recv_ref, w_ref, gain_ref, *refs):
    *outs, gain_grad_ref, unit = refs
    rows, quarter = half_ref.shape[0], outs[0].shape[0]
    rest = quarter - LANES
    for by, ref in enumerate((half_ref, recv_ref)):
        unit[pl.ds(pl.multiple_of((place[0] ^ by) * rows, 16), rows), :] = wide32(ref[...])
    for kind in range(3):
        outs[kind][:LANES, :] = unit[kind * LANES : (kind + 1) * LANES, :]
        outs[kind][LANES:, :] = unit[3 * LANES + kind * rest : 3 * LANES + (kind + 1) * rest, :]
    outs[3][...] = unit[3 * quarter : 4 * quarter, :]
    if len(outs) > 4:
        outs[4][...] = unit[4 * quarter :, :]
    sums = jnp.sum(unit[: 3 * quarter, :] * wide32(w_ref[...]), axis=0, keepdims=True)
    gain_grad_ref[...] = jnp.broadcast_to(sums / gain_ref[...], gain_grad_ref.shape)


def mixer_finish(place, half, recv, weights, gain, *after):
    rows, columns = half.shape
    quarter = weights.shape[0] // 3
    whole = lambda *shape: pl.BlockSpec(shape, lambda i, s: (0, 0))
    shapes = [(quarter, columns)] * 4 + [(2 * rows - 4 * quarter, columns)] * (2 * rows > 4 * quarter) + [(8, columns)]
    return kernel_call(
        mixer_finish_body,
        [made(shape, jnp.float32) for shape in shapes],
        [pltpu.VMEM((2 * rows, columns), jnp.float32)],
        (1,),
        [whole(rows, columns)] * 2 + [whole(*weights.shape), whole(*gain.shape)],
        [whole(*shape) for shape in shapes],
        1,
        "mixer_finish",
        after,
    )(place, half, recv, weights, gain)


def share_body(place, in_ref, out_ref, share_ref):
    share_ref[...] = jnp.where(place[0] == 0, in_ref[...], out_ref[...])


def far_share(place, w_in, w_out, count, *after):
    shape = (w_in.shape[0] // count, w_in.shape[1])
    rows = pl.BlockSpec(shape, lambda i, s: (s[1], 0))
    return kernel_call(
        share_body,
        [made(shape)],
        grid=(1,),
        in_specs=[rows, rows],
        out_specs=[pl.BlockSpec(shape, lambda i, s: (0, 0))],
        scalars=1,
        name="far_share",
        after=after,
    )(place, w_in, w_out)[0]


def exchanged(array, axis, by):
    devices = lax.axis_size(axis)
    return lax.ppermute(array, axis, [(i, i ^ by) for i in range(devices)])


def core_swap(array):
    return exchanged(array, TENSOR, 1)


def half_swap(array):
    return exchanged(array, TENSOR, 2)


def chip_place():
    return lax.axis_index(SEQ) * (lax.axis_size(TENSOR) // 2) + lax.axis_index(TENSOR) // 2


def swapped_rows(parts):
    return [parts[0]] + [exchanged(part, (SEQ, TENSOR), 2 * by) for by, part in enumerate(parts) if by]


def nt(left, right):
    return dot_nt(left, right)


def tn(left, right):
    return dot_tn(left, right)


def with_other(own):
    return jnp.concatenate([own, core_swap(own)], axis=0)


def closing_parts(parts):
    half = parts[0][0].shape[0] // 2
    other = sum(dot(left[half:], right, over) for left, right, over in parts)
    own = sum(dot(left[:half], right, over) for left, right, over in parts)
    return own, low16(other)


def closing(parts):
    own, other = closing_parts(parts)
    return own, core_swap(other)


def swapped_parts(parts):
    return lax.all_to_all(parts, DP, 0, 0)


def dealt(half):
    return swapped_parts(half.reshape(lax.axis_size(DP), -1, half.shape[1]))


def row_shards(
    tokens,
    out_grad,
    segments,
    gain_mix,
    query_mix,
    key_mix,
    value_mix,
    output_mix,
    shift_kernel,
    decay_rate,
    gain_ff1,
    ff_in1,
    ff_out1,
    gain_att,
    query_att,
    key_att,
    value_att,
    output_att,
    gain_ff2,
    ff_in2,
    ff_out2,
):
    features = tokens.shape[2]
    taps, quarter = shift_kernel.shape
    length = segments.shape[1]
    place = jnp.stack([lax.axis_index(SEQ), lax.axis_index(DP), chip_place()]).astype(jnp.int32)
    count = lax.axis_size(DP)

    mine = deal_rows(place, tokens)
    share = half_swap(far_share(place, ff_in1, ff_out1, count, mine[0]))
    mix_own = packed([query_mix.T, key_mix.T, value_mix.T], mine[0])
    mine = swapped_rows(mine)
    mix_far = half_swap(mix_own)
    far_one = lax.all_gather(share, (SEQ, DP), axis=0, tiled=True)
    few = jnp.concatenate([shift_kernel, decay_rate.reshape(1, -1) * (-1.0 / length)], axis=0)
    few_far = half_swap(few)
    both = jnp.concatenate([few, few_far], axis=1)

    seg_row = lax.dynamic_index_in_dim(segments, chip_place(), 0, False)
    core = (lax.axis_index(TENSOR) % 2).astype(jnp.int32)
    seg = jnp.concatenate([seg_row, core.reshape(1)])
    padded = jnp.pad(seg_row, (taps, taps), constant_values=-1)
    segb = jnp.broadcast_to(padded[:, None], (padded.shape[0], LANES))
    marks = (segb, seg_row.reshape(-1, CHUNK))
    att_marks = (segb, seg_row.reshape(-1, BLOCK))
    gains = [gain.reshape(1, -1) for gain in (gain_mix, gain_ff1, gain_att, gain_ff2)]
    h3 = [{"seg": seg, "kernel": table[:taps], "logdec": table[taps:], "marks": marks} for table in (few, both)]

    stream0, normed = first_norm(place, mine, gains[0], share, few_far)
    x_mix = with_other(normed)
    mix_w = [mix_own[: 3 * LANES]]
    qkv_mix = [low16(nt(x_mix, mix_w[0]))]
    kept_mix = [h3_forward_call(0, qkv_mix[0], **h3[0])]
    mix_w.append(joined_tiles(1, 2, mix_own, mix_far, kept_mix[0][0]))
    qkv_mix.append(low16(nt(x_mix, mix_w[1])))
    share = half_swap(far_share(place, ff_in2, ff_out2, count, mix_w[1]))
    mix_o = half_swap(copied(output_mix, mix_w[1]))
    kept_mix.append(touched(h3_forward_call(1, qkv_mix[1], **h3[1]), share, mix_o))
    out_mix = [kept[0] for kept in kept_mix]
    mix_o = stacked(output_mix, mix_o, out_mix[1])
    far_two = lax.all_gather(share, (SEQ, DP), axis=0, tiled=True)
    att_own = packed([query_att.T, key_att.T, value_att.T], mix_w[1])
    out_w = [mix_o[:LANES], mix_o[LANES:]]
    sums = closing([(out, weight, over_nn) for out, weight in zip(out_mix, out_w)])
    stream1, normed = add_norm(stream0, *sums, gains[1])
    x_one = with_other(normed)
    att_far = half_swap(att_own)
    kept_one = touched(ff_forward_call(x_one, ff_in1, ff_out1, far_one), att_far)
    att_w = joined_tiles(0, 3, att_own, att_far, kept_one[4])
    stream2, normed = add_norm(stream1, kept_one[4], core_swap(kept_one[5]), gains[2])
    x_att = with_other(normed)
    qkv_att = low16(nt(x_att, att_w))
    back_parts = swapped_rows(deal_rows(place, out_grad, kept_one[4]))
    att_o = half_swap(output_att)
    out_att, total = touched(att_forward_call(taps, seg, qkv_att, att_marks), *back_parts[1:], att_o, far_two)
    att_o = stacked(output_att, att_o, out_att)
    back_low = collect_rows(place, back_parts, jnp.bfloat16, out_att).reshape(-1, features)
    stream3, normed = add_norm(stream2, *closing([(out_att, att_o, over_nn)]), gains[3])
    x_two = with_other(normed)
    kept_two = ff_forward_call(x_two, ff_in2, ff_out2, far_two)
    mixed = stream3 + (kept_two[4] + wide32(core_swap(kept_two[5])))
    mixed_parts = deal_rows(place, mixed.reshape(tokens.shape))

    def ff_back(g, x, kept, w_in, w_out, far):
        far_in, far_out = far[:features], far[features:]
        far_grad = low16(nt(g, far_out) * wide32(kept[3]))
        own_grad = low16(nt(g, w_out) * wide32(kept[2]))
        sums = closing([(far_grad, far_in, over_nt), (own_grad, w_in, over_nt)])
        far_unit = (low16(tn(kept[1], g)), low16(tn(x, far_grad)))
        own_unit = (low16(tn(kept[0], g)), low16(tn(x, own_grad)))
        return sums, own_unit, far_unit

    g_two = with_other(back_low)
    sums, two_own, two_far = ff_back(g_two, x_two, kept_two, ff_in2, ff_out2, far_two)
    back, back_low = norm_back(wide32(back_low), *sums, stream3, gains[3], *two_far)
    two_recv = [half_swap(part) for part in two_far]

    g_att = with_other(back_low)
    dqkv_att = att_backward_call(taps, seg, qkv_att, low16(nt(g_att, att_o)), total, att_marks, mixed_parts[0])
    att_unit, att_far_unit = far_grads(0, x_att, dqkv_att, g_att, [out_att])
    att_recv = half_swap(att_far_unit)
    sums = closing([(dqkv_att, att_w, over_nn)])
    back, back_low = norm_back(back, *sums, stream2, gains[2], att_far_unit, two_recv[0])

    g_one = with_other(back_low)
    sums, one_own, one_far = ff_back(g_one, x_one, kept_one, ff_in1, ff_out1, far_one)
    two = ff_fold(place, two_own, two_recv, one_far[0])
    back, back_low = norm_back(back, *sums, stream1, gains[1], *one_far, two[1])
    one_recv = [half_swap(part) for part in one_far]

    g_mix = with_other(back_low)
    grad_mixed = low16(nt(g_mix, mix_o) * (1.0 / math.sqrt(HEAD_DIM)))
    att = fold(place, att_unit, att_recv, grad_mixed)
    att_got = exchanged(att[1], SEQ, 1)
    two_half = add_two(two[0], exchanged(two[1], SEQ, 1), grad_mixed)
    two_half = lax.psum(two_half, DP)

    def small_rows(kernel_grad, log_grad):
        small = jnp.concatenate([kernel_grad, log_grad * (-1.0 / length)], axis=0)
        return jnp.pad(low16(small), ((0, -small.shape[0] % 512), (0, 0))).reshape(-1, features)

    h3_back = lambda i, *after: h3_backward_call(
        i, qkv_mix[i], kept_mix[i][1], grad_mixed, kept_mix[i][2], **h3[i], after=after
    )
    late = touched(h3_back(1, att[1], *one_own), att_got, *one_recv)
    skip = quarter - LANES
    small = small_rows(late[1][:, skip:], late[2][:, skip:])
    one = ff_fold(place, one_own, one_recv, late[0])
    one_got = exchanged(one[1], SEQ, 1)
    att_half = add_two(att[0], att_got, one[1])
    att_parts = dealt(att_half)
    rest, mix_far_unit = far_grads(1, x_mix, late[0], g_mix, out_mix, small, after=(att_half,))
    mix_recv = half_swap(mix_far_unit)
    att_final = sum_parts(att_parts, count, mix_far_unit)
    att = swapped_parts(att_final)
    two_back = exchanged(two_half, SEQ, 1)
    early = touched(h3_back(0, att_final, two_half), att, one_got)
    small = small_rows(
        jnp.concatenate([early[1], late[1][:, :skip]], axis=1), jnp.concatenate([early[2], late[2][:, :skip]], axis=1)
    )

    one_half = add_two(one[0], one_got, early[0])
    one_parts = dealt(one_half)
    mix_unit = own_grads(x_mix, early[0], rest, small, one_half)
    mix = fold(place, mix_unit, mix_recv, two_back)
    mix_got = exchanged(mix[1], SEQ, 1)
    att = touched([att.reshape(-1, features)], mix[1])[0]
    mix_half = add_two(mix[0], mix_got, att)
    one_final = sum_parts(one_parts, 1, mix_half)[0]
    mix_parts = dealt(touched([mix_half], one_final)[0])
    att_back = exchanged(att, SEQ, 1)
    mixed_parts = swapped_rows(touched(mixed_parts, mix_half))
    own, other = closing_parts([(early[0], mix_w[0], over_nn), (late[0], mix_w[1], over_nn)])
    other = touched([other], one_final)[0]
    back, _ = norm_back(back, own, core_swap(other), stream0, gains[0])
    tokens_parts = deal_rows(place, back.reshape(tokens.shape))
    mix_final = sum_parts(mix_parts, count, tokens_parts[1], att_back)
    mix = swapped_parts(mix_final)
    one = lax.all_gather(touched([one_final], mix_final)[0], (SEQ, DP), axis=0, tiled=True)
    tokens_parts = swapped_rows(touched(tokens_parts, mix_final))
    mixed_out = collect_rows(place, mixed_parts, jnp.float32, mix_final)
    tokens_grad = collect_rows(place, tokens_parts, jnp.float32, mixed_out)
    in_two, out_two, two_gain = ff_finish(place, two_half, two_back, ff_in2, gains[3], mix_final)
    q_att, k_att, v_att, o_att, att_gain = mixer_finish(place, att, att_back, att_own, gains[2], mix_final)
    mix = touched([mix.reshape(-1, features)], att_gain, tokens_grad, two_gain)[0]
    mix_back = exchanged(mix, SEQ, 1)
    q_mix, k_mix, v_mix, o_mix, small, mix_gain = mixer_finish(place, mix, mix_back, mix_own, gains[0])
    in_one, out_one, one_gain = whole_finish(one, ff_in1, gains[1], mix_gain)
    gain_grads = jnp.concatenate([part[:1] for part in (mix_gain, one_gain, att_gain, two_gain)])
    gain_far = half_swap(gain_grads) + exchanged(gain_grads, TENSOR, 3)
    gain_grads = (gain_grads + core_swap(gain_grads)) + gain_far
    small = small.reshape(-1, quarter)
    return (
        mixed_out,
        tokens_grad,
        gain_grads[0],
        q_mix.T,
        k_mix.T,
        v_mix.T,
        o_mix,
        small[:taps],
        gain_grads[1],
        in_one,
        out_one,
        gain_grads[2],
        q_att.T,
        k_att.T,
        v_att.T,
        o_att,
        gain_grads[3],
        in_two,
        out_two,
        small[taps].reshape(decay_rate.shape),
    )


def row_plan_fits(sizes):
    return sizes[SEQ] == 2 and sizes[TENSOR] == 4


def solution(mesh):
    plan = row_shards if row_plan_fits(dict(mesh.shape)) else shards
    return jax.shard_map(
        plan,
        mesh=mesh,
        in_specs=(
            P(DP, (SEQ, TENSOR), None),
            P(DP, (SEQ, TENSOR), None),
            P(DP, None),
            P(),
            P(None, TENSOR),
            P(None, TENSOR),
            P(None, TENSOR),
            P(TENSOR, None),
            P(None, TENSOR),
            P(TENSOR, None),
            P(),
            P(None, TENSOR),
            P(TENSOR, None),
            P(),
            P(None, TENSOR),
            P(None, TENSOR),
            P(None, TENSOR),
            P(TENSOR, None),
            P(),
            P(None, TENSOR),
            P(TENSOR, None),
        ),
        out_specs=(
            P(DP, (SEQ, TENSOR), None),
            P(DP, (SEQ, TENSOR), None),
            P(),
            P(None, TENSOR),
            P(None, TENSOR),
            P(None, TENSOR),
            P(TENSOR, None),
            P(None, TENSOR),
            P(),
            P(None, TENSOR),
            P(TENSOR, None),
            P(),
            P(None, TENSOR),
            P(None, TENSOR),
            P(None, TENSOR),
            P(TENSOR, None),
            P(),
            P(None, TENSOR),
            P(TENSOR, None),
            P(TENSOR, None),
        ),
        check_vma=False,
    )
```
